32 devices in a mesh: ctx: 16 (over z, y, x), ch: 2 (over core).
Axes of the slice: x: 2, y: 2, z: 4, core: 2. Of those that a mesh axis runs over, the one named last changes fastest.
Arguments:
- query_input: bfloat16 [2048, 1024], P('ctx', 'ch'), may hold values from -6 to 6
- key_input: bfloat16 [2048, 1024], P('ctx', 'ch'), may hold values from -6 to 6
- value_input: bfloat16 [2048, 1024], P('ctx', 'ch'), may hold values from -6 to 6
- implicit_filter: float32 [2048, 1024], P('ctx', 'ch'), may hold values from -1.1 to 1.1
- explicit_taps: float32 [128, 1024], P(None, 'ch'), may hold values from -0.5 to 0.5
- skip_gain: float32 [1024], P('ch'), may hold values from -3 to 3
- out_grad: bfloat16 [2048, 1024], P('ctx', 'ch'), may hold values from -6 to 6
Outputs:
- mixed_output: float32 [2048, 1024], P('ctx', 'ch')
- query_grad: float32 [2048, 1024], P('ctx', 'ch')
- key_grad: float32 [2048, 1024], P('ctx', 'ch')
- value_grad: float32 [2048, 1024], P('ctx', 'ch')
- filter_grad: float32 [2048, 1024], P('ctx', 'ch')
- taps_grad: float32 [128, 1024], P(None, 'ch')
- skip_grad: float32 [1024], P('ch')
The draws below stay inside these ranges and needn't reach their ends.
All inputs are finite; a program needn't handle non-finite values.
Results may differ from the reference program's by a relative error of at most 0.0005.
Values sent between devices are 32-bit elements; how exact they have to be, the bound alone decides.
No kernel may reach another device: no remote copies, remote signals or barrier semaphores. Data moves between devices by JAX's collectives and lax.ppermute only.
A program may use at most 64 MiB of HBM per device.

```python
import math
import jax
import jax.numpy as jnp
from jax import lax

MIXER_CHANNELS = 1024
MTAPS = 128
SEQUENCE_TOKENS = 2048


def draw_implicit_filter(key, part):
    rate_key = jax.random.fold_in(key, 11)
    spike_random_key = jax.random.fold_in(key, 12)
    rough_key = jax.random.fold_in(key, 13)
    token_location = jnp.arange(SEQUENCE_TOKENS, dtype=jnp.float32)[:, None]
    rate_draw = jax.random.uniform(rate_key, (1, MIXER_CHANNELS), jnp.float32)
    decay_reach_scale = 30.0 * jnp.exp(rate_draw * math.log(1000.0 * SEQUENCE_TOKENS / 30.0))
    noisy_component = jnp.clip(jax.random.normal(rough_key, (SEQUENCE_TOKENS, MIXER_CHANNELS), jnp.float32), -4.0, 4.0)
    filter_spikes = jax.random.randint(spike_random_key, (3, MIXER_CHANNELS), 0, SEQUENCE_TOKENS).astype(jnp.float32)
    spike_multiplier = jnp.where(token_location >= filter_spikes[0][None, :], 0.6, 1.0)
    spike_multiplier = spike_multiplier * jnp.where(token_location >= filter_spikes[1][None, :], 0.6, 1.0)
    spike_multiplier = spike_multiplier * jnp.where(token_location >= filter_spikes[2][None, :], 0.6, 1.0)
    filter_magnitude = 1.0 / jnp.sqrt(jnp.minimum(0.5 * decay_reach_scale, float(SEQUENCE_TOKENS)))
    return noisy_component * filter_magnitude * jnp.exp(-token_location / decay_reach_scale) * spike_multiplier


def block_scale(rng, extent, pieces, smallest, high):
    level, own = 1.0, jax.random.fold_in(rng, 6)
    for axis_at, parts in pieces:
        heights = jnp.exp(jax.random.uniform(jax.random.fold_in(own, axis_at), (parts,), jnp.float32, smallest / len(pieces), high / len(pieces)))
        level = level * jnp.repeat(heights, extent[axis_at] // parts).reshape([-1 if axis == axis_at else 1 for axis in range(len(extent))])
    return level


def noise(stream_key, extent, deviation, bound, split=(), held_as=jnp.bfloat16):
    array = jax.random.normal(stream_key, extent, jnp.float32) * deviation
    if len(split) > 0:
        array = block_scale(stream_key, extent, split, -0.22, 0.18) * array
    return jnp.clip(array, min=-bound, max=bound).astype(held_as)


def setup_inputs(seed: int = 0) -> dict:
    seeds = jax.random.split(jax.random.key(seed), 8)
    return {
        "query_input": noise(seeds[0], (SEQUENCE_TOKENS, MIXER_CHANNELS), 1.0, 6.0, ((0, 16), (1, 2))),
        "key_input": noise(seeds[1], (SEQUENCE_TOKENS, MIXER_CHANNELS), 1.0, 6.0, ((0, 16), (1, 2))),
        "value_input": noise(seeds[2], (SEQUENCE_TOKENS, MIXER_CHANNELS), 1.0, 6.0, ((0, 16), (1, 2))),
        "implicit_filter": draw_implicit_filter(jax.random.fold_in(seeds[7], 71), 0),
        "explicit_taps": noise(seeds[4], (MTAPS, MIXER_CHANNELS), MTAPS ** -0.5, 0.5, ((1, 2),), jnp.float32),
        "skip_gain": noise(seeds[5], (MIXER_CHANNELS,), 1.0, 3.0, ((0, 2),), jnp.float32),
        "out_grad": noise(seeds[6], (SEQUENCE_TOKENS, MIXER_CHANNELS), 1.0, 6.0, ((0, 16), (1, 2))),
    }


def causal_mix(signal, kernel):
    padded_size = 2 * signal.shape[0]
    spectrum = jnp.fft.rfft(signal, n=padded_size, axis=0) * jnp.fft.rfft(kernel, n=padded_size, axis=0)
    return jnp.fft.irfft(spectrum, n=padded_size, axis=0)[:signal.shape[0]]

def lagged_sum(later, earlier):
    padded_size = 2 * later.shape[0]
    spectrum = jnp.fft.rfft(later, n=padded_size, axis=0) * jnp.conj(jnp.fft.rfft(earlier, n=padded_size, axis=0))
    return jnp.fft.irfft(spectrum, n=padded_size, axis=0)[:later.shape[0]]

def reference(query_input, key_input, value_input, implicit_filter, explicit_taps, skip_gain, out_grad):
    query_full = query_input.astype(jnp.float32)
    key_full = key_input.astype(jnp.float32)
    value_full = value_input.astype(jnp.float32)
    grad_full = out_grad.astype(jnp.float32)
    product = key_full * value_full
    mix_grad = grad_full * query_full
    seq_length = product.shape[0]
    chan_width = product.shape[1]
    zero_rows = jnp.zeros((MTAPS, chan_width), product.dtype)
    padded_back = jnp.concatenate([zero_rows, product], axis=0)
    padded_ahead = jnp.concatenate([mix_grad, zero_rows], axis=0)

    def tap_step(tap_lag, loop_state):
        explicit_part, explicit_grad, tap_rows = loop_state
        tap_lag = tap_lag.astype(jnp.int32)
        behind_rows = lax.dynamic_slice_in_dim(padded_back, (MTAPS - tap_lag).astype(jnp.int32), seq_length, 0)
        ahead_rows = lax.dynamic_slice_in_dim(padded_ahead, tap_lag, seq_length, 0)
        tap_weight = lax.dynamic_slice_in_dim(explicit_taps, tap_lag, 1, 0)
        tap_row = lax.optimization_barrier(jnp.sum(mix_grad * behind_rows, axis=0, keepdims=True))
        return (explicit_part + tap_weight * behind_rows, explicit_grad + tap_weight * ahead_rows, lax.dynamic_update_slice_in_dim(tap_rows, tap_row, tap_lag, 0))
    start_state = (jnp.zeros_like(product), jnp.zeros_like(product), jnp.zeros((MTAPS, chan_width), product.dtype))
    explicit_part, explicit_grad, tap_rows = lax.fori_loop(0, MTAPS, tap_step, start_state)
    implicit_part = causal_mix(product, implicit_filter)
    mixer = implicit_part + explicit_part + skip_gain[None, :] * product
    mixed_output = query_full * mixer
    query_grad = grad_full * mixer
    product_grad = lagged_sum(mix_grad, implicit_filter) + explicit_grad + skip_gain[None, :] * mix_grad
    key_grad = product_grad * value_full
    value_grad = product_grad * key_full
    grad_scale = 1.0 / jnp.sqrt(jnp.float32(SEQUENCE_TOKENS))
    filter_grad = lagged_sum(mix_grad, product) * grad_scale
    taps_grad = tap_rows * grad_scale
    skip_grad = lax.optimization_barrier(jnp.sum(mix_grad * product, axis=0)) * grad_scale
    return (mixed_output, query_grad, key_grad, value_grad, filter_grad, taps_grad, skip_grad)
```

```python
import functools
import math

import jax
import jax.numpy as jnp
import numpy as np
from jax import lax
from jax.experimental import pallas as pl
from jax.experimental.pallas import tpu as pltpu
from jax.sharding import PartitionSpec as P

VMEM_LIMIT = 48 * 1024 * 1024


def turn(value, turns):
    turns = turns % 1.0
    real, imag = value
    if turns == 0.0:
        return value
    if turns == 0.5:
        return (-real, -imag)
    if turns == 0.25:
        return (-imag, real)
    if turns == 0.75:
        return (imag, -real)
    cosine, sine = math.cos(2 * math.pi * turns), math.sin(2 * math.pi * turns)
    if abs(abs(cosine) - abs(sine)) < 1e-12:
        scale = abs(cosine)
        one, two = math.copysign(1.0, cosine), math.copysign(1.0, sine)
        new_real = (real if one > 0 else -real) - (imag if two > 0 else -imag)
        new_imag = (real if two > 0 else -real) + (imag if one > 0 else -imag)
        return (new_real * scale, new_imag * scale)
    return (real * cosine - imag * sine, real * sine + imag * cosine)


def plus(a, b):
    return (a[0] + b[0], a[1] + b[1])


def minus(a, b):
    return (a[0] - b[0], a[1] - b[1])


def complex_transform(values, sign):
    count = len(values)
    if count == 1:
        return values
    even = complex_transform(values[0::2], sign)
    odd = complex_transform(values[1::2], sign)
    odd = [turn(odd[k], sign * k / count) for k in range(count // 2)]
    return [plus(e, o) for e, o in zip(even, odd)] + [minus(e, o) for e, o in zip(even, odd)]


def odd_bins(values):
    length = len(values)
    half = length // 2
    turned = [turn((values[j], -values[j + half]), -j / (2 * length)) for j in range(half)]
    bins = {}
    for m, (real, imag) in enumerate(complex_transform(turned, -1)):
        p = 4 * m + 1
        if p < length:
            bins[p] = (real, imag)
        else:
            bins[2 * length - p] = (real, -imag)
    return bins


def real_bins(values):
    length = len(values)
    if length == 2:
        return {0: (values[0] + values[1], None), 1: (values[0] - values[1], None)}
    half = length // 2
    bins = {}
    for s, value in real_bins([values[j] + values[j + half] for j in range(half)]).items():
        bins[2 * s] = value
    bins.update(odd_bins([values[j] - values[j + half] for j in range(half)]))
    return bins


def padded_bins(values):
    bins = {2 * s: value for s, value in real_bins(values).items()}
    bins.update(odd_bins(values))
    return bins


def odd_bins_back(bins, length):
    half = length // 2
    spectrum = []
    for m in range(half):
        p = 4 * m + 1
        if p < length:
            spectrum.append(bins[p])
        else:
            real, imag = bins[2 * length - p]
            spectrum.append((real, -imag))
    values = complex_transform(spectrum, 1)
    values = [turn(value, j / (2 * length)) for j, value in enumerate(values)]
    return [value[0] for value in values] + [-value[1] for value in values]


def real_bins_back(bins, length):
    if length == 2:
        return [bins[0][0] + bins[1][0], bins[0][0] - bins[1][0]]
    half = length // 2
    even = real_bins_back({s: bins[2 * s] for s in range(half // 2 + 1)}, half)
    odd = odd_bins_back(bins, half)
    return [e + o for e, o in zip(even, odd)] + [e - o for e, o in zip(even, odd)]


def padded_bins_back(bins, length):
    even = real_bins_back({s: bins[2 * s] for s in range(length // 2 + 1)}, length)
    odd = odd_bins_back(bins, length)
    return [e + o for e, o in zip(even, odd)]


def tables(blocks, rows):
    extent = 2 * blocks * rows
    positions = np.arange(rows)
    angle = 2 * np.pi * (np.outer(positions, positions) % rows) / rows
    cosine, sine = np.cos(angle), np.sin(angle)
    forward = np.block([[cosine, -sine], [sine, cosine]])
    matrices = []
    for matrix in (forward, forward.T):
        high = matrix.astype(jnp.bfloat16)
        low = (matrix - high.astype(np.float64)).astype(jnp.bfloat16)
        matrices += [high, low]
    phase = 2 * np.pi * np.outer(np.arange(blocks + 1), positions) / extent
    weight = np.where(np.arange(blocks + 1) % blocks == 0, 1.0, 2.0)[:, None] / extent
    twists = np.stack(
        [np.cos(phase), -np.sin(phase), weight * np.cos(phase), weight * np.sin(phase)], 1
    )
    return np.stack(matrices), twists.astype(np.float32)


def multiply(values, high, low):
    values_high = values.astype(jnp.bfloat16)
    values_low = (values - values_high.astype(jnp.float32)).astype(jnp.bfloat16)
    dot = functools.partial(jnp.dot, preferred_element_type=jnp.float32)
    return dot(values_high, high) + (dot(values_low, high) + dot(values_high, low))


def pack_kernel(first, query, key, value, filt, taps, skip, grad, out):
    rows, channels = query.shape
    product = key[...].astype(jnp.float32) * value[...].astype(jnp.float32)
    mix_grad = grad[...].astype(jnp.float32) * query[...].astype(jnp.float32)
    row = lax.broadcasted_iota(jnp.int32, (rows, channels), 0)
    extra = taps[...] + jnp.where(row == 0, skip[...], 0.0)
    combined = filt[...] + jnp.where(first[0] == 1, extra, 0.0)
    for a, array in enumerate((product, combined, mix_grad)):
        turned = array.T
        if len(out.shape) == 4:
            out[:, a] = turned.reshape(out.shape[0], out.shape[2], rows)
        else:
            out[a] = turned


def mix_kernel(matrices, twists, arrays, out, taps, spectra, results, *, grad_scale):
    blocks, _, channels, rows = arrays.shape
    for a in range(3):
        for low in range(0, channels, 8):
            part = pl.ds(low, 8)
            bins = padded_bins([arrays[j, a, part, :] for j in range(blocks)])
            for p in range(blocks + 1):
                real, imag = bins[p]
                cosine, sine = twists[p, 0:1, :], twists[p, 1:2, :]
                place = pl.ds(p * channels + low, 8)
                if imag is None:
                    spectra[a, place, :rows] = real * cosine
                    spectra[a, place, rows:] = real * sine
                else:
                    spectra[a, place, :rows] = real * cosine - imag * sine
                    spectra[a, place, rows:] = real * sine + imag * cosine
    forward_high, forward_low = matrices[0], matrices[1]
    back_high, back_low = matrices[2], matrices[3]
    product, filt, mix_grad = [multiply(spectra[a], forward_high, forward_low) for a in range(3)]
    pr, pi = product[:, :rows], product[:, rows:]
    fr, fi = filt[:, :rows], filt[:, rows:]
    gr, gi = mix_grad[:, :rows], mix_grad[:, rows:]
    spectra[0, :, :rows] = fr * pr - fi * pi
    spectra[0, :, rows:] = fr * pi + fi * pr
    spectra[1, :, :rows] = fr * gr + fi * gi
    spectra[1, :, rows:] = fr * gi - fi * gr
    spectra[2, :, :rows] = pr * gr + pi * gi
    spectra[2, :, rows:] = pr * gi - pi * gr
    for a in range(3):
        results[a] = multiply(spectra[a], back_high, back_low)
        for low in range(0, channels, 8):
            bins = {}
            for p in range(blocks + 1):
                cosine, sine = twists[p, 2:3, :], twists[p, 3:4, :]
                place = pl.ds(p * channels + low, 8)
                real, imag = results[a, place, :rows], results[a, place, rows:]
                new_real = real * cosine - imag * sine
                if p % blocks == 0:
                    bins[p] = (new_real, None)
                else:
                    bins[p] = (new_real, real * sine + imag * cosine)
            values = padded_bins_back(bins, blocks)
            for j in range(blocks):
                value = values[j] * grad_scale if a == 2 else values[j]
                out[j, a, pl.ds(low, 8), :] = value
                if a == 2 and j == 0:
                    taps[pl.ds(low, 8), :] = value


def unpack_kernel(query, key, value, grad, parts, first_lags, mixed, dquery, dkey, dvalue, dfilter, dtaps, dskip):
    rows, channels = query.shape

    def whole(a):
        return parts[:, a].reshape(channels, rows).T

    mixer = whole(0)
    mixed[...] = query[...].astype(jnp.float32) * mixer
    dquery[...] = grad[...].astype(jnp.float32) * mixer
    product_grad = whole(1)
    dkey[...] = product_grad * value[...].astype(jnp.float32)
    dvalue[...] = product_grad * key[...].astype(jnp.float32)
    dfilter[...] = whole(2)
    turned = first_lags[...].T
    dtaps[...] = turned
    dskip[...] = turned[0:1, :]


def call(kernel, name, out_shape, in_count, scratch=(), smem=0, flops=0, size=0):
    vmem = pl.BlockSpec(memory_space=pltpu.VMEM)
    return pl.pallas_call(
        kernel,
        name=name,
        out_shape=out_shape,
        in_specs=[pl.BlockSpec(memory_space=pltpu.SMEM)] * smem + [vmem] * in_count,
        out_specs=jax.tree.map(lambda _: vmem, out_shape),
        scratch_shapes=list(scratch),
        compiler_params=pltpu.CompilerParams(vmem_limit_bytes=VMEM_LIMIT),
        cost_estimate=pl.CostEstimate(flops=flops, bytes_accessed=size, transcendentals=0),
    )


def body(query, key, value, implicit_filter, explicit_taps, skip_gain, out_grad):
    rows, channels = query.shape
    blocks = lax.axis_size("ctx")
    share = channels // blocks
    padded = -(-share // 8) * 8
    f32 = jnp.float32
    shape = functools.partial(jax.ShapeDtypeStruct, dtype=f32)
    grad_scale = 1.0 / math.sqrt(blocks * rows)
    first = (lax.axis_index("ctx") == 0).astype(jnp.int32).reshape(1)
    direct = share == padded

    packed_shape = (blocks, 3, share, rows) if direct else (3, channels, rows)
    packed = call(pack_kernel, "pack", shape(packed_shape), 7, smem=1, size=16 * rows * channels)(
        first, query, key, value, implicit_filter, explicit_taps, skip_gain.reshape(1, channels), out_grad
    )
    if not direct:
        packed = packed.reshape(3, blocks, share, rows).swapaxes(0, 1)
    arrays = lax.all_to_all(packed, "ctx", 0, 0, tiled=True)
    if not direct:
        arrays = jnp.pad(arrays, ((0, 0), (0, 0), (0, padded - share), (0, 0)))
    matrices, twists = tables(blocks, rows)
    height = (blocks + 1) * padded
    scratch = pltpu.VMEM((3, height, 2 * rows), f32)
    results, first_lags = call(
        functools.partial(mix_kernel, grad_scale=grad_scale),
        "mix",
        (shape((blocks, 3, padded, rows)), shape((padded, rows))),
        3,
        scratch=(scratch, scratch),
        flops=36 * height * (2 * rows) ** 2,
        size=24 * blocks * padded * rows,
    )(jnp.asarray(matrices), jnp.asarray(twists), arrays)
    if not direct:
        results, first_lags = results[:, :, :share], first_lags[:share]
    first_lags = lax.all_gather(first_lags, "ctx", axis=0, tiled=True)
    parts = lax.all_to_all(results, "ctx", 0, 0, tiled=True)
    full = shape((rows, channels))
    outs = call(
        unpack_kernel,
        "unpack",
        (full,) * 6 + (shape((1, channels)),),
        6,
        size=48 * rows * channels,
    )(query, key, value, out_grad, parts, first_lags)
    return (*outs[:6], outs[6].reshape(channels))


def solution(mesh):
    in_specs = (
        P("ctx", "ch"),
        P("ctx", "ch"),
        P("ctx", "ch"),
        P("ctx", "ch"),
        P(None, "ch"),
        P("ch"),
        P("ctx", "ch"),
    )
    out_specs = (
        P("ctx", "ch"),
        P("ctx", "ch"),
        P("ctx", "ch"),
        P("ctx", "ch"),
        P("ctx", "ch"),
        P(None, "ch"),
        P("ch"),
    )
    return jax.shard_map(body, mesh=mesh, in_specs=in_specs, out_specs=out_specs, check_vma=False)
```

```python
import functools
import math

import jax
import jax.numpy as jnp
import numpy as np
from jax import lax
from jax.experimental import pallas as pl
from jax.experimental.pallas import tpu as pltpu
from jax.sharding import PartitionSpec as P

VMEM_LIMIT = 48 * 1024 * 1024


def turn(value, turns):
    turns = turns % 1.0
    real, imag = value
    if turns == 0.0:
        return value
    if turns == 0.5:
        return (-real, -imag)
    if turns == 0.25:
        return (-imag, real)
    if turns == 0.75:
        return (imag, -real)
    cosine, sine = math.cos(2 * math.pi * turns), math.sin(2 * math.pi * turns)
    if abs(abs(cosine) - abs(sine)) < 1e-12:
        scale = abs(cosine)
        one, two = math.copysign(1.0, cosine), math.copysign(1.0, sine)
        new_real = (real if one > 0 else -real) - (imag if two > 0 else -imag)
        new_imag = (real if two > 0 else -real) + (imag if one > 0 else -imag)
        return (new_real * scale, new_imag * scale)
    return (real * cosine - imag * sine, real * sine + imag * cosine)


def plus(a, b):
    return (a[0] + b[0], a[1] + b[1])


def minus(a, b):
    return (a[0] - b[0], a[1] - b[1])


def complex_transform(values, sign):
    count = len(values)
    if count == 1:
        return values
    even = complex_transform(values[0::2], sign)
    odd = complex_transform(values[1::2], sign)
    odd = [turn(odd[k], sign * k / count) for k in range(count // 2)]
    return [plus(e, o) for e, o in zip(even, odd)] + [minus(e, o) for e, o in zip(even, odd)]


def odd_bins(values):
    length = len(values)
    half = length // 2
    turned = [turn((values[j], -values[j + half]), -j / (2 * length)) for j in range(half)]
    bins = {}
    for m, (real, imag) in enumerate(complex_transform(turned, -1)):
        p = 4 * m + 1
        if p < length:
            bins[p] = (real, imag)
        else:
            bins[2 * length - p] = (real, -imag)
    return bins


def real_bins(values):
    length = len(values)
    if length == 2:
        return {0: (values[0] + values[1], None), 1: (values[0] - values[1], None)}
    half = length // 2
    bins = {}
    for s, value in real_bins([values[j] + values[j + half] for j in range(half)]).items():
        bins[2 * s] = value
    bins.update(odd_bins([values[j] - values[j + half] for j in range(half)]))
    return bins


def padded_bins(values):
    bins = {2 * s: value for s, value in real_bins(values).items()}
    bins.update(odd_bins(values))
    return bins


def odd_bins_back(bins, length):
    half = length // 2
    spectrum = []
    for m in range(half):
        p = 4 * m + 1
        if p < length:
            spectrum.append(bins[p])
        else:
            real, imag = bins[2 * length - p]
            spectrum.append((real, -imag))
    values = complex_transform(spectrum, 1)
    values = [turn(value, j / (2 * length)) for j, value in enumerate(values)]
    return [value[0] for value in values] + [-value[1] for value in values]


def real_bins_back(bins, length):
    if length == 2:
        return [bins[0][0] + bins[1][0], bins[0][0] - bins[1][0]]
    half = length // 2
    even = real_bins_back({s: bins[2 * s] for s in range(half // 2 + 1)}, half)
    odd = odd_bins_back(bins, half)
    return [e + o for e, o in zip(even, odd)] + [e - o for e, o in zip(even, odd)]


def padded_bins_back(bins, length):
    even = real_bins_back({s: bins[2 * s] for s in range(length // 2 + 1)}, length)
    odd = odd_bins_back(bins, length)
    return [e + o for e, o in zip(even, odd)]


def tables(blocks, rows):
    extent = 2 * blocks * rows
    positions = np.arange(rows)
    angle = 2 * np.pi * (np.outer(positions, positions) % rows) / rows
    cosine, sine = np.cos(angle), np.sin(angle)
    forward = np.block([[cosine, -sine], [sine, cosine]])
    matrices = []
    for matrix in (forward, forward.T):
        high = matrix.astype(jnp.bfloat16)
        low = (matrix - high.astype(np.float64)).astype(jnp.bfloat16)
        matrices += [high, low]
    phase = 2 * np.pi * np.outer(np.arange(blocks + 1), positions) / extent
    weight = np.where(np.arange(blocks + 1) % blocks == 0, 1.0, 2.0)[:, None] / extent
    twists = np.stack(
        [np.cos(phase), -np.sin(phase), weight * np.cos(phase), weight * np.sin(phase)], 1
    )
    return np.stack(matrices), twists.astype(np.float32)


def multiply(values, high, low):
    values_high = values.astype(jnp.bfloat16)
    values_low = (values - values_high.astype(jnp.float32)).astype(jnp.bfloat16)
    dot = functools.partial(jnp.dot, preferred_element_type=jnp.float32)
    return dot(values_high, high) + (dot(values_low, high) + dot(values_high, low))


def pack_kernel(first, skip, query, key, value, filt, taps, grad, out, *scratch):
    *held, arrived = scratch
    copies = [
        pltpu.make_async_copy(source, target, arrived.at[i])
        for i, (source, target) in enumerate(zip((key, value, query, grad, filt, taps), held))
    ]
    for copy in copies:
        copy.start()
    key, value, query, grad, filt, taps = held
    rows, channels = query.shape

    def put(a, array):
        turned = array.T
        if len(out.shape) == 4:
            out[:, a] = turned.reshape(out.shape[0], out.shape[2], rows)
        else:
            out[a] = turned

    copies[0].wait()
    copies[1].wait()
    put(0, key[...].astype(jnp.float32) * value[...].astype(jnp.float32))
    copies[2].wait()
    copies[3].wait()
    put(2, grad[...].astype(jnp.float32) * query[...].astype(jnp.float32))
    copies[4].wait()
    copies[5].wait()
    row = lax.broadcasted_iota(jnp.int32, (rows, channels), 0)
    extra = taps[...] + jnp.where(row == 0, skip[...], 0.0)
    put(1, filt[...] + jnp.where(first[0] == 1, extra, 0.0))


def mix_kernel(matrices, twists, arrays, out, taps, spectra, results, *, grad_scale):
    blocks, _, channels, rows = arrays.shape
    for a in range(3):
        for low in range(0, channels, 8):
            part = pl.ds(low, 8)
            bins = padded_bins([arrays[j, a, part, :] for j in range(blocks)])
            for p in range(blocks + 1):
                real, imag = bins[p]
                cosine, sine = twists[p, 0:1, :], twists[p, 1:2, :]
                place = pl.ds(p * channels + low, 8)
                if imag is None:
                    spectra[a, place, :rows] = real * cosine
                    spectra[a, place, rows:] = real * sine
                else:
                    spectra[a, place, :rows] = real * cosine - imag * sine
                    spectra[a, place, rows:] = real * sine + imag * cosine
    forward_high, forward_low = matrices[0], matrices[1]
    back_high, back_low = matrices[2], matrices[3]
    product, filt, mix_grad = [multiply(spectra[a], forward_high, forward_low) for a in range(3)]
    pr, pi = product[:, :rows], product[:, rows:]
    fr, fi = filt[:, :rows], filt[:, rows:]
    gr, gi = mix_grad[:, :rows], mix_grad[:, rows:]
    spectra[0, :, :rows] = fr * pr - fi * pi
    spectra[0, :, rows:] = fr * pi + fi * pr
    spectra[1, :, :rows] = fr * gr + fi * gi
    spectra[1, :, rows:] = fr * gi - fi * gr
    spectra[2, :, :rows] = pr * gr + pi * gi
    spectra[2, :, rows:] = pr * gi - pi * gr
    for a in range(3):
        results[a] = multiply(spectra[a], back_high, back_low)
        for low in range(0, channels, 8):
            bins = {}
            for p in range(blocks + 1):
                cosine, sine = twists[p, 2:3, :], twists[p, 3:4, :]
                place = pl.ds(p * channels + low, 8)
                real, imag = results[a, place, :rows], results[a, place, rows:]
                new_real = real * cosine - imag * sine
                if p % blocks == 0:
                    bins[p] = (new_real, None)
                else:
                    bins[p] = (new_real, real * sine + imag * cosine)
            values = padded_bins_back(bins, blocks)
            for j in range(blocks):
                value = values[j] * grad_scale if a == 2 else values[j]
                out[j, a, pl.ds(low, 8), :] = value
                if a == 2 and j == 0:
                    taps[pl.ds(low, 8), :] = value


def unpack_kernel(me, query, key, value, grad, parts, first_lags, mixed, dquery, dkey, dvalue, dfilter, dtaps, dskip, ordered, *, flips):
    rows, channels = query.shape
    blocks, share = first_lags.shape[:2]

    def whole(a):
        return parts[:, a].reshape(channels, rows).T

    mixer = whole(0)
    mixed[...] = query[...].astype(jnp.float32) * mixer
    dquery[...] = grad[...].astype(jnp.float32) * mixer
    product_grad = whole(1)
    dkey[...] = product_grad * value[...].astype(jnp.float32)
    dvalue[...] = product_grad * key[...].astype(jnp.float32)
    dfilter[...] = whole(2)
    own = sum(((me[0] >> bit) & 1) * flipped for bit, flipped in enumerate(flips))
    for source in range(blocks):
        place = sum(flipped for bit, flipped in enumerate(flips) if source >> bit & 1)
        ordered[source * share : (source + 1) * share, :] = first_lags[own ^ place]
    turned = ordered[...].T
    dtaps[...] = turned
    dskip[...] = turned[0:1, :]


def call(kernel, name, out_shape, places, scratch=(), flops=0, size=0):
    vmem = pl.BlockSpec(memory_space=pltpu.VMEM)
    return pl.pallas_call(
        kernel,
        name=name,
        out_shape=out_shape,
        in_specs=[pl.BlockSpec(memory_space=place) for place in places],
        out_specs=jax.tree.map(lambda _: vmem, out_shape),
        scratch_shapes=list(scratch),
        compiler_params=pltpu.CompilerParams(vmem_limit_bytes=VMEM_LIMIT),
        cost_estimate=pl.CostEstimate(flops=flops, bytes_accessed=size, transcendentals=0),
    )


def gather_by_distance(value, axis):
    count = lax.axis_size(axis)
    gathered = value[None]
    flips = {}
    for bit in range(count.bit_length() - 2, -1, -1):
        flips[bit] = gathered.shape[0]
        pairs = [(i, i ^ (1 << bit)) for i in range(count)]
        gathered = jnp.concatenate([gathered, lax.ppermute(gathered, axis, pairs)], axis=0)
    return gathered, [flips[bit] for bit in range(len(flips))]


def body(query, key, value, implicit_filter, explicit_taps, skip_gain, out_grad):
    rows, channels = query.shape
    blocks = lax.axis_size("ctx")
    share = channels // blocks
    padded = -(-share // 8) * 8
    f32 = jnp.float32
    shape = functools.partial(jax.ShapeDtypeStruct, dtype=f32)
    grad_scale = 1.0 / math.sqrt(blocks * rows)
    me = lax.axis_index("ctx").astype(jnp.int32).reshape(1)
    first = (me == 0).astype(jnp.int32)
    direct = share == padded

    packed_shape = (blocks, 3, share, rows) if direct else (3, channels, rows)
    half = pltpu.VMEM((rows, channels), jnp.bfloat16)
    full = pltpu.VMEM((rows, channels), f32)
    packed = call(
        pack_kernel,
        "pack",
        shape(packed_shape),
        (pltpu.SMEM, pltpu.VMEM) + (pltpu.HBM,) * 6,
        scratch=(half,) * 4 + (full,) * 2 + (pltpu.SemaphoreType.DMA((6,)),),
        size=16 * rows * channels,
    )(first, skip_gain.reshape(1, channels), query, key, value, implicit_filter, explicit_taps, out_grad)
    if not direct:
        packed = packed.reshape(3, blocks, share, rows).swapaxes(0, 1)
    arrays = lax.all_to_all(packed, "ctx", 0, 0, tiled=True)
    if not direct:
        arrays = jnp.pad(arrays, ((0, 0), (0, 0), (0, padded - share), (0, 0)))
    matrices, twists = tables(blocks, rows)
    height = (blocks + 1) * padded
    scratch = pltpu.VMEM((3, height, 2 * rows), f32)
    results, first_lags = call(
        functools.partial(mix_kernel, grad_scale=grad_scale),
        "mix",
        (shape((blocks, 3, padded, rows)), shape((padded, rows))),
        (pltpu.VMEM,) * 3,
        scratch=(scratch, scratch),
        flops=36 * height * (2 * rows) ** 2,
        size=24 * blocks * padded * rows,
    )(jnp.asarray(matrices), jnp.asarray(twists), arrays)
    if not direct:
        results, first_lags = results[:, :, :share], first_lags[:share]
    parts = lax.all_to_all(results, "ctx", 0, 0, tiled=True)
    first_lags, flips = gather_by_distance(first_lags, "ctx")
    full = shape((rows, channels))
    outs = call(
        functools.partial(unpack_kernel, flips=flips),
        "unpack",
        (full,) * 6 + (shape((1, channels)),),
        (pltpu.SMEM,) + (pltpu.VMEM,) * 6,
        scratch=(pltpu.VMEM((channels, rows), f32),),
        size=48 * rows * channels,
    )(me, query, key, value, out_grad, parts, first_lags)
    return (*outs[:6], outs[6].reshape(channels))


def solution(mesh):
    in_specs = (
        P("ctx", "ch"),
        P("ctx", "ch"),
        P("ctx", "ch"),
        P("ctx", "ch"),
        P(None, "ch"),
        P("ch"),
        P("ctx", "ch"),
    )
    out_specs = (
        P("ctx", "ch"),
        P("ctx", "ch"),
        P("ctx", "ch"),
        P("ctx", "ch"),
        P("ctx", "ch"),
        P(None, "ch"),
        P("ch"),
    )
    return jax.shard_map(body, mesh=mesh, in_specs=in_specs, out_specs=out_specs, check_vma=False)
```

```python
import functools
import math

import jax
import jax.numpy as jnp
import numpy as np
from jax import lax
from jax.experimental import pallas as pl
from jax.experimental.pallas import tpu as pltpu
from jax.sharding import PartitionSpec as P

VMEM_LIMIT = 48 * 1024 * 1024
CHUNKS = 2


def turn(value, turns):
    turns = turns % 1.0
    real, imag = value
    if turns == 0.0:
        return value
    if turns == 0.5:
        return (-real, -imag)
    if turns == 0.25:
        return (-imag, real)
    if turns == 0.75:
        return (imag, -real)
    cosine, sine = math.cos(2 * math.pi * turns), math.sin(2 * math.pi * turns)
    if abs(abs(cosine) - abs(sine)) < 1e-12:
        scale = abs(cosine)
        one, two = math.copysign(1.0, cosine), math.copysign(1.0, sine)
        new_real = (real if one > 0 else -real) - (imag if two > 0 else -imag)
        new_imag = (real if two > 0 else -real) + (imag if one > 0 else -imag)
        return (new_real * scale, new_imag * scale)
    return (real * cosine - imag * sine, real * sine + imag * cosine)


def plus(a, b):
    return (a[0] + b[0], a[1] + b[1])


def minus(a, b):
    return (a[0] - b[0], a[1] - b[1])


def complex_transform(values, sign):
    count = len(values)
    if count == 1:
        return values
    even = complex_transform(values[0::2], sign)
    odd = complex_transform(values[1::2], sign)
    odd = [turn(odd[k], sign * k / count) for k in range(count // 2)]
    return [plus(e, o) for e, o in zip(even, odd)] + [minus(e, o) for e, o in zip(even, odd)]


def odd_bins(values):
    length = len(values)
    half = length // 2
    turned = [turn((values[j], -values[j + half]), -j / (2 * length)) for j in range(half)]
    bins = {}
    for m, (real, imag) in enumerate(complex_transform(turned, -1)):
        p = 4 * m + 1
        if p < length:
            bins[p] = (real, imag)
        else:
            bins[2 * length - p] = (real, -imag)
    return bins


def real_bins(values):
    length = len(values)
    if length == 2:
        return {0: (values[0] + values[1], None), 1: (values[0] - values[1], None)}
    half = length // 2
    bins = {}
    for s, value in real_bins([values[j] + values[j + half] for j in range(half)]).items():
        bins[2 * s] = value
    bins.update(odd_bins([values[j] - values[j + half] for j in range(half)]))
    return bins


def padded_bins(values):
    bins = {2 * s: value for s, value in real_bins(values).items()}
    bins.update(odd_bins(values))
    return bins


def odd_bins_back(bins, length):
    half = length // 2
    spectrum = []
    for m in range(half):
        p = 4 * m + 1
        if p < length:
            spectrum.append(bins[p])
        else:
            real, imag = bins[2 * length - p]
            spectrum.append((real, -imag))
    values = complex_transform(spectrum, 1)
    values = [turn(value, j / (2 * length)) for j, value in enumerate(values)]
    return [value[0] for value in values] + [-value[1] for value in values]


def real_bins_back(bins, length):
    if length == 2:
        return [bins[0][0] + bins[1][0], bins[0][0] - bins[1][0]]
    half = length // 2
    even = real_bins_back({s: bins[2 * s] for s in range(half // 2 + 1)}, half)
    odd = odd_bins_back(bins, half)
    return [e + o for e, o in zip(even, odd)] + [e - o for e, o in zip(even, odd)]


def padded_bins_back(bins, length):
    even = real_bins_back({s: bins[2 * s] for s in range(length // 2 + 1)}, length)
    odd = odd_bins_back(bins, length)
    return [e + o for e, o in zip(even, odd)]


def tables(blocks, rows):
    extent = 2 * blocks * rows
    positions = np.arange(rows)
    angle = 2 * np.pi * (np.outer(positions, positions) % rows) / rows
    cosine, sine = np.cos(angle), np.sin(angle)
    forward = np.block([[cosine, -sine], [sine, cosine]])
    matrices = []
    for matrix in (forward, forward.T):
        high = matrix.astype(jnp.bfloat16)
        low = (matrix - high.astype(np.float64)).astype(jnp.bfloat16)
        matrices += [high, low]
    phase = 2 * np.pi * np.outer(np.arange(blocks + 1), positions) / extent
    weight = np.where(np.arange(blocks + 1) % blocks == 0, 1.0, 2.0)[:, None] / extent
    twists = np.stack(
        [np.cos(phase), -np.sin(phase), weight * np.cos(phase), weight * np.sin(phase)], 1
    )
    return np.stack(matrices), twists.astype(np.float32)


def multiply(values, high, low):
    values_high = values.astype(jnp.bfloat16)
    values_low = (values - values_high.astype(jnp.float32)).astype(jnp.bfloat16)
    dot = functools.partial(jnp.dot, preferred_element_type=jnp.float32)
    return dot(values_high, high) + (dot(values_low, high) + dot(values_high, low))


def pack_kernel(first, skip, query, key, value, filt, taps, grad, *rest, chunks):
    outs, held, arrived = rest[:chunks], rest[chunks:-1], rest[-1]
    copies = [
        pltpu.make_async_copy(source, target, arrived.at[i])
        for i, (source, target) in enumerate(zip((key, value, query, grad, filt, taps), held))
    ]
    for copy in copies:
        copy.start()
    key, value, query, grad, filt, taps = held
    rows, channels = query.shape

    def put(a, array):
        turned = array.T
        if len(outs[0].shape) == 3:
            outs[0][a] = turned
            return
        blocks, _, part, _ = outs[0].shape
        turned = turned.reshape(blocks, chunks * part, rows)
        for k, out in enumerate(outs):
            out[:, a] = turned[:, k * part : (k + 1) * part]

    copies[0].wait()
    copies[1].wait()
    put(0, key[...].astype(jnp.float32) * value[...].astype(jnp.float32))
    copies[2].wait()
    copies[3].wait()
    put(2, grad[...].astype(jnp.float32) * query[...].astype(jnp.float32))
    copies[4].wait()
    copies[5].wait()
    row = lax.broadcasted_iota(jnp.int32, (rows, channels), 0)
    extra = taps[...] + jnp.where(row == 0, skip[...], 0.0)
    put(1, filt[...] + jnp.where(first[0] == 1, extra, 0.0))


def mix_kernel(matrices, twists, arrays, out, taps, spectra, results, *, grad_scale):
    blocks, _, channels, rows = arrays.shape
    for a in range(3):
        for low in range(0, channels, 8):
            part = pl.ds(low, 8)
            bins = padded_bins([arrays[j, a, part, :] for j in range(blocks)])
            for p in range(blocks + 1):
                real, imag = bins[p]
                cosine, sine = twists[p, 0:1, :], twists[p, 1:2, :]
                place = pl.ds(p * channels + low, 8)
                if imag is None:
                    spectra[a, place, :rows] = real * cosine
                    spectra[a, place, rows:] = real * sine
                else:
                    spectra[a, place, :rows] = real * cosine - imag * sine
                    spectra[a, place, rows:] = real * sine + imag * cosine
    forward_high, forward_low = matrices[0], matrices[1]
    back_high, back_low = matrices[2], matrices[3]
    product, filt, mix_grad = [multiply(spectra[a], forward_high, forward_low) for a in range(3)]
    pr, pi = product[:, :rows], product[:, rows:]
    fr, fi = filt[:, :rows], filt[:, rows:]
    gr, gi = mix_grad[:, :rows], mix_grad[:, rows:]
    spectra[0, :, :rows] = fr * pr - fi * pi
    spectra[0, :, rows:] = fr * pi + fi * pr
    spectra[1, :, :rows] = fr * gr + fi * gi
    spectra[1, :, rows:] = fr * gi - fi * gr
    spectra[2, :, :rows] = pr * gr + pi * gi
    spectra[2, :, rows:] = pr * gi - pi * gr
    for a in range(3):
        results[a] = multiply(spectra[a], back_high, back_low)
        for low in range(0, channels, 8):
            bins = {}
            for p in range(blocks + 1):
                cosine, sine = twists[p, 2:3, :], twists[p, 3:4, :]
                place = pl.ds(p * channels + low, 8)
                real, imag = results[a, place, :rows], results[a, place, rows:]
                new_real = real * cosine - imag * sine
                if p % blocks == 0:
                    bins[p] = (new_real, None)
                else:
                    bins[p] = (new_real, real * sine + imag * cosine)
            values = padded_bins_back(bins, blocks)
            for j in range(blocks):
                value = values[j] * grad_scale if a == 2 else values[j]
                out[j, a, pl.ds(low, 8), :] = value
                if a == 2 and j == 0:
                    taps[pl.ds(low, 8), :] = value


def unpack_kernel(me, query, key, value, grad, *rest, chunks, high):
    parts, rest = rest[:chunks], rest[chunks:]
    *lags, mixed, dquery, dkey, dvalue, dfilter, dtaps, dskip, ordered = rest
    rows, channels = query.shape

    def whole(a):
        return jnp.concatenate([part[:, a] for part in parts], axis=1).reshape(channels, rows).T

    mixer = whole(0)
    mixed[...] = query[...].astype(jnp.float32) * mixer
    dquery[...] = grad[...].astype(jnp.float32) * mixer
    product_grad = whole(1)
    dkey[...] = product_grad * value[...].astype(jnp.float32)
    dvalue[...] = product_grad * key[...].astype(jnp.float32)
    dfilter[...] = whole(2)
    if high == 0:
        turned = lags[0][...].T
    else:
        low, share = len(lags), lags[0].shape[1]
        for near in range(low):
            for far in range(high):
                source = me[0] ^ (far * low + near)
                place = pl.ds(pl.multiple_of(source * share, share), share)
                ordered[place, :] = lags[near][far]
        turned = ordered[...].T
    dtaps[...] = turned
    dskip[...] = turned[0:1, :]


def call(kernel, name, out_shape, places, scratch=(), flops=0, size=0, limit=VMEM_LIMIT):
    vmem = pl.BlockSpec(memory_space=pltpu.VMEM)
    return pl.pallas_call(
        kernel,
        name=name,
        out_shape=out_shape,
        in_specs=[pl.BlockSpec(memory_space=place) for place in places],
        out_specs=jax.tree.map(lambda _: vmem, out_shape),
        scratch_shapes=list(scratch),
        compiler_params=pltpu.CompilerParams(vmem_limit_bytes=limit),
        cost_estimate=pl.CostEstimate(flops=flops, bytes_accessed=size, transcendentals=0),
    )


def exchange(value, axis, distance):
    return lax.ppermute(value, axis, [(i, i ^ distance) for i in range(lax.axis_size(axis))])


def gather_by_distance(value, axis):
    count = lax.axis_size(axis)
    low = 1 << (count.bit_length() - 1) // 2
    stack = jnp.stack([value] + [exchange(value, axis, far * low) for far in range(1, count // low)])
    return [stack] + [exchange(stack, axis, near) for near in range(1, low)]


def body(query, key, value, implicit_filter, explicit_taps, skip_gain, out_grad):
    rows, channels = query.shape
    blocks = lax.axis_size("ctx")
    share = channels // blocks
    direct = share % (8 * CHUNKS) == 0
    chunks = CHUNKS if direct else 1
    part = share // chunks
    padded = -(-part // 8) * 8
    f32 = jnp.float32
    shape = functools.partial(jax.ShapeDtypeStruct, dtype=f32)
    grad_scale = 1.0 / math.sqrt(blocks * rows)
    me = lax.axis_index("ctx").astype(jnp.int32).reshape(1)
    first = (me == 0).astype(jnp.int32)

    packed_shape = (blocks, 3, part, rows) if direct else (3, channels, rows)
    half = pltpu.VMEM((rows, channels), jnp.bfloat16)
    full = pltpu.VMEM((rows, channels), f32)
    packed = call(
        functools.partial(pack_kernel, chunks=chunks),
        "pack",
        (shape(packed_shape),) * chunks,
        (pltpu.SMEM, pltpu.VMEM) + (pltpu.HBM,) * 6,
        scratch=(half,) * 4 + (full,) * 2 + (pltpu.SemaphoreType.DMA((6,)),),
        size=16 * rows * channels,
        limit=None,
    )(first, skip_gain.reshape(1, channels), query, key, value, implicit_filter, explicit_taps, out_grad)
    if not direct:
        packed = [packed[0].reshape(3, blocks, share, rows).swapaxes(0, 1)]
    matrices, twists = tables(blocks, rows)
    height = (blocks + 1) * padded
    scratch = pltpu.VMEM((3, height, 2 * rows), f32)
    mix = call(
        functools.partial(mix_kernel, grad_scale=grad_scale),
        "mix",
        (shape((blocks, 3, padded, rows)), shape((padded, rows))),
        (pltpu.VMEM,) * 3,
        scratch=(scratch, scratch),
        flops=36 * height * (2 * rows) ** 2,
        size=24 * blocks * padded * rows,
    )
    parts, lags = [], []
    for chunk in packed:
        arrays = lax.all_to_all(chunk, "ctx", 0, 0, tiled=True)
        if not direct:
            arrays = jnp.pad(arrays, ((0, 0), (0, 0), (0, padded - part), (0, 0)))
        results, first_lags = mix(jnp.asarray(matrices), jnp.asarray(twists), arrays)
        if not direct:
            results, first_lags = results[:, :, :part], first_lags[:part]
        parts.append(lax.all_to_all(results, "ctx", 0, 0, tiled=True))
        lags.append(first_lags)
    first_lags = jnp.concatenate(lags, axis=0)
    if direct:
        gathered = gather_by_distance(first_lags, "ctx")
        high = gathered[0].shape[0]
    else:
        gathered = [lax.all_gather(first_lags, "ctx", axis=0, tiled=True)]
        high = 0
    full = shape((rows, channels))
    outs = call(
        functools.partial(unpack_kernel, chunks=chunks, high=high),
        "unpack",
        (full,) * 6 + (shape((1, channels)),),
        (pltpu.SMEM,) + (pltpu.VMEM,) * (4 + chunks + len(gathered)),
        scratch=(pltpu.VMEM((channels, rows), f32),),
        size=48 * rows * channels,
    )(me, query, key, value, out_grad, *parts, *gathered)
    return (*outs[:6], outs[6].reshape(channels))


def solution(mesh):
    in_specs = (
        P("ctx", "ch"),
        P("ctx", "ch"),
        P("ctx", "ch"),
        P("ctx", "ch"),
        P(None, "ch"),
        P("ch"),
        P("ctx", "ch"),
    )
    out_specs = (
        P("ctx", "ch"),
        P("ctx", "ch"),
        P("ctx", "ch"),
        P("ctx", "ch"),
        P("ctx", "ch"),
        P(None, "ch"),
        P("ch"),
    )
    return jax.shard_map(body, mesh=mesh, in_specs=in_specs, out_specs=out_specs, check_vma=False)
```

```python
import functools
import math

import jax
import jax.numpy as jnp
import numpy as np
from jax import lax
from jax.experimental import pallas as pl
from jax.experimental.pallas import tpu as pltpu
from jax.sharding import PartitionSpec as P

VMEM_LIMIT = 48 * 1024 * 1024


def turn(value, turns):
    turns = turns % 1.0
    real, imag = value
    if turns == 0.0:
        return value
    if turns == 0.5:
        return (-real, -imag)
    if turns == 0.25:
        return (-imag, real)
    if turns == 0.75:
        return (imag, -real)
    cosine, sine = math.cos(2 * math.pi * turns), math.sin(2 * math.pi * turns)
    if abs(abs(cosine) - abs(sine)) < 1e-12:
        scale = abs(cosine)
        one, two = math.copysign(1.0, cosine), math.copysign(1.0, sine)
        new_real = (real if one > 0 else -real) - (imag if two > 0 else -imag)
        new_imag = (real if two > 0 else -real) + (imag if one > 0 else -imag)
        return (new_real * scale, new_imag * scale)
    return (real * cosine - imag * sine, real * sine + imag * cosine)


def plus(a, b):
    return (a[0] + b[0], a[1] + b[1])


def minus(a, b):
    return (a[0] - b[0], a[1] - b[1])


def complex_transform(values, sign):
    count = len(values)
    if count == 1:
        return values
    even = complex_transform(values[0::2], sign)
    odd = complex_transform(values[1::2], sign)
    odd = [turn(odd[k], sign * k / count) for k in range(count // 2)]
    return [plus(e, o) for e, o in zip(even, odd)] + [minus(e, o) for e, o in zip(even, odd)]


def odd_bins(values):
    length = len(values)
    half = length // 2
    turned = [turn((values[j], -values[j + half]), -j / (2 * length)) for j in range(half)]
    bins = {}
    for m, (real, imag) in enumerate(complex_transform(turned, -1)):
        p = 4 * m + 1
        if p < length:
            bins[p] = (real, imag)
        else:
            bins[2 * length - p] = (real, -imag)
    return bins


def real_bins(values):
    length = len(values)
    if length == 2:
        return {0: (values[0] + values[1], None), 1: (values[0] - values[1], None)}
    half = length // 2
    bins = {}
    for s, value in real_bins([values[j] + values[j + half] for j in range(half)]).items():
        bins[2 * s] = value
    bins.update(odd_bins([values[j] - values[j + half] for j in range(half)]))
    return bins


def padded_bins(values):
    bins = {2 * s: value for s, value in real_bins(values).items()}
    bins.update(odd_bins(values))
    return bins


def odd_bins_back(bins, length):
    half = length // 2
    spectrum = []
    for m in range(half):
        p = 4 * m + 1
        if p < length:
            spectrum.append(bins[p])
        else:
            real, imag = bins[2 * length - p]
            spectrum.append((real, -imag))
    values = complex_transform(spectrum, 1)
    values = [turn(value, j / (2 * length)) for j, value in enumerate(values)]
    return [value[0] for value in values] + [-value[1] for value in values]


def real_bins_back(bins, length):
    if length == 2:
        return [bins[0][0] + bins[1][0], bins[0][0] - bins[1][0]]
    half = length // 2
    even = real_bins_back({s: bins[2 * s] for s in range(half // 2 + 1)}, half)
    odd = odd_bins_back(bins, half)
    return [e + o for e, o in zip(even, odd)] + [e - o for e, o in zip(even, odd)]


def padded_bins_back(bins, length):
    even = real_bins_back({s: bins[2 * s] for s in range(length // 2 + 1)}, length)
    odd = odd_bins_back(bins, length)
    return [e + o for e, o in zip(even, odd)]


def tables(blocks, rows):
    extent = 2 * blocks * rows
    positions = np.arange(rows)
    angle = 2 * np.pi * (np.outer(positions, positions) % rows) / rows
    cosine, sine = np.cos(angle), np.sin(angle)
    forward = np.block([[cosine, -sine], [sine, cosine]])
    matrices = []
    for matrix in (forward, forward.T):
        high = matrix.astype(jnp.bfloat16)
        low = (matrix - high.astype(np.float64)).astype(jnp.bfloat16)
        matrices += [high, low]
    phase = 2 * np.pi * np.outer(np.arange(blocks + 1), positions) / extent
    weight = np.where(np.arange(blocks + 1) % blocks == 0, 1.0, 2.0)[:, None] / extent
    twists = np.stack(
        [np.cos(phase), -np.sin(phase), weight * np.cos(phase), weight * np.sin(phase)], 1
    )
    return np.stack(matrices), twists.astype(np.float32)


def multiply(values, high, low):
    values_high = values.astype(jnp.bfloat16)
    values_low = (values - values_high.astype(jnp.float32)).astype(jnp.bfloat16)
    dot = functools.partial(jnp.dot, preferred_element_type=jnp.float32)
    return dot(values_high, high) + (dot(values_low, high) + dot(values_high, low))


def pack_kernel(me, first, skip, query, key, value, filt, taps, grad, *rest):
    outs, held, packed, arrived = rest[:-8], rest[-8:-2], rest[-2], rest[-1]
    copies = [
        pltpu.make_async_copy(source, target, arrived.at[i])
        for i, (source, target) in enumerate(zip((key, value, query, grad, filt, taps), held))
    ]
    for copy in copies:
        copy.start()
    key, value, query, grad, filt, taps = held
    rows, channels = query.shape
    blocks, _, share, _ = packed.shape

    def put(a, array):
        packed[:, a] = array.T.reshape(blocks, share, rows)

    copies[0].wait()
    copies[1].wait()
    put(0, key[...].astype(jnp.float32) * value[...].astype(jnp.float32))
    copies[2].wait()
    copies[3].wait()
    put(2, grad[...].astype(jnp.float32) * query[...].astype(jnp.float32))
    copies[4].wait()
    copies[5].wait()
    row = lax.broadcasted_iota(jnp.int32, (rows, channels), 0)
    extra = taps[...] + jnp.where(row == 0, skip[...], 0.0)
    put(1, filt[...] + jnp.where(first[0] == 1, extra, 0.0))
    for distance, out in enumerate(outs):
        out[...] = packed[me[0] ^ distance]


def mix_kernel(me, matrices, twists, *rest, blocks, grad_scale):
    parts, outs = rest[:blocks], rest[blocks : 2 * blocks]
    arrays, spectra, results = rest[2 * blocks :]
    _, _, channels, rows = arrays.shape
    for distance, part in enumerate(parts):
        arrays[me[0] ^ distance] = part[...]
    for a in range(3):
        for low in range(0, channels, 8):
            part = pl.ds(low, 8)
            bins = padded_bins([arrays[j, a, part, :] for j in range(blocks)])
            for p in range(blocks + 1):
                real, imag = bins[p]
                cosine, sine = twists[p, 0:1, :], twists[p, 1:2, :]
                place = pl.ds(p * channels + low, 8)
                if imag is None:
                    spectra[a, place, :rows] = real * cosine
                    spectra[a, place, rows:] = real * sine
                else:
                    spectra[a, place, :rows] = real * cosine - imag * sine
                    spectra[a, place, rows:] = real * sine + imag * cosine
    forward_high, forward_low = matrices[0], matrices[1]
    back_high, back_low = matrices[2], matrices[3]
    product, filt, mix_grad = [multiply(spectra[a], forward_high, forward_low) for a in range(3)]
    pr, pi = product[:, :rows], product[:, rows:]
    fr, fi = filt[:, :rows], filt[:, rows:]
    gr, gi = mix_grad[:, :rows], mix_grad[:, rows:]
    spectra[0, :, :rows] = fr * pr - fi * pi
    spectra[0, :, rows:] = fr * pi + fi * pr
    spectra[1, :, :rows] = fr * gr + fi * gi
    spectra[1, :, rows:] = fr * gi - fi * gr
    spectra[2, :, :rows] = pr * gr + pi * gi
    spectra[2, :, rows:] = pr * gi - pi * gr
    for a in range(3):
        results[a] = multiply(spectra[a], back_high, back_low)
        for low in range(0, channels, 8):
            bins = {}
            for p in range(blocks + 1):
                cosine, sine = twists[p, 2:3, :], twists[p, 3:4, :]
                place = pl.ds(p * channels + low, 8)
                real, imag = results[a, place, :rows], results[a, place, rows:]
                new_real = real * cosine - imag * sine
                if p % blocks == 0:
                    bins[p] = (new_real, None)
                else:
                    bins[p] = (new_real, real * sine + imag * cosine)
            values = padded_bins_back(bins, blocks)
            for j in range(blocks):
                value = values[j] * grad_scale if a == 2 else values[j]
                arrays[j, a, pl.ds(low, 8), :] = value
    for distance, out in enumerate(outs):
        out[:3] = arrays[me[0] ^ distance]
        if out.shape[0] == 4:
            out[3] = arrays[0, 2]


def unpack_kernel(me, query, key, value, grad, *rest, blocks, low, lag_place):
    parts, rest = rest[:blocks], rest[blocks:]
    mixed, dquery, dkey, dvalue, dfilter, dtaps, dskip, arrays, first_lags = rest
    rows, channels = query.shape
    for distance, part in enumerate(parts):
        arrays[me[0] ^ distance] = part[:3]
        if distance < low:
            for far in range(blocks // low):
                holder, place = lag_place(distance, far)
                first_lags[me[0] ^ (far * low + distance)] = parts[holder][place]

    def whole(a):
        return arrays[:, a].reshape(channels, rows).T

    mixer = whole(0)
    mixed[...] = query[...].astype(jnp.float32) * mixer
    dquery[...] = grad[...].astype(jnp.float32) * mixer
    product_grad = whole(1)
    dkey[...] = product_grad * value[...].astype(jnp.float32)
    dvalue[...] = product_grad * key[...].astype(jnp.float32)
    dfilter[...] = whole(2)
    turned = first_lags[...].reshape(channels, rows).T
    dtaps[...] = turned
    dskip[...] = turned[0:1, :]


def call(kernel, name, out_shape, places, scratch=(), flops=0, size=0, limit=VMEM_LIMIT):
    vmem = pl.BlockSpec(memory_space=pltpu.VMEM)
    return pl.pallas_call(
        kernel,
        name=name,
        out_shape=out_shape,
        in_specs=[pl.BlockSpec(memory_space=place) for place in places],
        out_specs=jax.tree.map(lambda _: vmem, out_shape),
        scratch_shapes=list(scratch),
        compiler_params=pltpu.CompilerParams(vmem_limit_bytes=limit),
        cost_estimate=pl.CostEstimate(flops=flops, bytes_accessed=size, transcendentals=0),
    )


def exchange(value, axis, distance):
    return lax.ppermute(value, axis, [(i, i ^ distance) for i in range(lax.axis_size(axis))])


def send_all(parts, axis):
    received = list(parts)
    for distance in range(len(parts) - 1, 0, -1):
        received[distance] = exchange(parts[distance], axis, distance)
    return received


def send_all_with_lags(parts, axis, low):
    received = list(parts)
    for distance in range(len(parts) - 1, low - 1, -1):
        received[distance] = exchange(parts[distance], axis, distance)
    lags = [received[far][3:4] for far in range(0, len(parts), low)]
    for distance in range(low - 1, 0, -1):
        payload = jnp.concatenate([parts[distance]] + lags, axis=0)
        received[distance] = exchange(payload, axis, distance)
    return received


def body(query, key, value, implicit_filter, explicit_taps, skip_gain, out_grad):
    rows, channels = query.shape
    blocks = lax.axis_size("ctx")
    share = channels // blocks
    direct = share % 8 == 0
    padded = -(-share // 8) * 8
    low = 1 << (blocks.bit_length() - 1) // 2 if direct else 1
    f32 = jnp.float32
    shape = functools.partial(jax.ShapeDtypeStruct, dtype=f32)
    grad_scale = 1.0 / math.sqrt(blocks * rows)
    index = lax.axis_index("ctx").astype(jnp.int32).reshape(1)
    first = (index == 0).astype(jnp.int32)
    me = index if direct else jnp.zeros_like(index)

    half = pltpu.VMEM((rows, channels), jnp.bfloat16)
    full = pltpu.VMEM((rows, channels), f32)
    parts = call(
        pack_kernel,
        "pack",
        (shape((3, share, rows)),) * blocks,
        (pltpu.SMEM, pltpu.SMEM, pltpu.VMEM) + (pltpu.HBM,) * 6,
        scratch=(half,) * 4 + (full,) * 2 + (pltpu.VMEM((blocks, 3, share, rows), f32), pltpu.SemaphoreType.DMA((6,))),
        size=16 * rows * channels,
        limit=None,
    )(me, first, skip_gain.reshape(1, channels), query, key, value, implicit_filter, explicit_taps, out_grad)
    if direct:
        parts = send_all(parts, "ctx")
    else:
        arrays = lax.all_to_all(jnp.stack(parts), "ctx", 0, 0, tiled=True)
        parts = list(jnp.pad(arrays, ((0, 0), (0, 0), (0, padded - share), (0, 0))))

    matrices, twists = tables(blocks, rows)
    height = (blocks + 1) * padded
    scratch = pltpu.VMEM((3, height, 2 * rows), f32)
    depth = [4 if distance % low == 0 else 3 for distance in range(blocks)]
    parts = call(
        functools.partial(mix_kernel, blocks=blocks, grad_scale=grad_scale),
        "mix",
        tuple(shape((count, padded, rows)) for count in depth),
        (pltpu.SMEM,) + (pltpu.VMEM,) * (2 + blocks),
        scratch=(pltpu.VMEM((blocks, 3, padded, rows), f32), scratch, scratch),
        flops=36 * height * (2 * rows) ** 2,
        size=24 * blocks * padded * rows,
    )(me, jnp.asarray(matrices), jnp.asarray(twists), *parts)
    if direct:
        parts = send_all_with_lags(parts, "ctx", low)
    else:
        parts = list(lax.all_to_all(jnp.stack(parts)[:, :, :share], "ctx", 0, 0, tiled=True))

    def lag_place(near, far):
        if near == 0:
            return far * low, 3
        return near, 3 + far

    full = shape((rows, channels))
    outs = call(
        functools.partial(unpack_kernel, blocks=blocks, low=low, lag_place=lag_place),
        "unpack",
        (full,) * 6 + (shape((1, channels)),),
        (pltpu.SMEM,) + (pltpu.VMEM,) * (4 + blocks),
        scratch=(pltpu.VMEM((blocks, 3, share, rows), f32), pltpu.VMEM((blocks, share, rows), f32)),
        size=48 * rows * channels,
    )(me, query, key, value, out_grad, *parts)
    return (*outs[:6], outs[6].reshape(channels))


def solution(mesh):
    in_specs = (
        P("ctx", "ch"),
        P("ctx", "ch"),
        P("ctx", "ch"),
        P("ctx", "ch"),
        P(None, "ch"),
        P("ch"),
        P("ctx", "ch"),
    )
    out_specs = (
        P("ctx", "ch"),
        P("ctx", "ch"),
        P("ctx", "ch"),
        P("ctx", "ch"),
        P("ctx", "ch"),
        P(None, "ch"),
        P("ch"),
    )
    return jax.shard_map(body, mesh=mesh, in_specs=in_specs, out_specs=out_specs, check_vma=False)
```

```python
import functools
import math

import jax
import jax.numpy as jnp
import numpy as np
from jax import lax
from jax.experimental import pallas as pl
from jax.experimental.pallas import tpu as pltpu
from jax.sharding import PartitionSpec as P

VMEM_LIMIT = 48 * 1024 * 1024
IN_FLIGHT = 5


def turn(value, turns):
    turns = turns % 1.0
    real, imag = value
    if turns == 0.0:
        return value
    if turns == 0.5:
        return (-real, -imag)
    if turns == 0.25:
        return (-imag, real)
    if turns == 0.75:
        return (imag, -real)
    cosine, sine = math.cos(2 * math.pi * turns), math.sin(2 * math.pi * turns)
    if abs(abs(cosine) - abs(sine)) < 1e-12:
        scale = abs(cosine)
        one, two = math.copysign(1.0, cosine), math.copysign(1.0, sine)
        new_real = (real if one > 0 else -real) - (imag if two > 0 else -imag)
        new_imag = (real if two > 0 else -real) + (imag if one > 0 else -imag)
        return (new_real * scale, new_imag * scale)
    return (real * cosine - imag * sine, real * sine + imag * cosine)


def plus(a, b):
    return (a[0] + b[0], a[1] + b[1])


def minus(a, b):
    return (a[0] - b[0], a[1] - b[1])


def complex_transform(values, sign):
    count = len(values)
    if count == 1:
        return values
    even = complex_transform(values[0::2], sign)
    odd = complex_transform(values[1::2], sign)
    odd = [turn(odd[k], sign * k / count) for k in range(count // 2)]
    return [plus(e, o) for e, o in zip(even, odd)] + [minus(e, o) for e, o in zip(even, odd)]


def odd_bins(values):
    length = len(values)
    half = length // 2
    turned = [turn((values[j], -values[j + half]), -j / (2 * length)) for j in range(half)]
    bins = {}
    for m, (real, imag) in enumerate(complex_transform(turned, -1)):
        p = 4 * m + 1
        if p < length:
            bins[p] = (real, imag)
        else:
            bins[2 * length - p] = (real, -imag)
    return bins


def real_bins(values):
    length = len(values)
    if length == 2:
        return {0: (values[0] + values[1], None), 1: (values[0] - values[1], None)}
    half = length // 2
    bins = {}
    for s, value in real_bins([values[j] + values[j + half] for j in range(half)]).items():
        bins[2 * s] = value
    bins.update(odd_bins([values[j] - values[j + half] for j in range(half)]))
    return bins


def padded_bins(values):
    bins = {2 * s: value for s, value in real_bins(values).items()}
    bins.update(odd_bins(values))
    return bins


def odd_bins_back(bins, length):
    half = length // 2
    spectrum = []
    for m in range(half):
        p = 4 * m + 1
        if p < length:
            spectrum.append(bins[p])
        else:
            real, imag = bins[2 * length - p]
            spectrum.append((real, -imag))
    values = complex_transform(spectrum, 1)
    values = [turn(value, j / (2 * length)) for j, value in enumerate(values)]
    return [value[0] for value in values] + [-value[1] for value in values]


def real_bins_back(bins, length):
    if length == 2:
        return [bins[0][0] + bins[1][0], bins[0][0] - bins[1][0]]
    half = length // 2
    even = real_bins_back({s: bins[2 * s] for s in range(half // 2 + 1)}, half)
    odd = odd_bins_back(bins, half)
    return [e + o for e, o in zip(even, odd)] + [e - o for e, o in zip(even, odd)]


def padded_bins_back(bins, length):
    even = real_bins_back({s: bins[2 * s] for s in range(length // 2 + 1)}, length)
    odd = odd_bins_back(bins, length)
    return [e + o for e, o in zip(even, odd)]


def tables(blocks, rows):
    extent = 2 * blocks * rows
    positions = np.arange(rows)
    angle = 2 * np.pi * (np.outer(positions, positions) % rows) / rows
    cosine, sine = np.cos(angle), np.sin(angle)
    forward = np.block([[cosine, -sine], [sine, cosine]])
    matrices = []
    for matrix in (forward, forward.T):
        high = matrix.astype(jnp.bfloat16)
        low = (matrix - high.astype(np.float64)).astype(jnp.bfloat16)
        matrices += [high, low]
    phase = 2 * np.pi * np.outer(np.arange(blocks + 1), positions) / extent
    weight = np.where(np.arange(blocks + 1) % blocks == 0, 1.0, 2.0)[:, None] / extent
    twists = np.stack(
        [np.cos(phase), -np.sin(phase), weight * np.cos(phase), weight * np.sin(phase)], 1
    )
    return np.stack(matrices), twists.astype(np.float32)


def multiply(values, high, low):
    values_high = values.astype(jnp.bfloat16)
    values_low = (values - values_high.astype(jnp.float32)).astype(jnp.bfloat16)
    dot = functools.partial(jnp.dot, preferred_element_type=jnp.float32)
    return dot(values_high, high) + (dot(values_low, high) + dot(values_high, low))


def pack_kernel(me, first, skip, query, key, value, filt, taps, grad, *rest):
    outs, held, packed, arrived = rest[:-8], rest[-8:-2], rest[-2], rest[-1]
    copies = [
        pltpu.make_async_copy(source, target, arrived.at[i])
        for i, (source, target) in enumerate(zip((key, value, query, grad, filt, taps), held))
    ]
    for copy in copies:
        copy.start()
    key, value, query, grad, filt, taps = held
    rows, channels = query.shape
    blocks, _, share, _ = packed.shape

    def put(a, array):
        packed[:, a] = array.T.reshape(blocks, share, rows)

    copies[0].wait()
    copies[1].wait()
    put(0, key[...].astype(jnp.float32) * value[...].astype(jnp.float32))
    copies[2].wait()
    copies[3].wait()
    put(2, grad[...].astype(jnp.float32) * query[...].astype(jnp.float32))
    copies[4].wait()
    copies[5].wait()
    row = lax.broadcasted_iota(jnp.int32, (rows, channels), 0)
    extra = taps[...] + jnp.where(row == 0, skip[...], 0.0)
    put(1, filt[...] + jnp.where(first[0] == 1, extra, 0.0))
    for distance, out in enumerate(outs):
        out[...] = packed[me[0] ^ distance]


def mix_kernel(me, matrices, twists, *rest, order, grad_scale):
    blocks = len(order)
    parts, outs = rest[:blocks], rest[blocks : 2 * blocks]
    arrays, spectra, results = rest[2 * blocks :]
    _, _, channels, rows = arrays.shape
    for distance, part in zip(order, parts):
        arrays[me[0] ^ distance] = part[...]
    for a in range(3):
        for low in range(0, channels, 8):
            part = pl.ds(low, 8)
            bins = padded_bins([arrays[j, a, part, :] for j in range(blocks)])
            for p in range(blocks + 1):
                real, imag = bins[p]
                cosine, sine = twists[p, 0:1, :], twists[p, 1:2, :]
                place = pl.ds(p * channels + low, 8)
                if imag is None:
                    spectra[a, place, :rows] = real * cosine
                    spectra[a, place, rows:] = real * sine
                else:
                    spectra[a, place, :rows] = real * cosine - imag * sine
                    spectra[a, place, rows:] = real * sine + imag * cosine
    forward_high, forward_low = matrices[0], matrices[1]
    back_high, back_low = matrices[2], matrices[3]
    product, filt, mix_grad = [multiply(spectra[a], forward_high, forward_low) for a in range(3)]
    pr, pi = product[:, :rows], product[:, rows:]
    fr, fi = filt[:, :rows], filt[:, rows:]
    gr, gi = mix_grad[:, :rows], mix_grad[:, rows:]
    spectra[0, :, :rows] = fr * pr - fi * pi
    spectra[0, :, rows:] = fr * pi + fi * pr
    spectra[1, :, :rows] = fr * gr + fi * gi
    spectra[1, :, rows:] = fr * gi - fi * gr
    spectra[2, :, :rows] = pr * gr + pi * gi
    spectra[2, :, rows:] = pr * gi - pi * gr
    for a in range(3):
        results[a] = multiply(spectra[a], back_high, back_low)
        for low in range(0, channels, 8):
            bins = {}
            for p in range(blocks + 1):
                cosine, sine = twists[p, 2:3, :], twists[p, 3:4, :]
                place = pl.ds(p * channels + low, 8)
                real, imag = results[a, place, :rows], results[a, place, rows:]
                new_real = real * cosine - imag * sine
                if p % blocks == 0:
                    bins[p] = (new_real, None)
                else:
                    bins[p] = (new_real, real * sine + imag * cosine)
            values = padded_bins_back(bins, blocks)
            for j in range(blocks):
                value = values[j] * grad_scale if a == 2 else values[j]
                arrays[j, a, pl.ds(low, 8), :] = value
    for distance, out in enumerate(outs):
        out[:3] = arrays[me[0] ^ distance]
        if out.shape[0] == 4:
            out[3] = arrays[0, 2]


def unpack_kernel(me, query, key, value, grad, *rest, order, low, lag_place):
    blocks = len(order)
    parts, rest = dict(zip(order, rest[:blocks])), rest[blocks:]
    mixed, dquery, dkey, dvalue, dfilter, dtaps, dskip, arrays, first_lags = rest
    rows, channels = query.shape
    for distance, part in parts.items():
        arrays[me[0] ^ distance] = part[:3]
        if distance < low:
            for far in range(blocks // low):
                holder, place = lag_place(distance, far)
                first_lags[me[0] ^ (far * low + distance)] = parts[holder][place]

    def whole(a):
        return arrays[:, a].reshape(channels, rows).T

    mixer = whole(0)
    mixed[...] = query[...].astype(jnp.float32) * mixer
    dquery[...] = grad[...].astype(jnp.float32) * mixer
    product_grad = whole(1)
    dkey[...] = product_grad * value[...].astype(jnp.float32)
    dvalue[...] = product_grad * key[...].astype(jnp.float32)
    dfilter[...] = whole(2)
    turned = first_lags[...].reshape(channels, rows).T
    dtaps[...] = turned
    dskip[...] = turned[0:1, :]


def call(kernel, name, out_shape, places, scratch=(), flops=0, size=0, limit=VMEM_LIMIT):
    vmem = pl.BlockSpec(memory_space=pltpu.VMEM)
    return pl.pallas_call(
        kernel,
        name=name,
        out_shape=out_shape,
        in_specs=[pl.BlockSpec(memory_space=place) for place in places],
        out_specs=jax.tree.map(lambda _: vmem, out_shape),
        scratch_shapes=list(scratch),
        compiler_params=pltpu.CompilerParams(vmem_limit_bytes=limit),
        cost_estimate=pl.CostEstimate(flops=flops, bytes_accessed=size, transcendentals=0),
    )


def exchange(value, axis, distance):
    return lax.ppermute(value, axis, [(i, i ^ distance) for i in range(lax.axis_size(axis))])


def send_all(parts, axis, order, low=0):
    received, started = {0: parts[0]}, []
    for distance in order[1:]:
        payload = parts[distance]
        if distance < low:
            lags = [received[far][3:4] for far in range(0, len(parts), low)]
            payload = jnp.concatenate([payload] + lags, axis=0)
        if len(started) >= IN_FLIGHT:
            earlier = started[-IN_FLIGHT]
            payload, received[earlier] = lax.optimization_barrier((payload, received[earlier]))
        received[distance] = exchange(payload, axis, distance)
        started.append(distance)
    return received


def send_order(count, early):
    crossing = [d for d in range(count // 2, count) if d not in early]
    others = [d for d in range(count // 2 - 1, 0, -1) if d not in early]
    order = sorted(early, reverse=True)
    while crossing or others:
        order += [group.pop(0) for group in (crossing, others) if group]
    return [0] + order


def body(query, key, value, implicit_filter, explicit_taps, skip_gain, out_grad):
    rows, channels = query.shape
    blocks = lax.axis_size("ctx")
    share = channels // blocks
    direct = share % 8 == 0
    padded = -(-share // 8) * 8
    low = 1 << (blocks.bit_length() - 1) // 2 if direct else 1
    f32 = jnp.float32
    shape = functools.partial(jax.ShapeDtypeStruct, dtype=f32)
    grad_scale = 1.0 / math.sqrt(blocks * rows)
    index = lax.axis_index("ctx").astype(jnp.int32).reshape(1)
    first = (index == 0).astype(jnp.int32)
    me = index if direct else jnp.zeros_like(index)

    order_in = send_order(blocks, [])
    order_out = send_order(blocks, range(low, blocks, low))

    half = pltpu.VMEM((rows, channels), jnp.bfloat16)
    full = pltpu.VMEM((rows, channels), f32)
    parts = call(
        pack_kernel,
        "pack",
        (shape((3, share, rows)),) * blocks,
        (pltpu.SMEM, pltpu.SMEM, pltpu.VMEM) + (pltpu.HBM,) * 6,
        scratch=(half,) * 4 + (full,) * 2 + (pltpu.VMEM((blocks, 3, share, rows), f32), pltpu.SemaphoreType.DMA((6,))),
        size=16 * rows * channels,
        limit=None,
    )(me, first, skip_gain.reshape(1, channels), query, key, value, implicit_filter, explicit_taps, out_grad)
    if direct:
        parts = send_all(parts, "ctx", order_in)
    else:
        arrays = lax.all_to_all(jnp.stack(parts), "ctx", 0, 0, tiled=True)
        parts = list(jnp.pad(arrays, ((0, 0), (0, 0), (0, padded - share), (0, 0))))

    matrices, twists = tables(blocks, rows)
    height = (blocks + 1) * padded
    scratch = pltpu.VMEM((3, height, 2 * rows), f32)
    depth = [4 if distance % low == 0 else 3 for distance in range(blocks)]
    parts = call(
        functools.partial(mix_kernel, order=order_in, grad_scale=grad_scale),
        "mix",
        tuple(shape((count, padded, rows)) for count in depth),
        (pltpu.SMEM,) + (pltpu.VMEM,) * (2 + blocks),
        scratch=(pltpu.VMEM((blocks, 3, padded, rows), f32), scratch, scratch),
        flops=36 * height * (2 * rows) ** 2,
        size=24 * blocks * padded * rows,
    )(me, jnp.asarray(matrices), jnp.asarray(twists), *[parts[distance] for distance in order_in])
    if direct:
        parts = send_all(parts, "ctx", order_out, low)
    else:
        parts = list(lax.all_to_all(jnp.stack(parts)[:, :, :share], "ctx", 0, 0, tiled=True))

    def lag_place(near, far):
        if near == 0:
            return far * low, 3
        return near, 3 + far

    full = shape((rows, channels))
    outs = call(
        functools.partial(unpack_kernel, order=order_out, low=low, lag_place=lag_place),
        "unpack",
        (full,) * 6 + (shape((1, channels)),),
        (pltpu.SMEM,) + (pltpu.VMEM,) * (4 + blocks),
        scratch=(pltpu.VMEM((blocks, 3, share, rows), f32), pltpu.VMEM((blocks, share, rows), f32)),
        size=48 * rows * channels,
    )(me, query, key, value, out_grad, *[parts[distance] for distance in order_out])
    return (*outs[:6], outs[6].reshape(channels))


def solution(mesh):
    in_specs = (
        P("ctx", "ch"),
        P("ctx", "ch"),
        P("ctx", "ch"),
        P("ctx", "ch"),
        P(None, "ch"),
        P("ch"),
        P("ctx", "ch"),
    )
    out_specs = (
        P("ctx", "ch"),
        P("ctx", "ch"),
        P("ctx", "ch"),
        P("ctx", "ch"),
        P("ctx", "ch"),
        P(None, "ch"),
        P("ch"),
    )
    return jax.shard_map(body, mesh=mesh, in_specs=in_specs, out_specs=out_specs, check_vma=False)
```

```python
import functools
import math

import jax
import jax.numpy as jnp
import numpy as np
from jax import lax
from jax.experimental import pallas as pl
from jax.experimental.pallas import tpu as pltpu
from jax.sharding import PartitionSpec as P

VMEM_LIMIT = 48 * 1024 * 1024


def turn(value, turns):
    turns = turns % 1.0
    real, imag = value
    if turns == 0.0:
        return value
    if turns == 0.5:
        return (-real, -imag)
    if turns == 0.25:
        return (-imag, real)
    if turns == 0.75:
        return (imag, -real)
    cosine, sine = math.cos(2 * math.pi * turns), math.sin(2 * math.pi * turns)
    if abs(abs(cosine) - abs(sine)) < 1e-12:
        scale = abs(cosine)
        one, two = math.copysign(1.0, cosine), math.copysign(1.0, sine)
        new_real = (real if one > 0 else -real) - (imag if two > 0 else -imag)
        new_imag = (real if two > 0 else -real) + (imag if one > 0 else -imag)
        return (new_real * scale, new_imag * scale)
    return (real * cosine - imag * sine, real * sine + imag * cosine)


def plus(a, b):
    return (a[0] + b[0], a[1] + b[1])


def minus(a, b):
    return (a[0] - b[0], a[1] - b[1])


def complex_transform(values, sign):
    count = len(values)
    if count == 1:
        return values
    even = complex_transform(values[0::2], sign)
    odd = complex_transform(values[1::2], sign)
    odd = [turn(odd[k], sign * k / count) for k in range(count // 2)]
    return [plus(e, o) for e, o in zip(even, odd)] + [minus(e, o) for e, o in zip(even, odd)]


def odd_bins(values):
    length = len(values)
    half = length // 2
    turned = [turn((values[j], -values[j + half]), -j / (2 * length)) for j in range(half)]
    bins = {}
    for m, (real, imag) in enumerate(complex_transform(turned, -1)):
        p = 4 * m + 1
        if p < length:
            bins[p] = (real, imag)
        else:
            bins[2 * length - p] = (real, -imag)
    return bins


def real_bins(values):
    length = len(values)
    if length == 2:
        return {0: (values[0] + values[1], None), 1: (values[0] - values[1], None)}
    half = length // 2
    bins = {}
    for s, value in real_bins([values[j] + values[j + half] for j in range(half)]).items():
        bins[2 * s] = value
    bins.update(odd_bins([values[j] - values[j + half] for j in range(half)]))
    return bins


def padded_bins(values):
    bins = {2 * s: value for s, value in real_bins(values).items()}
    bins.update(odd_bins(values))
    return bins


def odd_bins_back(bins, length):
    half = length // 2
    spectrum = []
    for m in range(half):
        p = 4 * m + 1
        if p < length:
            spectrum.append(bins[p])
        else:
            real, imag = bins[2 * length - p]
            spectrum.append((real, -imag))
    values = complex_transform(spectrum, 1)
    values = [turn(value, j / (2 * length)) for j, value in enumerate(values)]
    return [value[0] for value in values] + [-value[1] for value in values]


def real_bins_back(bins, length):
    if length == 2:
        return [bins[0][0] + bins[1][0], bins[0][0] - bins[1][0]]
    half = length // 2
    even = real_bins_back({s: bins[2 * s] for s in range(half // 2 + 1)}, half)
    odd = odd_bins_back(bins, half)
    return [e + o for e, o in zip(even, odd)] + [e - o for e, o in zip(even, odd)]


def padded_bins_back(bins, length):
    even = real_bins_back({s: bins[2 * s] for s in range(length // 2 + 1)}, length)
    odd = odd_bins_back(bins, length)
    return [e + o for e, o in zip(even, odd)]


def tables(blocks, rows):
    extent = 2 * blocks * rows
    positions = np.arange(rows)
    angle = 2 * np.pi * (np.outer(positions, positions) % rows) / rows
    cosine, sine = np.cos(angle), np.sin(angle)
    forward = np.block([[cosine, -sine], [sine, cosine]])
    matrices = []
    for matrix in (forward, forward.T):
        high = matrix.astype(jnp.bfloat16)
        low = (matrix - high.astype(np.float64)).astype(jnp.bfloat16)
        matrices += [high, low]
    phase = 2 * np.pi * np.outer(np.arange(blocks + 1), positions) / extent
    weight = np.where(np.arange(blocks + 1) % blocks == 0, 1.0, 2.0)[:, None] / extent
    twists = np.stack(
        [np.cos(phase), -np.sin(phase), weight * np.cos(phase), weight * np.sin(phase)], 1
    )
    return np.stack(matrices), twists.astype(np.float32)


def multiply(values, high, low):
    values_high = values.astype(jnp.bfloat16)
    values_low = (values - values_high.astype(jnp.float32)).astype(jnp.bfloat16)
    dot = functools.partial(jnp.dot, preferred_element_type=jnp.float32)
    return dot(values_high, high) + (dot(values_low, high) + dot(values_high, low))


def pack_kernel(first, skip, query, key, value, filt, taps, grad, out, *scratch):
    *held, arrived = scratch
    copies = [
        pltpu.make_async_copy(source, target, arrived.at[i])
        for i, (source, target) in enumerate(zip((key, value, query, grad, filt, taps), held))
    ]
    for copy in copies:
        copy.start()
    key, value, query, grad, filt, taps = held
    rows, channels = query.shape
    blocks, _, share, _ = out.shape

    def put(a, array):
        out[:, a] = array.T.reshape(blocks, share, rows)

    copies[0].wait()
    copies[1].wait()
    put(0, key[...].astype(jnp.float32) * value[...].astype(jnp.float32))
    copies[2].wait()
    copies[3].wait()
    put(2, grad[...].astype(jnp.float32) * query[...].astype(jnp.float32))
    copies[4].wait()
    copies[5].wait()
    row = lax.broadcasted_iota(jnp.int32, (rows, channels), 0)
    extra = taps[...] + jnp.where(row == 0, skip[...], 0.0)
    put(1, filt[...] + jnp.where(first[0] == 1, extra, 0.0))


def mix_kernel(matrices, twists, arrays, out, spectra, results, *, grad_scale):
    blocks, _, channels, rows = arrays.shape
    for a in range(3):
        for low in range(0, channels, 8):
            part = pl.ds(low, 8)
            bins = padded_bins([arrays[j, a, part, :] for j in range(blocks)])
            for p in range(blocks + 1):
                real, imag = bins[p]
                cosine, sine = twists[p, 0:1, :], twists[p, 1:2, :]
                place = pl.ds(p * channels + low, 8)
                if imag is None:
                    spectra[a, place, :rows] = real * cosine
                    spectra[a, place, rows:] = real * sine
                else:
                    spectra[a, place, :rows] = real * cosine - imag * sine
                    spectra[a, place, rows:] = real * sine + imag * cosine
    forward_high, forward_low = matrices[0], matrices[1]
    back_high, back_low = matrices[2], matrices[3]
    product, filt, mix_grad = [multiply(spectra[a], forward_high, forward_low) for a in range(3)]
    pr, pi = product[:, :rows], product[:, rows:]
    fr, fi = filt[:, :rows], filt[:, rows:]
    gr, gi = mix_grad[:, :rows], mix_grad[:, rows:]
    spectra[0, :, :rows] = fr * pr - fi * pi
    spectra[0, :, rows:] = fr * pi + fi * pr
    spectra[1, :, :rows] = fr * gr + fi * gi
    spectra[1, :, rows:] = fr * gi - fi * gr
    spectra[2, :, :rows] = pr * gr + pi * gi
    spectra[2, :, rows:] = pr * gi - pi * gr
    for a in range(3):
        results[a] = multiply(spectra[a], back_high, back_low)
        for low in range(0, channels, 8):
            bins = {}
            for p in range(blocks + 1):
                cosine, sine = twists[p, 2:3, :], twists[p, 3:4, :]
                place = pl.ds(p * channels + low, 8)
                real, imag = results[a, place, :rows], results[a, place, rows:]
                new_real = real * cosine - imag * sine
                if p % blocks == 0:
                    bins[p] = (new_real, None)
                else:
                    bins[p] = (new_real, real * sine + imag * cosine)
            values = padded_bins_back(bins, blocks)
            for j in range(blocks):
                value = values[j] * grad_scale if a == 2 else values[j]
                out[j, a, pl.ds(low, 8), :] = value
            if a == 2:
                for j in range(blocks):
                    out[j, 3, pl.ds(low, 8), :] = values[0] * grad_scale


def unpack_kernel(query, key, value, grad, parts, mixed, dquery, dkey, dvalue, dfilter, dtaps, dskip):
    rows, channels = query.shape

    def whole(a):
        return parts[:, a].reshape(channels, rows).T

    mixer = whole(0)
    mixed[...] = query[...].astype(jnp.float32) * mixer
    dquery[...] = grad[...].astype(jnp.float32) * mixer
    product_grad = whole(1)
    dkey[...] = product_grad * value[...].astype(jnp.float32)
    dvalue[...] = product_grad * key[...].astype(jnp.float32)
    dfilter[...] = whole(2)
    first_lags = whole(3)
    dtaps[...] = first_lags
    dskip[...] = first_lags[0:1, :]


def call(kernel, name, out_shape, places, scratch=(), flops=0, size=0, limit=VMEM_LIMIT):
    vmem = pl.BlockSpec(memory_space=pltpu.VMEM)
    return pl.pallas_call(
        kernel,
        name=name,
        out_shape=out_shape,
        in_specs=[pl.BlockSpec(memory_space=place) for place in places],
        out_specs=jax.tree.map(lambda _: vmem, out_shape),
        scratch_shapes=list(scratch),
        compiler_params=pltpu.CompilerParams(vmem_limit_bytes=limit),
        cost_estimate=pl.CostEstimate(flops=flops, bytes_accessed=size, transcendentals=0),
    )


def body(query, key, value, implicit_filter, explicit_taps, skip_gain, out_grad):
    rows, channels = query.shape
    blocks = lax.axis_size("ctx")
    share = channels // blocks
    padded = -(-share // 8) * 8
    f32 = jnp.float32
    shape = functools.partial(jax.ShapeDtypeStruct, dtype=f32)
    grad_scale = 1.0 / math.sqrt(blocks * rows)
    first = (lax.axis_index("ctx") == 0).astype(jnp.int32).reshape(1)

    half = pltpu.VMEM((rows, channels), jnp.bfloat16)
    full = pltpu.VMEM((rows, channels), f32)
    packed = call(
        pack_kernel,
        "pack",
        shape((blocks, 3, share, rows)),
        (pltpu.SMEM, pltpu.VMEM) + (pltpu.HBM,) * 6,
        scratch=(half,) * 4 + (full,) * 2 + (pltpu.SemaphoreType.DMA((6,)),),
        size=16 * rows * channels,
        limit=None,
    )(first, skip_gain.reshape(1, channels), query, key, value, implicit_filter, explicit_taps, out_grad)
    arrays = lax.all_to_all(packed, "ctx", 0, 0, tiled=True)
    if share != padded:
        arrays = jnp.pad(arrays, ((0, 0), (0, 0), (0, padded - share), (0, 0)))
    matrices, twists = tables(blocks, rows)
    height = (blocks + 1) * padded
    scratch = pltpu.VMEM((3, height, 2 * rows), f32)
    results = call(
        functools.partial(mix_kernel, grad_scale=grad_scale),
        "mix",
        shape((blocks, 4, padded, rows)),
        (pltpu.VMEM,) * 3,
        scratch=(scratch, scratch),
        flops=36 * height * (2 * rows) ** 2,
        size=24 * blocks * padded * rows,
    )(jnp.asarray(matrices), jnp.asarray(twists), arrays)
    parts = lax.all_to_all(results[:, :, :share], "ctx", 0, 0, tiled=True)
    full = shape((rows, channels))
    outs = call(
        unpack_kernel,
        "unpack",
        (full,) * 6 + (shape((1, channels)),),
        (pltpu.VMEM,) * 5,
        size=48 * rows * channels,
    )(query, key, value, out_grad, parts)
    return (*outs[:6], outs[6].reshape(channels))


def solution(mesh):
    in_specs = (
        P("ctx", "ch"),
        P("ctx", "ch"),
        P("ctx", "ch"),
        P("ctx", "ch"),
        P(None, "ch"),
        P("ch"),
        P("ctx", "ch"),
    )
    out_specs = (
        P("ctx", "ch"),
        P("ctx", "ch"),
        P("ctx", "ch"),
        P("ctx", "ch"),
        P("ctx", "ch"),
        P(None, "ch"),
        P("ch"),
    )
    return jax.shard_map(body, mesh=mesh, in_specs=in_specs, out_specs=out_specs, check_vma=False)
```

```python
import functools
import math

import jax
import jax.numpy as jnp
import numpy as np
from jax import lax
from jax.experimental import pallas as pl
from jax.experimental.pallas import tpu as pltpu
from jax.sharding import PartitionSpec as P

VMEM_LIMIT = 48 * 1024 * 1024


def turn(value, turns):
    turns = turns % 1.0
    real, imag = value
    if turns == 0.0:
        return value
    if turns == 0.5:
        return (-real, -imag)
    if turns == 0.25:
        return (-imag, real)
    if turns == 0.75:
        return (imag, -real)
    cosine, sine = math.cos(2 * math.pi * turns), math.sin(2 * math.pi * turns)
    if abs(abs(cosine) - abs(sine)) < 1e-12:
        scale = abs(cosine)
        one, two = math.copysign(1.0, cosine), math.copysign(1.0, sine)
        new_real = (real if one > 0 else -real) - (imag if two > 0 else -imag)
        new_imag = (real if two > 0 else -real) + (imag if one > 0 else -imag)
        return (new_real * scale, new_imag * scale)
    return (real * cosine - imag * sine, real * sine + imag * cosine)


def plus(a, b):
    return (a[0] + b[0], a[1] + b[1])


def minus(a, b):
    return (a[0] - b[0], a[1] - b[1])


def complex_transform(values, sign):
    count = len(values)
    if count == 1:
        return values
    even = complex_transform(values[0::2], sign)
    odd = complex_transform(values[1::2], sign)
    odd = [turn(odd[k], sign * k / count) for k in range(count // 2)]
    return [plus(e, o) for e, o in zip(even, odd)] + [minus(e, o) for e, o in zip(even, odd)]


def odd_bins(values):
    length = len(values)
    half = length // 2
    turned = [turn((values[j], -values[j + half]), -j / (2 * length)) for j in range(half)]
    bins = {}
    for m, (real, imag) in enumerate(complex_transform(turned, -1)):
        p = 4 * m + 1
        if p < length:
            bins[p] = (real, imag)
        else:
            bins[2 * length - p] = (real, -imag)
    return bins


def real_bins(values):
    length = len(values)
    if length == 2:
        return {0: (values[0] + values[1], None), 1: (values[0] - values[1], None)}
    half = length // 2
    bins = {}
    for s, value in real_bins([values[j] + values[j + half] for j in range(half)]).items():
        bins[2 * s] = value
    bins.update(odd_bins([values[j] - values[j + half] for j in range(half)]))
    return bins


def padded_bins(values):
    bins = {2 * s: value for s, value in real_bins(values).items()}
    bins.update(odd_bins(values))
    return bins


def odd_bins_back(bins, length):
    half = length // 2
    spectrum = []
    for m in range(half):
        p = 4 * m + 1
        if p < length:
            spectrum.append(bins[p])
        else:
            real, imag = bins[2 * length - p]
            spectrum.append((real, -imag))
    values = complex_transform(spectrum, 1)
    values = [turn(value, j / (2 * length)) for j, value in enumerate(values)]
    return [value[0] for value in values] + [-value[1] for value in values]


def real_bins_back(bins, length):
    if length == 2:
        return [bins[0][0] + bins[1][0], bins[0][0] - bins[1][0]]
    half = length // 2
    even = real_bins_back({s: bins[2 * s] for s in range(half // 2 + 1)}, half)
    odd = odd_bins_back(bins, half)
    return [e + o for e, o in zip(even, odd)] + [e - o for e, o in zip(even, odd)]


def padded_bins_back(bins, length):
    even = real_bins_back({s: bins[2 * s] for s in range(length // 2 + 1)}, length)
    odd = odd_bins_back(bins, length)
    return [e + o for e, o in zip(even, odd)]


def tables(blocks, rows):
    extent = 2 * blocks * rows
    positions = np.arange(rows)
    angle = 2 * np.pi * (np.outer(positions, positions) % rows) / rows
    cosine, sine = np.cos(angle), np.sin(angle)
    forward = np.block([[cosine, -sine], [sine, cosine]])
    matrices = []
    for matrix in (forward, forward.T):
        high = matrix.astype(jnp.bfloat16)
        low = (matrix - high.astype(np.float64)).astype(jnp.bfloat16)
        matrices += [high, low]
    phase = 2 * np.pi * np.outer(np.arange(blocks + 1), positions) / extent
    weight = np.where(np.arange(blocks + 1) % blocks == 0, 1.0, 2.0)[:, None] / extent
    twists = np.stack(
        [np.cos(phase), -np.sin(phase), weight * np.cos(phase), weight * np.sin(phase)], 1
    )
    return np.stack(matrices), twists.astype(np.float32)


def multiply(values, high, low):
    values_high = values.astype(jnp.bfloat16)
    values_low = (values - values_high.astype(jnp.float32)).astype(jnp.bfloat16)
    dot = functools.partial(jnp.dot, preferred_element_type=jnp.float32)
    return dot(values_high, high) + (dot(values_low, high) + dot(values_high, low))


def pack_kernel(first, skip, query, key, value, filt, taps, grad, out, *scratch):
    *held, packed, arrived, sent = scratch
    copies = [
        pltpu.make_async_copy(source, target, arrived.at[i])
        for i, (source, target) in enumerate(zip((key, value, query, grad, filt, taps), held))
    ]
    for copy in copies:
        copy.start()
    key, value, query, grad, filt, taps = held
    rows, channels = query.shape
    blocks, _, share, _ = out.shape

    sends = [pltpu.make_async_copy(packed.at[:, a], out.at[:, a], sent.at[a]) for a in range(3)]

    def put(a, array):
        packed[:, a] = array.T.reshape(blocks, share, rows)
        sends[a].start()

    copies[0].wait()
    copies[1].wait()
    put(0, key[...].astype(jnp.float32) * value[...].astype(jnp.float32))
    copies[2].wait()
    copies[3].wait()
    put(2, grad[...].astype(jnp.float32) * query[...].astype(jnp.float32))
    copies[4].wait()
    copies[5].wait()
    row = lax.broadcasted_iota(jnp.int32, (rows, channels), 0)
    extra = taps[...] + jnp.where(row == 0, skip[...], 0.0)
    put(1, filt[...] + jnp.where(first[0] == 1, extra, 0.0))
    for send in sends:
        send.wait()


def mix_kernel(matrices, twists, arrays, out, spectra, results, *, grad_scale):
    blocks, _, channels, rows = arrays.shape
    for a in range(3):
        for low in range(0, channels, 8):
            part = pl.ds(low, 8)
            bins = padded_bins([arrays[j, a, part, :] for j in range(blocks)])
            for p in range(blocks + 1):
                real, imag = bins[p]
                cosine, sine = twists[p, 0:1, :], twists[p, 1:2, :]
                place = pl.ds(p * channels + low, 8)
                if imag is None:
                    spectra[a, place, :rows] = real * cosine
                    spectra[a, place, rows:] = real * sine
                else:
                    spectra[a, place, :rows] = real * cosine - imag * sine
                    spectra[a, place, rows:] = real * sine + imag * cosine
    forward_high, forward_low = matrices[0], matrices[1]
    back_high, back_low = matrices[2], matrices[3]
    product, filt, mix_grad = [multiply(spectra[a], forward_high, forward_low) for a in range(3)]
    pr, pi = product[:, :rows], product[:, rows:]
    fr, fi = filt[:, :rows], filt[:, rows:]
    gr, gi = mix_grad[:, :rows], mix_grad[:, rows:]
    spectra[0, :, :rows] = fr * pr - fi * pi
    spectra[0, :, rows:] = fr * pi + fi * pr
    spectra[1, :, :rows] = fr * gr + fi * gi
    spectra[1, :, rows:] = fr * gi - fi * gr
    spectra[2, :, :rows] = pr * gr + pi * gi
    spectra[2, :, rows:] = pr * gi - pi * gr
    for a in range(3):
        results[a] = multiply(spectra[a], back_high, back_low)
        for low in range(0, channels, 8):
            bins = {}
            for p in range(blocks + 1):
                cosine, sine = twists[p, 2:3, :], twists[p, 3:4, :]
                place = pl.ds(p * channels + low, 8)
                real, imag = results[a, place, :rows], results[a, place, rows:]
                new_real = real * cosine - imag * sine
                if p % blocks == 0:
                    bins[p] = (new_real, None)
                else:
                    bins[p] = (new_real, real * sine + imag * cosine)
            values = padded_bins_back(bins, blocks)
            for j in range(blocks):
                value = values[j] * grad_scale if a == 2 else values[j]
                out[j, a, pl.ds(low, 8), :] = value
            if a == 2:
                for j in range(blocks):
                    out[j, 3, pl.ds(low, 8), :] = values[0] * grad_scale


def unpack_kernel(query, key, value, grad, parts, *rest):
    outs, held, sent = rest[:7], rest[7:14], rest[14]
    rows, channels = query.shape
    copies = [
        pltpu.make_async_copy(source, target, sent.at[i])
        for i, (source, target) in enumerate(zip(held, outs))
    ]

    def whole(a):
        return parts[:, a].reshape(channels, rows).T

    def put(i, array):
        held[i][...] = array
        copies[i].start()

    first_lags = whole(3)
    put(5, first_lags)
    put(6, first_lags[0:1, :])
    put(4, whole(2))
    mixer = whole(0)
    put(0, query[...].astype(jnp.float32) * mixer)
    put(1, grad[...].astype(jnp.float32) * mixer)
    product_grad = whole(1)
    put(2, product_grad * value[...].astype(jnp.float32))
    put(3, product_grad * key[...].astype(jnp.float32))
    for copy in copies:
        copy.wait()


def call(kernel, name, out_shape, places, scratch=(), flops=0, size=0, limit=VMEM_LIMIT, to=pltpu.VMEM):
    return pl.pallas_call(
        kernel,
        name=name,
        out_shape=out_shape,
        in_specs=[pl.BlockSpec(memory_space=place) for place in places],
        out_specs=jax.tree.map(lambda _: pl.BlockSpec(memory_space=to), out_shape),
        scratch_shapes=list(scratch),
        compiler_params=pltpu.CompilerParams(vmem_limit_bytes=limit),
        cost_estimate=pl.CostEstimate(flops=flops, bytes_accessed=size, transcendentals=0),
    )


def body(query, key, value, implicit_filter, explicit_taps, skip_gain, out_grad):
    rows, channels = query.shape
    blocks = lax.axis_size("ctx")
    share = channels // blocks
    padded = -(-share // 8) * 8
    f32 = jnp.float32
    shape = functools.partial(jax.ShapeDtypeStruct, dtype=f32)
    grad_scale = 1.0 / math.sqrt(blocks * rows)
    first = (lax.axis_index("ctx") == 0).astype(jnp.int32).reshape(1)

    half = pltpu.VMEM((rows, channels), jnp.bfloat16)
    full = pltpu.VMEM((rows, channels), f32)
    packed = call(
        pack_kernel,
        "pack",
        shape((blocks, 3, share, rows)),
        (pltpu.SMEM, pltpu.VMEM) + (pltpu.HBM,) * 6,
        scratch=(half,) * 4
        + (full,) * 2
        + (pltpu.VMEM((blocks, 3, share, rows), f32), pltpu.SemaphoreType.DMA((6,)), pltpu.SemaphoreType.DMA((3,))),
        size=16 * rows * channels,
        limit=None,
        to=pltpu.HBM,
    )(first, skip_gain.reshape(1, channels), query, key, value, implicit_filter, explicit_taps, out_grad)
    arrays = lax.all_to_all(packed, "ctx", 0, 0, tiled=True)
    if share != padded:
        arrays = jnp.pad(arrays, ((0, 0), (0, 0), (0, padded - share), (0, 0)))
    matrices, twists = tables(blocks, rows)
    height = (blocks + 1) * padded
    scratch = pltpu.VMEM((3, height, 2 * rows), f32)
    results = call(
        functools.partial(mix_kernel, grad_scale=grad_scale),
        "mix",
        shape((blocks, 4, padded, rows)),
        (pltpu.VMEM,) * 3,
        scratch=(scratch, scratch),
        flops=36 * height * (2 * rows) ** 2,
        size=24 * blocks * padded * rows,
    )(jnp.asarray(matrices), jnp.asarray(twists), arrays)
    parts = lax.all_to_all(results[:, :, :share], "ctx", 0, 0, tiled=True)
    full, one = shape((rows, channels)), shape((1, channels))
    outs = call(
        unpack_kernel,
        "unpack",
        (full,) * 6 + (one,),
        (pltpu.VMEM,) * 5,
        scratch=tuple(pltpu.VMEM(out.shape, f32) for out in (full,) * 6 + (one,)) + (pltpu.SemaphoreType.DMA((7,)),),
        to=pltpu.HBM,
        size=48 * rows * channels,
    )(query, key, value, out_grad, parts)
    return (*outs[:6], outs[6].reshape(channels))


def solution(mesh):
    in_specs = (
        P("ctx", "ch"),
        P("ctx", "ch"),
        P("ctx", "ch"),
        P("ctx", "ch"),
        P(None, "ch"),
        P("ch"),
        P("ctx", "ch"),
    )
    out_specs = (
        P("ctx", "ch"),
        P("ctx", "ch"),
        P("ctx", "ch"),
        P("ctx", "ch"),
        P("ctx", "ch"),
        P(None, "ch"),
        P("ch"),
    )
    return jax.shard_map(body, mesh=mesh, in_specs=in_specs, out_specs=out_specs, check_vma=False)
```

```python
import functools
import math

import jax
import jax.numpy as jnp
import numpy as np
from jax import lax
from jax.experimental import pallas as pl
from jax.experimental.pallas import tpu as pltpu
from jax.sharding import PartitionSpec as P

VMEM_LIMIT = 48 * 1024 * 1024


def turn(value, turns):
    turns = turns % 1.0
    real, imag = value
    if turns == 0.0:
        return value
    if turns == 0.5:
        return (-real, -imag)
    if turns == 0.25:
        return (-imag, real)
    if turns == 0.75:
        return (imag, -real)
    cosine, sine = math.cos(2 * math.pi * turns), math.sin(2 * math.pi * turns)
    if abs(abs(cosine) - abs(sine)) < 1e-12:
        scale = abs(cosine)
        one, two = math.copysign(1.0, cosine), math.copysign(1.0, sine)
        new_real = (real if one > 0 else -real) - (imag if two > 0 else -imag)
        new_imag = (real if two > 0 else -real) + (imag if one > 0 else -imag)
        return (new_real * scale, new_imag * scale)
    return (real * cosine - imag * sine, real * sine + imag * cosine)


def plus(a, b):
    return (a[0] + b[0], a[1] + b[1])


def minus(a, b):
    return (a[0] - b[0], a[1] - b[1])


def complex_transform(values, sign):
    count = len(values)
    if count == 1:
        return values
    even = complex_transform(values[0::2], sign)
    odd = complex_transform(values[1::2], sign)
    odd = [turn(odd[k], sign * k / count) for k in range(count // 2)]
    return [plus(e, o) for e, o in zip(even, odd)] + [minus(e, o) for e, o in zip(even, odd)]


def odd_bins(values):
    length = len(values)
    half = length // 2
    turned = [turn((values[j], -values[j + half]), -j / (2 * length)) for j in range(half)]
    bins = {}
    for m, (real, imag) in enumerate(complex_transform(turned, -1)):
        p = 4 * m + 1
        if p < length:
            bins[p] = (real, imag)
        else:
            bins[2 * length - p] = (real, -imag)
    return bins


def real_bins(values):
    length = len(values)
    if length == 2:
        return {0: (values[0] + values[1], None), 1: (values[0] - values[1], None)}
    half = length // 2
    bins = {}
    for s, value in real_bins([values[j] + values[j + half] for j in range(half)]).items():
        bins[2 * s] = value
    bins.update(odd_bins([values[j] - values[j + half] for j in range(half)]))
    return bins


def padded_bins(values):
    bins = {2 * s: value for s, value in real_bins(values).items()}
    bins.update(odd_bins(values))
    return bins


def odd_bins_back(bins, length):
    half = length // 2
    spectrum = []
    for m in range(half):
        p = 4 * m + 1
        if p < length:
            spectrum.append(bins[p])
        else:
            real, imag = bins[2 * length - p]
            spectrum.append((real, -imag))
    values = complex_transform(spectrum, 1)
    values = [turn(value, j / (2 * length)) for j, value in enumerate(values)]
    return [value[0] for value in values] + [-value[1] for value in values]


def real_bins_back(bins, length):
    if length == 2:
        return [bins[0][0] + bins[1][0], bins[0][0] - bins[1][0]]
    half = length // 2
    even = real_bins_back({s: bins[2 * s] for s in range(half // 2 + 1)}, half)
    odd = odd_bins_back(bins, half)
    return [e + o for e, o in zip(even, odd)] + [e - o for e, o in zip(even, odd)]


def padded_bins_back(bins, length):
    even = real_bins_back({s: bins[2 * s] for s in range(length // 2 + 1)}, length)
    odd = odd_bins_back(bins, length)
    return [e + o for e, o in zip(even, odd)]


def tables(blocks, rows):
    extent = 2 * blocks * rows
    positions = np.arange(rows)
    angle = 2 * np.pi * (np.outer(positions, positions) % rows) / rows
    cosine, sine = np.cos(angle), np.sin(angle)
    forward = np.block([[cosine, -sine], [sine, cosine]])
    matrices = []
    for matrix in (forward, forward.T):
        high = matrix.astype(jnp.bfloat16)
        low = (matrix - high.astype(np.float64)).astype(jnp.bfloat16)
        matrices += [high, low]
    phase = 2 * np.pi * np.outer(np.arange(blocks + 1), positions) / extent
    weight = np.where(np.arange(blocks + 1) % blocks == 0, 1.0, 2.0)[:, None] / extent
    twists = np.stack(
        [np.cos(phase), -np.sin(phase), weight * np.cos(phase), weight * np.sin(phase)], 1
    )
    return np.stack(matrices), twists.astype(np.float32)


def multiply(values, high, low):
    values_high = values.astype(jnp.bfloat16)
    values_low = (values - values_high.astype(jnp.float32)).astype(jnp.bfloat16)
    dot = functools.partial(jnp.dot, preferred_element_type=jnp.float32)
    return dot(values_high, high) + (dot(values_low, high) + dot(values_high, low))


def pack_kernel(product, filt, mix_grad, out):
    blocks, _, share, rows = out.shape
    for a, field in enumerate((product, filt, mix_grad)):
        out[:, a] = field[...].T.reshape(blocks, share, rows)


def mix_kernel(matrices, twists, arrays, out, spectra, results, *, grad_scale):
    blocks, _, channels, rows = arrays.shape
    for a in range(3):
        for low in range(0, channels, 8):
            part = pl.ds(low, 8)
            bins = padded_bins([arrays[j, a, part, :] for j in range(blocks)])
            for p in range(blocks + 1):
                real, imag = bins[p]
                cosine, sine = twists[p, 0:1, :], twists[p, 1:2, :]
                place = pl.ds(p * channels + low, 8)
                if imag is None:
                    spectra[a, place, :rows] = real * cosine
                    spectra[a, place, rows:] = real * sine
                else:
                    spectra[a, place, :rows] = real * cosine - imag * sine
                    spectra[a, place, rows:] = real * sine + imag * cosine
    forward_high, forward_low = matrices[0], matrices[1]
    back_high, back_low = matrices[2], matrices[3]
    product, filt, mix_grad = [multiply(spectra[a], forward_high, forward_low) for a in range(3)]
    pr, pi = product[:, :rows], product[:, rows:]
    fr, fi = filt[:, :rows], filt[:, rows:]
    gr, gi = mix_grad[:, :rows], mix_grad[:, rows:]
    spectra[0, :, :rows] = fr * pr - fi * pi
    spectra[0, :, rows:] = fr * pi + fi * pr
    spectra[1, :, :rows] = fr * gr + fi * gi
    spectra[1, :, rows:] = fr * gi - fi * gr
    spectra[2, :, :rows] = pr * gr + pi * gi
    spectra[2, :, rows:] = pr * gi - pi * gr
    for a in range(3):
        results[a] = multiply(spectra[a], back_high, back_low)
        for low in range(0, channels, 8):
            bins = {}
            for p in range(blocks + 1):
                cosine, sine = twists[p, 2:3, :], twists[p, 3:4, :]
                place = pl.ds(p * channels + low, 8)
                real, imag = results[a, place, :rows], results[a, place, rows:]
                new_real = real * cosine - imag * sine
                if p % blocks == 0:
                    bins[p] = (new_real, None)
                else:
                    bins[p] = (new_real, real * sine + imag * cosine)
            values = padded_bins_back(bins, blocks)
            for j in range(blocks):
                value = values[j] * grad_scale if a == 2 else values[j]
                out[j, a, pl.ds(low, 8), :] = value
            if a == 2:
                for j in range(blocks):
                    out[j, 3, pl.ds(low, 8), :] = values[0] * grad_scale


def unpack_kernel(query, key, value, grad, parts, *rest):
    outs, held, sent = rest[:7], rest[7:14], rest[14]
    rows, channels = query.shape
    copies = [
        pltpu.make_async_copy(source, target, sent.at[i])
        for i, (source, target) in enumerate(zip(held, outs))
    ]

    def whole(a):
        return parts[:, a].reshape(channels, rows).T

    def put(i, array):
        held[i][...] = array
        copies[i].start()

    first_lags = whole(3)
    put(5, first_lags)
    put(6, first_lags[0:1, :])
    put(4, whole(2))
    mixer = whole(0)
    put(0, query[...].astype(jnp.float32) * mixer)
    put(1, grad[...].astype(jnp.float32) * mixer)
    product_grad = whole(1)
    put(2, product_grad * value[...].astype(jnp.float32))
    put(3, product_grad * key[...].astype(jnp.float32))
    for copy in copies:
        copy.wait()


def call(kernel, name, out_shape, places, scratch=(), flops=0, size=0, limit=VMEM_LIMIT, to=pltpu.VMEM):
    return pl.pallas_call(
        kernel,
        name=name,
        out_shape=out_shape,
        in_specs=[pl.BlockSpec(memory_space=place) for place in places],
        out_specs=jax.tree.map(lambda _: pl.BlockSpec(memory_space=to), out_shape),
        scratch_shapes=list(scratch),
        compiler_params=pltpu.CompilerParams(vmem_limit_bytes=limit),
        cost_estimate=pl.CostEstimate(flops=flops, bytes_accessed=size, transcendentals=0),
    )


def body(query, key, value, implicit_filter, explicit_taps, skip_gain, out_grad):
    rows, channels = query.shape
    blocks = lax.axis_size("ctx")
    share = channels // blocks
    padded = -(-share // 8) * 8
    f32 = jnp.float32
    shape = functools.partial(jax.ShapeDtypeStruct, dtype=f32)
    grad_scale = 1.0 / math.sqrt(blocks * rows)
    first = lax.axis_index("ctx") == 0

    product = key.astype(f32) * value.astype(f32)
    mix_grad = out_grad.astype(f32) * query.astype(f32)
    direct = jnp.where(jnp.arange(rows)[:, None] == 0, skip_gain, 0.0)
    combined = implicit_filter + jnp.where(first, explicit_taps + direct, 0.0)
    packed = call(
        pack_kernel, "pack", shape((blocks, 3, share, rows)), (pltpu.VMEM,) * 3, size=24 * rows * channels
    )(product, combined, mix_grad)
    arrays = lax.all_to_all(packed, "ctx", 0, 0, tiled=True)
    if share != padded:
        arrays = jnp.pad(arrays, ((0, 0), (0, 0), (0, padded - share), (0, 0)))
    matrices, twists = tables(blocks, rows)
    height = (blocks + 1) * padded
    scratch = pltpu.VMEM((3, height, 2 * rows), f32)
    results = call(
        functools.partial(mix_kernel, grad_scale=grad_scale),
        "mix",
        shape((blocks, 4, padded, rows)),
        (pltpu.VMEM,) * 3,
        scratch=(scratch, scratch),
        flops=36 * height * (2 * rows) ** 2,
        size=24 * blocks * padded * rows,
    )(jnp.asarray(matrices), jnp.asarray(twists), arrays)
    parts = lax.all_to_all(results[:, :, :share], "ctx", 0, 0, tiled=True)
    full, one = shape((rows, channels)), shape((1, channels))
    outs = call(
        unpack_kernel,
        "unpack",
        (full,) * 6 + (one,),
        (pltpu.VMEM,) * 5,
        scratch=tuple(pltpu.VMEM(out.shape, f32) for out in (full,) * 6 + (one,)) + (pltpu.SemaphoreType.DMA((7,)),),
        to=pltpu.HBM,
        size=48 * rows * channels,
    )(query, key, value, out_grad, parts)
    return (*outs[:6], outs[6].reshape(channels))


def solution(mesh):
    in_specs = (
        P("ctx", "ch"),
        P("ctx", "ch"),
        P("ctx", "ch"),
        P("ctx", "ch"),
        P(None, "ch"),
        P("ch"),
        P("ctx", "ch"),
    )
    out_specs = (
        P("ctx", "ch"),
        P("ctx", "ch"),
        P("ctx", "ch"),
        P("ctx", "ch"),
        P("ctx", "ch"),
        P(None, "ch"),
        P("ch"),
    )
    return jax.shard_map(body, mesh=mesh, in_specs=in_specs, out_specs=out_specs, check_vma=False)
```

```python
import functools
import math

import jax
import jax.numpy as jnp
import numpy as np
from jax import lax
from jax.experimental import pallas as pl
from jax.experimental.pallas import tpu as pltpu
from jax.sharding import PartitionSpec as P

VMEM_LIMIT = 48 * 1024 * 1024


def turn(value, turns):
    turns = turns % 1.0
    real, imag = value
    if turns == 0.0:
        return value
    if turns == 0.5:
        return (-real, -imag)
    if turns == 0.25:
        return (-imag, real)
    if turns == 0.75:
        return (imag, -real)
    cosine, sine = math.cos(2 * math.pi * turns), math.sin(2 * math.pi * turns)
    if abs(abs(cosine) - abs(sine)) < 1e-12:
        scale = abs(cosine)
        one, two = math.copysign(1.0, cosine), math.copysign(1.0, sine)
        new_real = (real if one > 0 else -real) - (imag if two > 0 else -imag)
        new_imag = (real if two > 0 else -real) + (imag if one > 0 else -imag)
        return (new_real * scale, new_imag * scale)
    return (real * cosine - imag * sine, real * sine + imag * cosine)


def plus(a, b):
    return (a[0] + b[0], a[1] + b[1])


def minus(a, b):
    return (a[0] - b[0], a[1] - b[1])


def complex_transform(values, sign):
    count = len(values)
    if count == 1:
        return values
    even = complex_transform(values[0::2], sign)
    odd = complex_transform(values[1::2], sign)
    odd = [turn(odd[k], sign * k / count) for k in range(count // 2)]
    return [plus(e, o) for e, o in zip(even, odd)] + [minus(e, o) for e, o in zip(even, odd)]


def odd_bins(values):
    length = len(values)
    half = length // 2
    turned = [turn((values[j], -values[j + half]), -j / (2 * length)) for j in range(half)]
    bins = {}
    for m, (real, imag) in enumerate(complex_transform(turned, -1)):
        p = 4 * m + 1
        if p < length:
            bins[p] = (real, imag)
        else:
            bins[2 * length - p] = (real, -imag)
    return bins


def real_bins(values):
    length = len(values)
    if length == 2:
        return {0: (values[0] + values[1], None), 1: (values[0] - values[1], None)}
    half = length // 2
    bins = {}
    for s, value in real_bins([values[j] + values[j + half] for j in range(half)]).items():
        bins[2 * s] = value
    bins.update(odd_bins([values[j] - values[j + half] for j in range(half)]))
    return bins


def padded_bins(values):
    bins = {2 * s: value for s, value in real_bins(values).items()}
    bins.update(odd_bins(values))
    return bins


def odd_bins_back(bins, length):
    half = length // 2
    spectrum = []
    for m in range(half):
        p = 4 * m + 1
        if p < length:
            spectrum.append(bins[p])
        else:
            real, imag = bins[2 * length - p]
            spectrum.append((real, -imag))
    values = complex_transform(spectrum, 1)
    values = [turn(value, j / (2 * length)) for j, value in enumerate(values)]
    return [value[0] for value in values] + [-value[1] for value in values]


def real_bins_back(bins, length):
    if length == 2:
        return [bins[0][0] + bins[1][0], bins[0][0] - bins[1][0]]
    half = length // 2
    even = real_bins_back({s: bins[2 * s] for s in range(half // 2 + 1)}, half)
    odd = odd_bins_back(bins, half)
    return [e + o for e, o in zip(even, odd)] + [e - o for e, o in zip(even, odd)]


def padded_bins_back(bins, length):
    even = real_bins_back({s: bins[2 * s] for s in range(length // 2 + 1)}, length)
    odd = odd_bins_back(bins, length)
    return [e + o for e, o in zip(even, odd)]


def tables(blocks, rows):
    extent = 2 * blocks * rows
    positions = np.arange(rows)
    angle = 2 * np.pi * (np.outer(positions, positions) % rows) / rows
    cosine, sine = np.cos(angle), np.sin(angle)
    forward = np.block([[cosine, -sine], [sine, cosine]])
    matrices = []
    for matrix in (forward, forward.T):
        high = matrix.astype(jnp.bfloat16)
        low = (matrix - high.astype(np.float64)).astype(jnp.bfloat16)
        matrices += [high, low]
    phase = 2 * np.pi * np.outer(np.arange(blocks + 1), positions) / extent
    weight = np.where(np.arange(blocks + 1) % blocks == 0, 1.0, 2.0)[:, None] / extent
    twists = np.stack(
        [np.cos(phase), -np.sin(phase), weight * np.cos(phase), weight * np.sin(phase)], 1
    )
    return np.stack(matrices), twists.astype(np.float32)


def multiply(values, high, low):
    values_high = values.astype(jnp.bfloat16)
    values_low = (values - values_high.astype(jnp.float32)).astype(jnp.bfloat16)
    dot = functools.partial(jnp.dot, preferred_element_type=jnp.float32)
    return dot(values_high, high) + (dot(values_low, high) + dot(values_high, low))


def pack_kernel(product, query, grad, filt, out):
    blocks, _, share, rows = out.shape

    def put(a, field):
        out[:, a] = field.T.reshape(blocks, share, rows)

    put(0, product[...])
    put(2, grad[...].astype(jnp.float32) * query[...].astype(jnp.float32))
    put(1, filt[...])


def mix_kernel(taps, skip, matrices, twists, arrays, out, spectra, results, direct, *, grad_scale):
    blocks, _, channels, rows = arrays.shape
    row = lax.broadcasted_iota(jnp.int32, taps.shape, 0)
    direct[...] = (taps[...] + jnp.where(row == 0, skip[...], 0.0)).T
    own = 0 if direct.shape[0] == channels else pl.multiple_of(lax.axis_index("ctx") * channels, channels)
    for a in range(3):
        for low in range(0, channels, 8):
            part = pl.ds(low, 8)
            values = [arrays[j, a, part, :] for j in range(blocks)]
            if a == 1:
                values[0] = values[0] + direct[pl.ds(own + low, 8), :]
            bins = padded_bins(values)
            for p in range(blocks + 1):
                real, imag = bins[p]
                cosine, sine = twists[p, 0:1, :], twists[p, 1:2, :]
                place = pl.ds(p * channels + low, 8)
                if imag is None:
                    spectra[a, place, :rows] = real * cosine
                    spectra[a, place, rows:] = real * sine
                else:
                    spectra[a, place, :rows] = real * cosine - imag * sine
                    spectra[a, place, rows:] = real * sine + imag * cosine
    forward_high, forward_low = matrices[0], matrices[1]
    back_high, back_low = matrices[2], matrices[3]
    product, filt, mix_grad = [multiply(spectra[a], forward_high, forward_low) for a in range(3)]
    pr, pi = product[:, :rows], product[:, rows:]
    fr, fi = filt[:, :rows], filt[:, rows:]
    gr, gi = mix_grad[:, :rows], mix_grad[:, rows:]
    spectra[0, :, :rows] = fr * pr - fi * pi
    spectra[0, :, rows:] = fr * pi + fi * pr
    spectra[1, :, :rows] = fr * gr + fi * gi
    spectra[1, :, rows:] = fr * gi - fi * gr
    spectra[2, :, :rows] = pr * gr + pi * gi
    spectra[2, :, rows:] = pr * gi - pi * gr
    for a in range(3):
        results[a] = multiply(spectra[a], back_high, back_low)
        for low in range(0, channels, 8):
            bins = {}
            for p in range(blocks + 1):
                cosine, sine = twists[p, 2:3, :], twists[p, 3:4, :]
                place = pl.ds(p * channels + low, 8)
                real, imag = results[a, place, :rows], results[a, place, rows:]
                new_real = real * cosine - imag * sine
                if p % blocks == 0:
                    bins[p] = (new_real, None)
                else:
                    bins[p] = (new_real, real * sine + imag * cosine)
            values = padded_bins_back(bins, blocks)
            for j in range(blocks):
                value = values[j] * grad_scale if a == 2 else values[j]
                out[j, a, pl.ds(low, 8), :] = value
            if a == 2:
                for j in range(blocks):
                    out[j, 3, pl.ds(low, 8), :] = values[0] * grad_scale


def unpack_kernel(query, key, value, grad, parts, *rest):
    outs, held, sent = rest[:7], rest[7:14], rest[14]
    rows, channels = query.shape
    copies = [
        pltpu.make_async_copy(source, target, sent.at[i])
        for i, (source, target) in enumerate(zip(held, outs))
    ]

    def whole(a):
        return parts[:, a].reshape(channels, rows).T

    def put(i, array):
        held[i][...] = array
        copies[i].start()

    first_lags = whole(3)
    put(5, first_lags)
    put(6, first_lags[0:1, :])
    put(4, whole(2))
    mixer = whole(0)
    put(0, query[...].astype(jnp.float32) * mixer)
    put(1, grad[...].astype(jnp.float32) * mixer)
    product_grad = whole(1)
    put(2, product_grad * value[...].astype(jnp.float32))
    put(3, product_grad * key[...].astype(jnp.float32))
    for copy in copies:
        copy.wait()


def call(kernel, name, out_shape, places, scratch=(), flops=0, size=0, limit=VMEM_LIMIT, to=pltpu.VMEM):
    return pl.pallas_call(
        kernel,
        name=name,
        out_shape=out_shape,
        in_specs=[pl.BlockSpec(memory_space=place) for place in places],
        out_specs=jax.tree.map(lambda _: pl.BlockSpec(memory_space=to), out_shape),
        scratch_shapes=list(scratch),
        compiler_params=pltpu.CompilerParams(vmem_limit_bytes=limit),
        cost_estimate=pl.CostEstimate(flops=flops, bytes_accessed=size, transcendentals=0),
    )


def body(query, key, value, implicit_filter, explicit_taps, skip_gain, out_grad):
    rows, channels = query.shape
    blocks = lax.axis_size("ctx")
    share = channels // blocks
    padded = -(-share // 8) * 8
    f32 = jnp.float32
    shape = functools.partial(jax.ShapeDtypeStruct, dtype=f32)
    grad_scale = 1.0 / math.sqrt(blocks * rows)
    taps, skip = explicit_taps, skip_gain.reshape(1, channels)

    product = key.astype(f32) * value.astype(f32)
    packed = call(
        pack_kernel, "pack", shape((blocks, 3, share, rows)), (pltpu.VMEM,) * 4, size=24 * rows * channels
    )(product, query, out_grad, implicit_filter)
    arrays = lax.all_to_all(packed, "ctx", 0, 0, tiled=True)
    if share != padded:
        arrays = jnp.pad(arrays, ((0, 0), (0, 0), (0, padded - share), (0, 0)))
        own = lax.axis_index("ctx") * share
        taps, skip = [
            jnp.pad(lax.dynamic_slice_in_dim(each, own, share, 1), ((0, 0), (0, padded - share)))
            for each in (taps, skip)
        ]
    matrices, twists = tables(blocks, rows)
    height = (blocks + 1) * padded
    scratch = pltpu.VMEM((3, height, 2 * rows), f32)
    results = call(
        functools.partial(mix_kernel, grad_scale=grad_scale),
        "mix",
        shape((blocks, 4, padded, rows)),
        (pltpu.VMEM,) * 5,
        scratch=(scratch, scratch, pltpu.VMEM(taps.shape[::-1], f32)),
        flops=36 * height * (2 * rows) ** 2,
        size=24 * blocks * padded * rows,
    )(taps, skip, jnp.asarray(matrices), jnp.asarray(twists), arrays)
    parts = lax.all_to_all(results[:, :, :share], "ctx", 0, 0, tiled=True)
    full, one = shape((rows, channels)), shape((1, channels))
    outs = call(
        unpack_kernel,
        "unpack",
        (full,) * 6 + (one,),
        (pltpu.VMEM,) * 5,
        scratch=tuple(pltpu.VMEM(out.shape, f32) for out in (full,) * 6 + (one,)) + (pltpu.SemaphoreType.DMA((7,)),),
        to=pltpu.HBM,
        size=48 * rows * channels,
    )(query, key, value, out_grad, parts)
    return (*outs[:6], outs[6].reshape(channels))


def solution(mesh):
    in_specs = (
        P("ctx", "ch"),
        P("ctx", "ch"),
        P("ctx", "ch"),
        P("ctx", "ch"),
        P(None, "ch"),
        P("ch"),
        P("ctx", "ch"),
    )
    out_specs = (
        P("ctx", "ch"),
        P("ctx", "ch"),
        P("ctx", "ch"),
        P("ctx", "ch"),
        P("ctx", "ch"),
        P(None, "ch"),
        P("ch"),
    )
    return jax.shard_map(body, mesh=mesh, in_specs=in_specs, out_specs=out_specs, check_vma=False)
```

```python
import functools
import math

import jax
import jax.numpy as jnp
import numpy as np
from jax import lax
from jax.experimental import pallas as pl
from jax.experimental.pallas import tpu as pltpu
from jax.sharding import PartitionSpec as P

VMEM_LIMIT = 48 * 1024 * 1024
RELAY_WEIGHT = 10**11


def turn(value, turns):
    turns = turns % 1.0
    real, imag = value
    if turns == 0.0:
        return value
    if turns == 0.5:
        return (-real, -imag)
    if turns == 0.25:
        return (-imag, real)
    if turns == 0.75:
        return (imag, -real)
    cosine, sine = math.cos(2 * math.pi * turns), math.sin(2 * math.pi * turns)
    if abs(abs(cosine) - abs(sine)) < 1e-12:
        scale = abs(cosine)
        one, two = math.copysign(1.0, cosine), math.copysign(1.0, sine)
        new_real = (real if one > 0 else -real) - (imag if two > 0 else -imag)
        new_imag = (real if two > 0 else -real) + (imag if one > 0 else -imag)
        return (new_real * scale, new_imag * scale)
    return (real * cosine - imag * sine, real * sine + imag * cosine)


def plus(a, b):
    return (a[0] + b[0], a[1] + b[1])


def minus(a, b):
    return (a[0] - b[0], a[1] - b[1])


def complex_transform(values, sign):
    count = len(values)
    if count == 1:
        return values
    even = complex_transform(values[0::2], sign)
    odd = complex_transform(values[1::2], sign)
    odd = [turn(odd[k], sign * k / count) for k in range(count // 2)]
    return [plus(e, o) for e, o in zip(even, odd)] + [minus(e, o) for e, o in zip(even, odd)]


def odd_bins(values):
    length = len(values)
    half = length // 2
    turned = [turn((values[j], -values[j + half]), -j / (2 * length)) for j in range(half)]
    bins = {}
    for m, (real, imag) in enumerate(complex_transform(turned, -1)):
        p = 4 * m + 1
        if p < length:
            bins[p] = (real, imag)
        else:
            bins[2 * length - p] = (real, -imag)
    return bins


def real_bins(values):
    length = len(values)
    if length == 2:
        return {0: (values[0] + values[1], None), 1: (values[0] - values[1], None)}
    half = length // 2
    bins = {}
    for s, value in real_bins([values[j] + values[j + half] for j in range(half)]).items():
        bins[2 * s] = value
    bins.update(odd_bins([values[j] - values[j + half] for j in range(half)]))
    return bins


def padded_bins(values):
    bins = {2 * s: value for s, value in real_bins(values).items()}
    bins.update(odd_bins(values))
    return bins


def odd_bins_back(bins, length):
    half = length // 2
    spectrum = []
    for m in range(half):
        p = 4 * m + 1
        if p < length:
            spectrum.append(bins[p])
        else:
            real, imag = bins[2 * length - p]
            spectrum.append((real, -imag))
    values = complex_transform(spectrum, 1)
    values = [turn(value, j / (2 * length)) for j, value in enumerate(values)]
    return [value[0] for value in values] + [-value[1] for value in values]


def real_bins_back(bins, length):
    if length == 2:
        return [bins[0][0] + bins[1][0], bins[0][0] - bins[1][0]]
    half = length // 2
    even = real_bins_back({s: bins[2 * s] for s in range(half // 2 + 1)}, half)
    odd = odd_bins_back(bins, half)
    return [e + o for e, o in zip(even, odd)] + [e - o for e, o in zip(even, odd)]


def padded_bins_back(bins, length):
    even = real_bins_back({s: bins[2 * s] for s in range(length // 2 + 1)}, length)
    odd = odd_bins_back(bins, length)
    return [e + o for e, o in zip(even, odd)]


def tables(blocks, rows):
    extent = 2 * blocks * rows
    positions = np.arange(rows)
    angle = 2 * np.pi * (np.outer(positions, positions) % rows) / rows
    cosine, sine = np.cos(angle), np.sin(angle)
    forward = np.block([[cosine, -sine], [sine, cosine]])
    matrices = []
    for matrix in (forward, forward.T):
        high = matrix.astype(jnp.bfloat16)
        low = (matrix - high.astype(np.float64)).astype(jnp.bfloat16)
        matrices += [high, low]
    phase = 2 * np.pi * np.outer(np.arange(blocks + 1), positions) / extent
    weight = np.where(np.arange(blocks + 1) % blocks == 0, 1.0, 2.0)[:, None] / extent
    twists = np.stack(
        [np.cos(phase), -np.sin(phase), weight * np.cos(phase), weight * np.sin(phase)], 1
    )
    return np.stack(matrices), twists.astype(np.float32)


def multiply(values, high, low):
    values_high = values.astype(jnp.bfloat16)
    values_low = (values - values_high.astype(jnp.float32)).astype(jnp.bfloat16)
    dot = functools.partial(jnp.dot, preferred_element_type=jnp.float32)
    return dot(values_high, high) + (dot(values_low, high) + dot(values_high, low))


def pack_kernel(product, grad, filt, out):
    blocks, _, share, rows = out.shape

    def put(a, field):
        out[:, a] = field.T.reshape(blocks, share, rows)

    put(0, product[...])
    put(2, grad[...])
    put(1, filt[...])


def spectra_kernel(taps, skip, matrices, twists, arrays, products, *rest, near_count, grad_scale):
    *lag_outs, spectra, results, direct, lags = rest
    blocks, _, channels, rows = arrays.shape
    row = lax.broadcasted_iota(jnp.int32, taps.shape, 0)
    direct[...] = (taps[...] + jnp.where(row == 0, skip[...], 0.0)).T
    own = 0 if direct.shape[0] == channels else pl.multiple_of(lax.axis_index("ctx") * channels, channels)
    for a in range(3):
        for low in range(0, channels, 8):
            part = pl.ds(low, 8)
            values = [arrays[j, a, part, :] for j in range(blocks)]
            if a == 1:
                values[0] = values[0] + direct[pl.ds(own + low, 8), :]
            bins = padded_bins(values)
            for p in range(blocks + 1):
                real, imag = bins[p]
                cosine, sine = twists[p, 0:1, :], twists[p, 1:2, :]
                place = pl.ds(p * channels + low, 8)
                if imag is None:
                    spectra[a, place, :rows] = real * cosine
                    spectra[a, place, rows:] = real * sine
                else:
                    spectra[a, place, :rows] = real * cosine - imag * sine
                    spectra[a, place, rows:] = real * sine + imag * cosine
    product, filt, mix_grad = [multiply(spectra[a], matrices[0], matrices[1]) for a in range(3)]
    pr, pi = product[:, :rows], product[:, rows:]
    fr, fi = filt[:, :rows], filt[:, rows:]
    gr, gi = mix_grad[:, :rows], mix_grad[:, rows:]
    spectra[0, :, :rows] = pr * gr + pi * gi
    spectra[0, :, rows:] = pr * gi - pi * gr
    products[0, :, :rows] = fr * pr - fi * pi
    products[0, :, rows:] = fr * pi + fi * pr
    products[1, :, :rows] = fr * gr + fi * gi
    products[1, :, rows:] = fr * gi - fi * gr
    for low, values in blocks_back(spectra.at[0], results, matrices, twists, channels):
        for j, value in enumerate(values):
            lags[j, pl.ds(low, 8), :] = value * grad_scale
    me = lax.axis_index("ctx") if near_count > 1 else 0
    for far, lag_out in enumerate(lag_outs):
        for near in range(near_count):
            lag_out[near] = lags[me ^ (far * near_count + near)]
        lag_out[near_count] = lags[0]


def blocks_back(spectrum, result, matrices, twists, channels):
    blocks, rows = twists.shape[0] - 1, twists.shape[2]
    result[...] = multiply(spectrum[...], matrices[2], matrices[3])
    for low in range(0, channels, 8):
        bins = {}
        for p in range(blocks + 1):
            cosine, sine = twists[p, 2:3, :], twists[p, 3:4, :]
            place = pl.ds(p * channels + low, 8)
            real, imag = result[place, :rows], result[place, rows:]
            new_real = real * cosine - imag * sine
            bins[p] = (new_real, None if p % blocks == 0 else real * sine + imag * cosine)
        yield low, padded_bins_back(bins, blocks)


def mix_kernel(matrices, twists, products, out, results):
    for a in range(2):
        for low, values in blocks_back(products.at[a], results.at[a], matrices, twists, out.shape[2]):
            for j, value in enumerate(values):
                out[j, a, pl.ds(low, 8), :] = value


def relay_kernel(*refs):
    near_count = refs[0].shape[0] - 1
    far_count = len(refs) - near_count + 1
    parts, outs = refs[:far_count], refs[far_count:]
    for near, out in enumerate(outs, 1):
        for far, part in enumerate(parts):
            out[far] = part[near]
            out[far_count + far] = part[near_count]


def unpack_kernel(query, key, value, grad, parts, *rest, far_count, near_count):
    far_parts, rest = rest[:far_count], rest[far_count:]
    near_parts, rest = rest[: near_count - 1], rest[near_count - 1 :]
    outs, held, sent, lags, first_lags = rest[:7], rest[7:14], rest[14], rest[15], rest[16]
    rows, channels = query.shape
    copies = [
        pltpu.make_async_copy(source, target, sent.at[i])
        for i, (source, target) in enumerate(zip(held, outs))
    ]

    def whole(array):
        return array.reshape(channels, rows).T

    def put(i, array):
        held[i][...] = array
        copies[i].start()

    mixer = whole(parts[:, 0])
    put(0, query[...].astype(jnp.float32) * mixer)
    put(1, grad[...].astype(jnp.float32) * mixer)
    product_grad = whole(parts[:, 1])
    put(2, product_grad * value[...].astype(jnp.float32))
    put(3, product_grad * key[...].astype(jnp.float32))
    me = lax.axis_index("ctx") if near_count > 1 else 0
    for far, part in enumerate(far_parts):
        source = me ^ (far * near_count)
        lags[source] = part[0]
        first_lags[source] = part[near_count]
    for near, part in enumerate(near_parts, 1):
        for far in range(far_count):
            source = me ^ (far * near_count + near)
            lags[source] = part[far]
            first_lags[source] = part[far_count + far]
    put(4, whole(lags[...]))
    first = whole(first_lags[...])
    put(5, first)
    put(6, first[0:1, :])
    for copy in copies:
        copy.wait()


def call(kernel, name, out_shape, places, scratch=(), flops=0, size=0, limit=VMEM_LIMIT, to=pltpu.VMEM):
    return pl.pallas_call(
        kernel,
        name=name,
        out_shape=out_shape,
        in_specs=[pl.BlockSpec(memory_space=place) for place in places],
        out_specs=jax.tree.map(lambda _: pl.BlockSpec(memory_space=to), out_shape),
        scratch_shapes=list(scratch),
        compiler_params=pltpu.CompilerParams(vmem_limit_bytes=limit),
        cost_estimate=pl.CostEstimate(flops=flops, bytes_accessed=size, transcendentals=0),
    )


def exchange(value, axis, distance):
    return lax.ppermute(value, axis, [(i, i ^ distance) for i in range(lax.axis_size(axis))])


def send_lags(lag_parts, axis, near_count):
    far_parts = list(lag_parts)
    for far in range(len(far_parts) - 1, 0, -1):
        far_parts[far] = exchange(lag_parts[far], axis, far * near_count)
    payload = jax.ShapeDtypeStruct((2 * len(far_parts), *lag_parts[0].shape[1:]), jnp.float32)
    relay = call(
        relay_kernel, "relay", (payload,) * (near_count - 1), (pltpu.VMEM,) * len(far_parts), flops=RELAY_WEIGHT
    )
    near_parts = relay(*far_parts)
    return far_parts, [exchange(part, axis, near) for near, part in enumerate(near_parts, 1)]


def body(query, key, value, implicit_filter, explicit_taps, skip_gain, out_grad):
    rows, channels = query.shape
    blocks = lax.axis_size("ctx")
    share = channels // blocks
    padded = -(-share // 8) * 8
    f32 = jnp.float32
    shape = functools.partial(jax.ShapeDtypeStruct, dtype=f32)
    grad_scale = 1.0 / math.sqrt(blocks * rows)
    taps, skip = explicit_taps, skip_gain.reshape(1, channels)

    product = key.astype(f32) * value.astype(f32)
    mix_grad = out_grad.astype(f32) * query.astype(f32)
    packed = call(
        pack_kernel, "pack", shape((blocks, 3, share, rows)), (pltpu.VMEM,) * 3, size=24 * rows * channels
    )(product, mix_grad, implicit_filter)
    arrays = lax.all_to_all(packed, "ctx", 0, 0, tiled=True)
    if share != padded:
        arrays = jnp.pad(arrays, ((0, 0), (0, 0), (0, padded - share), (0, 0)))
        own = lax.axis_index("ctx") * share
        taps, skip = [
            jnp.pad(lax.dynamic_slice_in_dim(each, own, share, 1), ((0, 0), (0, padded - share)))
            for each in (taps, skip)
        ]
    matrices, twists = tables(blocks, rows)
    height = (blocks + 1) * padded
    near_count = 1 << (blocks.bit_length() - 1) // 2 if share == padded else 1
    far_count = blocks // near_count
    matrices, twists = jnp.asarray(matrices), jnp.asarray(twists)
    products, *lag_parts = call(
        functools.partial(spectra_kernel, near_count=near_count, grad_scale=grad_scale),
        "spectra",
        (shape((2, height, 2 * rows)),) + (shape((near_count + 1, padded, rows)),) * far_count,
        (pltpu.VMEM,) * 5,
        scratch=(
            pltpu.VMEM((3, height, 2 * rows), f32),
            pltpu.VMEM((height, 2 * rows), f32),
            pltpu.VMEM(taps.shape[::-1], f32),
            pltpu.VMEM((blocks, padded, rows), f32),
        ),
        flops=24 * height * (2 * rows) ** 2,
        size=24 * blocks * padded * rows,
    )(taps, skip, matrices, twists, arrays)
    if near_count > 1:
        far_parts, near_parts = send_lags(lag_parts, "ctx", near_count)
    results = call(
        mix_kernel,
        "mix",
        shape((blocks, 2, padded, rows)),
        (pltpu.VMEM,) * 3,
        scratch=(pltpu.VMEM((2, height, 2 * rows), f32),),
        flops=12 * height * (2 * rows) ** 2,
        size=24 * blocks * padded * rows,
    )(matrices, twists, products)
    if near_count > 1:
        parts = lax.all_to_all(results, "ctx", 0, 0, tiled=True)
    else:
        together = jnp.concatenate([results, jnp.stack(lag_parts)], axis=1)[:, :, :share]
        together = lax.all_to_all(together, "ctx", 0, 0, tiled=True)
        parts, far_parts, near_parts = together[:, :2], list(together[:, 2:]), []
    full, one = shape((rows, channels)), shape((1, channels))
    lags = pltpu.VMEM((blocks, share, rows), f32)
    outs = call(
        functools.partial(unpack_kernel, far_count=far_count, near_count=near_count),
        "unpack",
        (full,) * 6 + (one,),
        (pltpu.VMEM,) * (4 + far_count + near_count),
        scratch=tuple(pltpu.VMEM(out.shape, f32) for out in (full,) * 6 + (one,))
        + (pltpu.SemaphoreType.DMA((7,)), lags, lags),
        to=pltpu.HBM,
        size=48 * rows * channels,
    )(query, key, value, out_grad, parts, *far_parts, *near_parts)
    return (*outs[:6], outs[6].reshape(channels))


def solution(mesh):
    in_specs = (
        P("ctx", "ch"),
        P("ctx", "ch"),
        P("ctx", "ch"),
        P("ctx", "ch"),
        P(None, "ch"),
        P("ch"),
        P("ctx", "ch"),
    )
    out_specs = (
        P("ctx", "ch"),
        P("ctx", "ch"),
        P("ctx", "ch"),
        P("ctx", "ch"),
        P("ctx", "ch"),
        P(None, "ch"),
        P("ch"),
    )
    return jax.shard_map(body, mesh=mesh, in_specs=in_specs, out_specs=out_specs, check_vma=False)
```

```python
import functools
import math

import jax
import jax.numpy as jnp
import numpy as np
from jax import lax
from jax.experimental import pallas as pl
from jax.experimental.pallas import tpu as pltpu
from jax.sharding import PartitionSpec as P

VMEM_LIMIT = 48 * 1024 * 1024
RELAY_WEIGHT = 10**11


def turn(value, turns):
    turns = turns % 1.0
    real, imag = value
    if turns == 0.0:
        return value
    if turns == 0.5:
        return (-real, -imag)
    if turns == 0.25:
        return (-imag, real)
    if turns == 0.75:
        return (imag, -real)
    cosine, sine = math.cos(2 * math.pi * turns), math.sin(2 * math.pi * turns)
    if abs(abs(cosine) - abs(sine)) < 1e-12:
        scale = abs(cosine)
        one, two = math.copysign(1.0, cosine), math.copysign(1.0, sine)
        new_real = (real if one > 0 else -real) - (imag if two > 0 else -imag)
        new_imag = (real if two > 0 else -real) + (imag if one > 0 else -imag)
        return (new_real * scale, new_imag * scale)
    return (real * cosine - imag * sine, real * sine + imag * cosine)


def plus(a, b):
    return (a[0] + b[0], a[1] + b[1])


def minus(a, b):
    return (a[0] - b[0], a[1] - b[1])


def complex_transform(values, sign):
    count = len(values)
    if count == 1:
        return values
    even = complex_transform(values[0::2], sign)
    odd = complex_transform(values[1::2], sign)
    odd = [turn(odd[k], sign * k / count) for k in range(count // 2)]
    return [plus(e, o) for e, o in zip(even, odd)] + [minus(e, o) for e, o in zip(even, odd)]


def odd_bins(values):
    length = len(values)
    half = length // 2
    turned = [turn((values[j], -values[j + half]), -j / (2 * length)) for j in range(half)]
    bins = {}
    for m, (real, imag) in enumerate(complex_transform(turned, -1)):
        p = 4 * m + 1
        if p < length:
            bins[p] = (real, imag)
        else:
            bins[2 * length - p] = (real, -imag)
    return bins


def real_bins(values):
    length = len(values)
    if length == 2:
        return {0: (values[0] + values[1], None), 1: (values[0] - values[1], None)}
    half = length // 2
    bins = {}
    for s, value in real_bins([values[j] + values[j + half] for j in range(half)]).items():
        bins[2 * s] = value
    bins.update(odd_bins([values[j] - values[j + half] for j in range(half)]))
    return bins


def padded_bins(values):
    bins = {2 * s: value for s, value in real_bins(values).items()}
    bins.update(odd_bins(values))
    return bins


def odd_bins_back(bins, length):
    half = length // 2
    spectrum = []
    for m in range(half):
        p = 4 * m + 1
        if p < length:
            spectrum.append(bins[p])
        else:
            real, imag = bins[2 * length - p]
            spectrum.append((real, -imag))
    values = complex_transform(spectrum, 1)
    values = [turn(value, j / (2 * length)) for j, value in enumerate(values)]
    return [value[0] for value in values] + [-value[1] for value in values]


def real_bins_back(bins, length):
    if length == 2:
        return [bins[0][0] + bins[1][0], bins[0][0] - bins[1][0]]
    half = length // 2
    even = real_bins_back({s: bins[2 * s] for s in range(half // 2 + 1)}, half)
    odd = odd_bins_back(bins, half)
    return [e + o for e, o in zip(even, odd)] + [e - o for e, o in zip(even, odd)]


def padded_bins_back(bins, length):
    even = real_bins_back({s: bins[2 * s] for s in range(length // 2 + 1)}, length)
    odd = odd_bins_back(bins, length)
    return [e + o for e, o in zip(even, odd)]


def tables(blocks, rows):
    extent = 2 * blocks * rows
    positions = np.arange(rows)
    angle = 2 * np.pi * (np.outer(positions, positions) % rows) / rows
    cosine, sine = np.cos(angle), np.sin(angle)
    forward = np.block([[cosine, -sine], [sine, cosine]])
    matrices = []
    for matrix in (forward, forward.T):
        high = matrix.astype(jnp.bfloat16)
        low = (matrix - high.astype(np.float64)).astype(jnp.bfloat16)
        matrices += [high, low]
    phase = 2 * np.pi * np.outer(np.arange(blocks + 1), positions) / extent
    weight = np.where(np.arange(blocks + 1) % blocks == 0, 1.0, 2.0)[:, None] / extent
    twists = np.stack(
        [np.cos(phase), -np.sin(phase), weight * np.cos(phase), weight * np.sin(phase)], 1
    )
    return np.stack(matrices), twists.astype(np.float32)


def multiply(values, high, low):
    values_high = values.astype(jnp.bfloat16)
    values_low = (values - values_high.astype(jnp.float32)).astype(jnp.bfloat16)
    dot = functools.partial(jnp.dot, preferred_element_type=jnp.float32)
    return dot(values_high, high) + (dot(values_low, high) + dot(values_high, low))


def pack_kernel(product, mix_grad, out):
    blocks, _, share, rows = out.shape
    for a, field in enumerate((product, mix_grad)):
        out[:, a] = field[...].T.reshape(blocks, share, rows)


def split_kernel(field, *rest, near_count):
    outs, turned = rest[:-1], rest[-1]
    share = outs[0].shape[1]
    turned[...] = field[...].T
    me = lax.axis_index("ctx") if near_count > 1 else 0
    for far, out in enumerate(outs):
        for near in range(near_count):
            start = (me ^ (far * near_count + near)) * share
            out[near] = turned[pl.ds(start if near_count == 1 else pl.multiple_of(start, share), share), :]


def spectra_kernel(taps, skip, matrices, twists, arrays, *rest, near_count, grad_scale):
    blocks, _, channels, rows = arrays.shape
    far_count = blocks // near_count
    far_parts, rest = rest[:far_count], rest[far_count:]
    near_parts, rest = rest[: near_count - 1], rest[near_count - 1 :]
    products, *lag_outs, spectra, results, direct, lags, filter_blocks = rest
    me = lax.axis_index("ctx") if near_count > 1 else 0
    for far, part in enumerate(far_parts):
        filter_blocks[me ^ (far * near_count)] = part[0]
        for near, near_part in enumerate(near_parts, 1):
            filter_blocks[me ^ (far * near_count + near)] = near_part[far]
    row = lax.broadcasted_iota(jnp.int32, taps.shape, 0)
    direct[...] = (taps[...] + jnp.where(row == 0, skip[...], 0.0)).T
    own = 0 if direct.shape[0] == channels else pl.multiple_of(lax.axis_index("ctx") * channels, channels)
    for a in range(3):
        for low in range(0, channels, 8):
            part = pl.ds(low, 8)
            if a == 1:
                values = [filter_blocks[j, part, :] for j in range(blocks)]
                values[0] = values[0] + direct[pl.ds(own + low, 8), :]
            else:
                values = [arrays[j, a // 2, part, :] for j in range(blocks)]
            bins = padded_bins(values)
            for p in range(blocks + 1):
                real, imag = bins[p]
                cosine, sine = twists[p, 0:1, :], twists[p, 1:2, :]
                place = pl.ds(p * channels + low, 8)
                if imag is None:
                    spectra[a, place, :rows] = real * cosine
                    spectra[a, place, rows:] = real * sine
                else:
                    spectra[a, place, :rows] = real * cosine - imag * sine
                    spectra[a, place, rows:] = real * sine + imag * cosine
    product, filt, mix_grad = [multiply(spectra[a], matrices[0], matrices[1]) for a in range(3)]
    pr, pi = product[:, :rows], product[:, rows:]
    fr, fi = filt[:, :rows], filt[:, rows:]
    gr, gi = mix_grad[:, :rows], mix_grad[:, rows:]
    spectra[0, :, :rows] = pr * gr + pi * gi
    spectra[0, :, rows:] = pr * gi - pi * gr
    products[0, :, :rows] = fr * pr - fi * pi
    products[0, :, rows:] = fr * pi + fi * pr
    products[1, :, :rows] = fr * gr + fi * gi
    products[1, :, rows:] = fr * gi - fi * gr
    for low, values in blocks_back(spectra.at[0], results, matrices, twists, channels):
        for j, value in enumerate(values):
            lags[j, pl.ds(low, 8), :] = value * grad_scale
    for far, lag_out in enumerate(lag_outs):
        for near in range(near_count):
            lag_out[near] = lags[me ^ (far * near_count + near)]
        lag_out[near_count] = lags[0]


def blocks_back(spectrum, result, matrices, twists, channels):
    blocks, rows = twists.shape[0] - 1, twists.shape[2]
    result[...] = multiply(spectrum[...], matrices[2], matrices[3])
    for low in range(0, channels, 8):
        bins = {}
        for p in range(blocks + 1):
            cosine, sine = twists[p, 2:3, :], twists[p, 3:4, :]
            place = pl.ds(p * channels + low, 8)
            real, imag = result[place, :rows], result[place, rows:]
            new_real = real * cosine - imag * sine
            bins[p] = (new_real, None if p % blocks == 0 else real * sine + imag * cosine)
        yield low, padded_bins_back(bins, blocks)


def mix_kernel(matrices, twists, products, out, results):
    for a in range(2):
        for low, values in blocks_back(products.at[a], results.at[a], matrices, twists, out.shape[2]):
            for j, value in enumerate(values):
                out[j, a, pl.ds(low, 8), :] = value


def relay_kernel(*refs, far_count):
    parts = (refs[0], *refs[1:far_count][::-1])
    outs = refs[far_count:]
    near_count = len(outs) + 1
    for near, out in enumerate(outs, 1):
        for far, part in enumerate(parts):
            out[far] = part[near]
            if part.shape[0] > near_count:
                out[far_count + far] = part[near_count]


def unpack_kernel(query, key, value, grad, parts, *rest, far_count, near_count):
    far_parts, rest = rest[:far_count], rest[far_count:]
    near_parts, rest = rest[: near_count - 1], rest[near_count - 1 :]
    outs, held, sent, lags, first_lags = rest[:7], rest[7:14], rest[14], rest[15], rest[16]
    rows, channels = query.shape
    copies = [
        pltpu.make_async_copy(source, target, sent.at[i])
        for i, (source, target) in enumerate(zip(held, outs))
    ]

    def whole(array):
        return array.reshape(channels, rows).T

    def put(i, array):
        held[i][...] = array
        copies[i].start()

    mixer = whole(parts[:, 0])
    put(0, query[...].astype(jnp.float32) * mixer)
    put(1, grad[...].astype(jnp.float32) * mixer)
    product_grad = whole(parts[:, 1])
    put(2, product_grad * value[...].astype(jnp.float32))
    put(3, product_grad * key[...].astype(jnp.float32))
    me = lax.axis_index("ctx") if near_count > 1 else 0
    for far, part in enumerate(far_parts):
        source = me ^ (far * near_count)
        lags[source] = part[0]
        first_lags[source] = part[near_count]
    for near, part in enumerate(near_parts, 1):
        for far in range(far_count):
            source = me ^ (far * near_count + near)
            lags[source] = part[far]
            first_lags[source] = part[far_count + far]
    put(4, whole(lags[...]))
    first = whole(first_lags[...])
    put(5, first)
    put(6, first[0:1, :])
    for copy in copies:
        copy.wait()


def call(kernel, name, out_shape, places, scratch=(), flops=0, size=0, limit=VMEM_LIMIT, to=pltpu.VMEM):
    return pl.pallas_call(
        kernel,
        name=name,
        out_shape=out_shape,
        in_specs=[pl.BlockSpec(memory_space=place) for place in places],
        out_specs=jax.tree.map(lambda _: pl.BlockSpec(memory_space=to), out_shape),
        scratch_shapes=list(scratch),
        compiler_params=pltpu.CompilerParams(vmem_limit_bytes=limit),
        cost_estimate=pl.CostEstimate(flops=flops, bytes_accessed=size, transcendentals=0),
    )


def exchange(value, axis, distance):
    return lax.ppermute(value, axis, [(i, i ^ distance) for i in range(lax.axis_size(axis))])


def send_parts(parts, axis, near_count):
    far_parts, far_count = list(parts), len(parts)
    for far in range(far_count - 1, 0, -1):
        far_parts[far] = exchange(parts[far], axis, far * near_count)
    depth = far_count * (1 + parts[0].shape[0] - near_count)
    payload = jax.ShapeDtypeStruct((depth, *parts[0].shape[1:]), jnp.float32)
    relay = call(
        functools.partial(relay_kernel, far_count=far_count),
        "relay",
        (payload,) * (near_count - 1),
        (pltpu.VMEM,) * far_count,
        flops=RELAY_WEIGHT,
    )
    near_parts = relay(far_parts[0], *far_parts[:0:-1])
    return far_parts, [exchange(part, axis, near) for near, part in enumerate(near_parts, 1)]


def body(query, key, value, implicit_filter, explicit_taps, skip_gain, out_grad):
    rows, channels = query.shape
    blocks = lax.axis_size("ctx")
    share = channels // blocks
    padded = -(-share // 8) * 8
    f32 = jnp.float32
    shape = functools.partial(jax.ShapeDtypeStruct, dtype=f32)
    grad_scale = 1.0 / math.sqrt(blocks * rows)
    taps, skip = explicit_taps, skip_gain.reshape(1, channels)

    near_count = 1 << (blocks.bit_length() - 1) // 2 if share == padded else 1
    far_count = blocks // near_count
    product = key.astype(f32) * value.astype(f32)
    mix_grad = out_grad.astype(f32) * query.astype(f32)
    filter_parts = call(
        functools.partial(split_kernel, near_count=near_count),
        "split",
        (shape((near_count, share, rows)),) * far_count,
        (pltpu.VMEM,),
        scratch=(pltpu.VMEM((channels, rows), f32),),
        size=8 * rows * channels,
    )(implicit_filter)
    packed = call(
        pack_kernel, "pack", shape((blocks, 2, share, rows)), (pltpu.VMEM,) * 2, size=16 * rows * channels
    )(product, mix_grad)
    if near_count > 1:
        filter_far, filter_near = send_parts(filter_parts, "ctx", near_count)
        arrays = lax.all_to_all(packed, "ctx", 0, 0, tiled=True)
    else:
        arrays = lax.all_to_all(jnp.concatenate([packed, jnp.stack(filter_parts)], axis=1), "ctx", 0, 0, tiled=True)
        arrays = jnp.pad(arrays, ((0, 0), (0, 0), (0, padded - share), (0, 0)))
        arrays, filter_far, filter_near = arrays[:, :2], list(arrays[:, 2:]), []
        own = lax.axis_index("ctx") * share
        taps, skip = [
            jnp.pad(lax.dynamic_slice_in_dim(each, own, share, 1), ((0, 0), (0, padded - share)))
            for each in (taps, skip)
        ]
    matrices, twists = tables(blocks, rows)
    height = (blocks + 1) * padded
    matrices, twists = jnp.asarray(matrices), jnp.asarray(twists)
    products, *lag_parts = call(
        functools.partial(spectra_kernel, near_count=near_count, grad_scale=grad_scale),
        "spectra",
        (shape((2, height, 2 * rows)),) + (shape((near_count + 1, padded, rows)),) * far_count,
        (pltpu.VMEM,) * (4 + far_count + near_count),
        scratch=(
            pltpu.VMEM((3, height, 2 * rows), f32),
            pltpu.VMEM((height, 2 * rows), f32),
            pltpu.VMEM(taps.shape[::-1], f32),
            pltpu.VMEM((blocks, padded, rows), f32),
            pltpu.VMEM((blocks, padded, rows), f32),
        ),
        flops=24 * height * (2 * rows) ** 2,
        size=24 * blocks * padded * rows,
    )(taps, skip, matrices, twists, arrays, *filter_far, *filter_near)
    if near_count > 1:
        far_parts, near_parts = send_parts(lag_parts, "ctx", near_count)
    results = call(
        mix_kernel,
        "mix",
        shape((blocks, 2, padded, rows)),
        (pltpu.VMEM,) * 3,
        scratch=(pltpu.VMEM((2, height, 2 * rows), f32),),
        flops=12 * height * (2 * rows) ** 2,
        size=24 * blocks * padded * rows,
    )(matrices, twists, products)
    if near_count > 1:
        parts = lax.all_to_all(results, "ctx", 0, 0, tiled=True)
    else:
        together = jnp.concatenate([results, jnp.stack(lag_parts)], axis=1)[:, :, :share]
        together = lax.all_to_all(together, "ctx", 0, 0, tiled=True)
        parts, far_parts, near_parts = together[:, :2], list(together[:, 2:]), []
    full, one = shape((rows, channels)), shape((1, channels))
    lags = pltpu.VMEM((blocks, share, rows), f32)
    outs = call(
        functools.partial(unpack_kernel, far_count=far_count, near_count=near_count),
        "unpack",
        (full,) * 6 + (one,),
        (pltpu.VMEM,) * (4 + far_count + near_count),
        scratch=tuple(pltpu.VMEM(out.shape, f32) for out in (full,) * 6 + (one,))
        + (pltpu.SemaphoreType.DMA((7,)), lags, lags),
        to=pltpu.HBM,
        size=48 * rows * channels,
    )(query, key, value, out_grad, parts, *far_parts, *near_parts)
    return (*outs[:6], outs[6].reshape(channels))


def solution(mesh):
    in_specs = (
        P("ctx", "ch"),
        P("ctx", "ch"),
        P("ctx", "ch"),
        P("ctx", "ch"),
        P(None, "ch"),
        P("ch"),
        P("ctx", "ch"),
    )
    out_specs = (
        P("ctx", "ch"),
        P("ctx", "ch"),
        P("ctx", "ch"),
        P("ctx", "ch"),
        P("ctx", "ch"),
        P(None, "ch"),
        P("ch"),
    )
    return jax.shard_map(body, mesh=mesh, in_specs=in_specs, out_specs=out_specs, check_vma=False)
```

```python
import functools
import math

import jax
import jax.numpy as jnp
import numpy as np
from jax import lax
from jax.experimental import pallas as pl
from jax.experimental.pallas import tpu as pltpu
from jax.sharding import PartitionSpec as P

VMEM_LIMIT = 48 * 1024 * 1024
RELAY_WEIGHT = 10**11


def turn(value, turns):
    turns = turns % 1.0
    real, imag = value
    if turns == 0.0:
        return value
    if turns == 0.5:
        return (-real, -imag)
    if turns == 0.25:
        return (-imag, real)
    if turns == 0.75:
        return (imag, -real)
    cosine, sine = math.cos(2 * math.pi * turns), math.sin(2 * math.pi * turns)
    if abs(abs(cosine) - abs(sine)) < 1e-12:
        scale = abs(cosine)
        one, two = math.copysign(1.0, cosine), math.copysign(1.0, sine)
        new_real = (real if one > 0 else -real) - (imag if two > 0 else -imag)
        new_imag = (real if two > 0 else -real) + (imag if one > 0 else -imag)
        return (new_real * scale, new_imag * scale)
    return (real * cosine - imag * sine, real * sine + imag * cosine)


def plus(a, b):
    return (a[0] + b[0], a[1] + b[1])


def minus(a, b):
    return (a[0] - b[0], a[1] - b[1])


def complex_transform(values, sign):
    count = len(values)
    if count == 1:
        return values
    even = complex_transform(values[0::2], sign)
    odd = complex_transform(values[1::2], sign)
    odd = [turn(odd[k], sign * k / count) for k in range(count // 2)]
    return [plus(e, o) for e, o in zip(even, odd)] + [minus(e, o) for e, o in zip(even, odd)]


def odd_bins(values):
    length = len(values)
    half = length // 2
    turned = [turn((values[j], -values[j + half]), -j / (2 * length)) for j in range(half)]
    bins = {}
    for m, (real, imag) in enumerate(complex_transform(turned, -1)):
        p = 4 * m + 1
        if p < length:
            bins[p] = (real, imag)
        else:
            bins[2 * length - p] = (real, -imag)
    return bins


def real_bins(values):
    length = len(values)
    if length == 2:
        return {0: (values[0] + values[1], None), 1: (values[0] - values[1], None)}
    half = length // 2
    bins = {}
    for s, value in real_bins([values[j] + values[j + half] for j in range(half)]).items():
        bins[2 * s] = value
    bins.update(odd_bins([values[j] - values[j + half] for j in range(half)]))
    return bins


def padded_bins(values):
    bins = {2 * s: value for s, value in real_bins(values).items()}
    bins.update(odd_bins(values))
    return bins


def odd_bins_back(bins, length):
    half = length // 2
    spectrum = []
    for m in range(half):
        p = 4 * m + 1
        if p < length:
            spectrum.append(bins[p])
        else:
            real, imag = bins[2 * length - p]
            spectrum.append((real, -imag))
    values = complex_transform(spectrum, 1)
    values = [turn(value, j / (2 * length)) for j, value in enumerate(values)]
    return [value[0] for value in values] + [-value[1] for value in values]


def real_bins_back(bins, length):
    if length == 2:
        return [bins[0][0] + bins[1][0], bins[0][0] - bins[1][0]]
    half = length // 2
    even = real_bins_back({s: bins[2 * s] for s in range(half // 2 + 1)}, half)
    odd = odd_bins_back(bins, half)
    return [e + o for e, o in zip(even, odd)] + [e - o for e, o in zip(even, odd)]


def padded_bins_back(bins, length):
    even = real_bins_back({s: bins[2 * s] for s in range(length // 2 + 1)}, length)
    odd = odd_bins_back(bins, length)
    return [e + o for e, o in zip(even, odd)]


def tables(blocks, rows):
    extent = 2 * blocks * rows
    positions = np.arange(rows)
    angle = 2 * np.pi * (np.outer(positions, positions) % rows) / rows
    cosine, sine = np.cos(angle), np.sin(angle)
    forward = np.block([[cosine, -sine], [sine, cosine]])
    matrices = []
    for matrix in (forward, forward.T):
        high = matrix.astype(jnp.bfloat16)
        low = (matrix - high.astype(np.float64)).astype(jnp.bfloat16)
        matrices += [high, low]
    phase = 2 * np.pi * np.outer(np.arange(blocks + 1), positions) / extent
    weight = np.where(np.arange(blocks + 1) % blocks == 0, 1.0, 2.0)[:, None] / extent
    twists = np.stack(
        [np.cos(phase), -np.sin(phase), weight * np.cos(phase), weight * np.sin(phase)], 1
    )
    return np.stack(matrices), twists.astype(np.float32)


def multiply(values, high, low):
    values_high = values.astype(jnp.bfloat16)
    values_low = (values - values_high.astype(jnp.float32)).astype(jnp.bfloat16)
    dot = functools.partial(jnp.dot, preferred_element_type=jnp.float32)
    return dot(values_high, high) + (dot(values_low, high) + dot(values_high, low))


def pack_kernel(field, out):
    blocks, share, rows = out.shape
    out[...] = field[...].T.reshape(blocks, share, rows)


def chunk(sizes, count, field, at):
    return pl.ds(count * sum(sizes[:field]) + at * sizes[field], sizes[field])


def split_kernel(*refs, near_count):
    fields, outs, turned = refs[:2], refs[2:-1], refs[-1]
    share = outs[0].shape[0] // (2 * near_count)
    me = lax.axis_index("ctx") if near_count > 1 else 0
    for k, field in enumerate(fields):
        turned[...] = field[...].T
        for far, out in enumerate(outs):
            for near in range(near_count):
                start = (me ^ (far * near_count + near)) * share
                start = start if near_count == 1 else pl.multiple_of(start, share)
                out[chunk((share, share), near_count, k, near), :] = turned[pl.ds(start, share), :]


def gather_blocks(outs, sizes, far_parts, near_parts, me):
    far_count, near_count = len(far_parts), len(near_parts) + 1
    for far, part in enumerate(far_parts):
        for near in range(near_count):
            source = me ^ (far * near_count + near)
            for k, size in enumerate(sizes):
                if near:
                    rows = near_parts[near - 1][chunk(sizes, far_count, k, far), :]
                else:
                    rows = part[chunk(sizes, near_count, k, 0), :]
                outs[k][source, :size, :] = rows
            if len(outs) > len(sizes):
                extra = outs[len(sizes)].shape[1]
                if near:
                    rows = near_parts[near - 1][pl.ds(far_count * sum(sizes) + far * extra, extra), :]
                else:
                    rows = part[pl.ds(near_count * sum(sizes), extra), :]
                outs[len(sizes)][source] = rows


def spectra_kernel(taps, skip, matrices, twists, mix_grads, *rest, near_count, early, grad_scale):
    blocks, channels, rows = mix_grads.shape
    far_count = blocks // near_count
    far_parts, rest = rest[:far_count], rest[far_count:]
    near_parts, rest = rest[: near_count - 1], rest[near_count - 1 :]
    products, *outs, spectra, results, direct, lags, back, filters, gates = rest
    me = lax.axis_index("ctx") if near_count > 1 else 0
    gather_blocks((filters, gates), (channels, channels), far_parts, near_parts, me)
    row = lax.broadcasted_iota(jnp.int32, taps.shape, 0)
    direct[...] = (taps[...] + jnp.where(row == 0, skip[...], 0.0)).T
    own = 0 if direct.shape[0] == channels else pl.multiple_of(lax.axis_index("ctx") * channels, channels)
    for a in range(3):
        for low in range(0, channels, 8):
            part = pl.ds(low, 8)
            values = [(gates, filters, mix_grads)[a][j, part, :] for j in range(blocks)]
            if a == 1:
                values[0] = values[0] + direct[pl.ds(own + low, 8), :]
            bins = padded_bins(values)
            for p in range(blocks + 1):
                real, imag = bins[p]
                cosine, sine = twists[p, 0:1, :], twists[p, 1:2, :]
                place = pl.ds(p * channels + low, 8)
                if imag is None:
                    spectra[a, place, :rows] = real * cosine
                    spectra[a, place, rows:] = real * sine
                else:
                    spectra[a, place, :rows] = real * cosine - imag * sine
                    spectra[a, place, rows:] = real * sine + imag * cosine
    product, filt, mix_grad = [multiply(spectra[a], matrices[0], matrices[1]) for a in range(3)]
    pr, pi = product[:, :rows], product[:, rows:]
    fr, fi = filt[:, :rows], filt[:, rows:]
    gr, gi = mix_grad[:, :rows], mix_grad[:, rows:]
    spectra[0, :, :rows] = pr * gr + pi * gi
    spectra[0, :, rows:] = pr * gi - pi * gr
    products[0, :, :rows] = fr * pr - fi * pi
    products[0, :, rows:] = fr * pi + fi * pr
    products[1, :, :rows] = fr * gr + fi * gi
    products[1, :, rows:] = fr * gi - fi * gr
    for low, values in blocks_back(spectra.at[0], results, matrices, twists, channels, 0, channels):
        for j, value in enumerate(values):
            lags[j, pl.ds(low, 8), :] = value * grad_scale
    for low, values in blocks_back(products.at[1], results, matrices, twists, channels, 0, early):
        for j, value in enumerate(values):
            back[j, pl.ds(low, 8), :] = value
    sizes = (channels, early) if early else (channels,)
    for far, out in enumerate(outs):
        for near in range(near_count):
            target = me ^ (far * near_count + near)
            for k, size in enumerate(sizes):
                out[chunk(sizes, near_count, k, near), :] = (lags, back)[k][target]
        out[pl.ds(near_count * sum(sizes), channels), :] = lags[0]


def blocks_back(spectrum, result, matrices, twists, channels, first, last):
    blocks, rows = twists.shape[0] - 1, twists.shape[2]
    count = last - first
    if count == 0:
        return
    height = (blocks + 1) * count
    wanted = spectrum[...].reshape(blocks + 1, channels, 2 * rows)[:, first:last].reshape(height, 2 * rows)
    result[:height, :] = multiply(wanted, matrices[2], matrices[3])
    for low in range(0, count, 8):
        bins = {}
        for p in range(blocks + 1):
            cosine, sine = twists[p, 2:3, :], twists[p, 3:4, :]
            place = pl.ds(p * count + low, 8)
            real, imag = result[place, :rows], result[place, rows:]
            new_real = real * cosine - imag * sine
            bins[p] = (new_real, None if p % blocks == 0 else real * sine + imag * cosine)
        yield low, padded_bins_back(bins, blocks)


def mix_kernel(matrices, twists, products, out, results, *, channels, early):
    for a, first in enumerate((0, early)):
        for low, values in blocks_back(products.at[a], results.at[a], matrices, twists, channels, first, channels):
            for j, value in enumerate(values):
                out[j, pl.ds(a * channels + low, 8), :] = value


def relay_kernel(*refs, far_count, sizes, extra):
    parts = (refs[0], *refs[1:far_count][::-1])
    outs = refs[far_count:]
    near_count = len(outs) + 1
    for near, out in enumerate(outs, 1):
        for far, part in enumerate(parts):
            for k in range(len(sizes)):
                out[chunk(sizes, far_count, k, far), :] = part[chunk(sizes, near_count, k, near), :]
            if extra:
                place = pl.ds(far_count * sum(sizes) + far * extra, extra)
                out[place, :] = part[pl.ds(near_count * sum(sizes), extra), :]


def unpack_kernel(query, key, value, grad, parts, *rest, far_count, near_count, early):
    far_parts, rest = rest[:far_count], rest[far_count:]
    near_parts, rest = rest[: near_count - 1], rest[near_count - 1 :]
    outs, held, sent, lags, back, first_lags = rest[:7], rest[7:14], rest[14], rest[15], rest[16], rest[17]
    rows, channels = query.shape
    blocks, share, _ = lags.shape
    copies = [
        pltpu.make_async_copy(source, target, sent.at[i])
        for i, (source, target) in enumerate(zip(held, outs))
    ]

    def whole(array):
        return array.reshape(channels, rows).T

    def put(i, array):
        held[i][...] = array
        copies[i].start()

    mixer = whole(parts[:, :share])
    put(0, query[...].astype(jnp.float32) * mixer)
    put(1, grad[...].astype(jnp.float32) * mixer)
    me = lax.axis_index("ctx") if near_count > 1 else 0
    if early:
        gather_blocks((lags, back, first_lags), (share, early), far_parts, near_parts, me)
    else:
        gather_blocks((lags, first_lags), (share,), far_parts, near_parts, me)
    back[:, early:, :] = parts[:, share:]
    product_grad = whole(back[...])
    put(2, product_grad * value[...].astype(jnp.float32))
    put(3, product_grad * key[...].astype(jnp.float32))
    put(4, whole(lags[...]))
    first = whole(first_lags[...])
    put(5, first)
    put(6, first[0:1, :])
    for copy in copies:
        copy.wait()


def call(kernel, name, out_shape, places, scratch=(), flops=0, size=0, limit=VMEM_LIMIT, to=pltpu.VMEM):
    return pl.pallas_call(
        kernel,
        name=name,
        out_shape=out_shape,
        in_specs=[pl.BlockSpec(memory_space=place) for place in places],
        out_specs=jax.tree.map(lambda _: pl.BlockSpec(memory_space=to), out_shape),
        scratch_shapes=list(scratch),
        compiler_params=pltpu.CompilerParams(vmem_limit_bytes=limit),
        cost_estimate=pl.CostEstimate(flops=flops, bytes_accessed=size, transcendentals=0),
    )


def exchange(value, axis, distance):
    return lax.ppermute(value, axis, [(i, i ^ distance) for i in range(lax.axis_size(axis))])


def send_parts(parts, axis, near_count, sizes, extra=0):
    far_parts, far_count = list(parts), len(parts)
    for far in range(far_count - 1, 0, -1):
        far_parts[far] = exchange(parts[far], axis, far * near_count)
    payload = jax.ShapeDtypeStruct((far_count * (sum(sizes) + extra), parts[0].shape[1]), jnp.float32)
    relay = call(
        functools.partial(relay_kernel, far_count=far_count, sizes=sizes, extra=extra),
        "relay",
        (payload,) * (near_count - 1),
        (pltpu.VMEM,) * far_count,
        flops=RELAY_WEIGHT,
    )
    near_parts = relay(far_parts[0], *far_parts[:0:-1])
    return far_parts, [exchange(part, axis, near) for near, part in enumerate(near_parts, 1)]


def body(query, key, value, implicit_filter, explicit_taps, skip_gain, out_grad):
    rows, channels = query.shape
    blocks = lax.axis_size("ctx")
    share = channels // blocks
    padded = -(-share // 8) * 8
    f32 = jnp.float32
    shape = functools.partial(jax.ShapeDtypeStruct, dtype=f32)
    grad_scale = 1.0 / math.sqrt(blocks * rows)
    taps, skip = explicit_taps, skip_gain.reshape(1, channels)

    near_count = 1 << (blocks.bit_length() - 1) // 2 if share == padded else 1
    far_count = blocks // near_count
    product = key.astype(f32) * value.astype(f32)
    mix_grad = out_grad.astype(f32) * query.astype(f32)
    split_parts = call(
        functools.partial(split_kernel, near_count=near_count),
        "split",
        (shape((2 * near_count * share, rows)),) * far_count,
        (pltpu.VMEM,) * 2,
        scratch=(pltpu.VMEM((channels, rows), f32),),
        size=16 * rows * channels,
    )(implicit_filter, product)
    packed = call(pack_kernel, "pack", shape((blocks, share, rows)), (pltpu.VMEM,), size=8 * rows * channels)(mix_grad)
    if near_count > 1:
        far_parts, near_parts = send_parts(split_parts, "ctx", near_count, (share, share))
        mix_grads = lax.all_to_all(packed, "ctx", 0, 0, tiled=True)
    else:
        together = jnp.concatenate([packed, jnp.stack(split_parts)], axis=1)
        together = lax.all_to_all(together, "ctx", 0, 0, tiled=True).reshape(blocks, 3, share, rows)
        together = jnp.pad(together, ((0, 0), (0, 0), (0, padded - share), (0, 0)))
        mix_grads, near_parts = together[:, 0], []
        far_parts = list(together[:, 1:].reshape(blocks, 2 * padded, rows))
        own = lax.axis_index("ctx") * share
        taps, skip = [
            jnp.pad(lax.dynamic_slice_in_dim(each, own, share, 1), ((0, 0), (0, padded - share)))
            for each in (taps, skip)
        ]
    matrices, twists = tables(blocks, rows)
    height = (blocks + 1) * padded
    matrices, twists = jnp.asarray(matrices), jnp.asarray(twists)
    early = padded // 16 * 8 if near_count > 1 else 0
    block = pltpu.VMEM((blocks, padded, rows), f32)
    products, *split_parts = call(
        functools.partial(spectra_kernel, near_count=near_count, early=early, grad_scale=grad_scale),
        "spectra",
        (shape((2, height, 2 * rows)),) + (shape((near_count * (padded + early) + padded, rows)),) * far_count,
        (pltpu.VMEM,) * (4 + far_count + near_count),
        scratch=(
            pltpu.VMEM((3, height, 2 * rows), f32),
            pltpu.VMEM((height, 2 * rows), f32),
            pltpu.VMEM(taps.shape[::-1], f32),
            block,
            pltpu.VMEM((blocks, max(early, 8), rows), f32),
            block,
            block,
        ),
        flops=27 * height * (2 * rows) ** 2,
        size=24 * blocks * padded * rows,
    )(taps, skip, matrices, twists, mix_grads, *far_parts, *near_parts)
    if near_count > 1:
        sizes = (share, early) if early else (share,)
        far_parts, near_parts = send_parts(split_parts, "ctx", near_count, sizes, share)
    results = call(
        functools.partial(mix_kernel, channels=padded, early=early),
        "mix",
        shape((blocks, 2 * padded - early, rows)),
        (pltpu.VMEM,) * 3,
        scratch=(pltpu.VMEM((2, height, 2 * rows), f32),),
        flops=9 * height * (2 * rows) ** 2,
        size=24 * blocks * padded * rows,
    )(matrices, twists, products)
    if near_count > 1:
        parts = lax.all_to_all(results, "ctx", 0, 0, tiled=True)
    else:
        together = jnp.concatenate([results, jnp.stack(split_parts)], axis=1).reshape(blocks, 4, padded, rows)
        together = lax.all_to_all(together[:, :, :share], "ctx", 0, 0, tiled=True).reshape(blocks, 4 * share, rows)
        parts, far_parts, near_parts = together[:, : 2 * share], list(together[:, 2 * share :]), []
    full, one = shape((rows, channels)), shape((1, channels))
    block = pltpu.VMEM((blocks, share, rows), f32)
    outs = call(
        functools.partial(unpack_kernel, far_count=far_count, near_count=near_count, early=early),
        "unpack",
        (full,) * 6 + (one,),
        (pltpu.VMEM,) * (4 + far_count + near_count),
        scratch=tuple(pltpu.VMEM(out.shape, f32) for out in (full,) * 6 + (one,))
        + (pltpu.SemaphoreType.DMA((7,)), block, block, block),
        to=pltpu.HBM,
        size=48 * rows * channels,
    )(query, key, value, out_grad, parts, *far_parts, *near_parts)
    return (*outs[:6], outs[6].reshape(channels))


def solution(mesh):
    in_specs = (
        P("ctx", "ch"),
        P("ctx", "ch"),
        P("ctx", "ch"),
        P("ctx", "ch"),
        P(None, "ch"),
        P("ch"),
        P("ctx", "ch"),
    )
    out_specs = (
        P("ctx", "ch"),
        P("ctx", "ch"),
        P("ctx", "ch"),
        P("ctx", "ch"),
        P("ctx", "ch"),
        P(None, "ch"),
        P("ch"),
    )
    return jax.shard_map(body, mesh=mesh, in_specs=in_specs, out_specs=out_specs, check_vma=False)
```

```python
import functools
import math

import jax
import jax.numpy as jnp
import numpy as np
from jax import lax
from jax.experimental import pallas as pl
from jax.experimental.pallas import tpu as pltpu
from jax.sharding import PartitionSpec as P

VMEM_LIMIT = 48 * 1024 * 1024
RELAY_WEIGHT = 10**11


def turn(value, turns):
    turns = turns % 1.0
    real, imag = value
    if turns == 0.0:
        return value
    if turns == 0.5:
        return (-real, -imag)
    if turns == 0.25:
        return (-imag, real)
    if turns == 0.75:
        return (imag, -real)
    cosine, sine = math.cos(2 * math.pi * turns), math.sin(2 * math.pi * turns)
    if abs(abs(cosine) - abs(sine)) < 1e-12:
        scale = abs(cosine)
        one, two = math.copysign(1.0, cosine), math.copysign(1.0, sine)
        new_real = (real if one > 0 else -real) - (imag if two > 0 else -imag)
        new_imag = (real if two > 0 else -real) + (imag if one > 0 else -imag)
        return (new_real * scale, new_imag * scale)
    return (real * cosine - imag * sine, real * sine + imag * cosine)


def plus(a, b):
    return (a[0] + b[0], a[1] + b[1])


def minus(a, b):
    return (a[0] - b[0], a[1] - b[1])


def complex_transform(values, sign):
    count = len(values)
    if count == 1:
        return values
    even = complex_transform(values[0::2], sign)
    odd = complex_transform(values[1::2], sign)
    odd = [turn(odd[k], sign * k / count) for k in range(count // 2)]
    return [plus(e, o) for e, o in zip(even, odd)] + [minus(e, o) for e, o in zip(even, odd)]


def odd_bins(values):
    length = len(values)
    half = length // 2
    turned = [turn((values[j], -values[j + half]), -j / (2 * length)) for j in range(half)]
    bins = {}
    for m, (real, imag) in enumerate(complex_transform(turned, -1)):
        p = 4 * m + 1
        if p < length:
            bins[p] = (real, imag)
        else:
            bins[2 * length - p] = (real, -imag)
    return bins


def real_bins(values):
    length = len(values)
    if length == 2:
        return {0: (values[0] + values[1], None), 1: (values[0] - values[1], None)}
    half = length // 2
    bins = {}
    for s, value in real_bins([values[j] + values[j + half] for j in range(half)]).items():
        bins[2 * s] = value
    bins.update(odd_bins([values[j] - values[j + half] for j in range(half)]))
    return bins


def padded_bins(values):
    bins = {2 * s: value for s, value in real_bins(values).items()}
    bins.update(odd_bins(values))
    return bins


def odd_bins_back(bins, length):
    half = length // 2
    spectrum = []
    for m in range(half):
        p = 4 * m + 1
        if p < length:
            spectrum.append(bins[p])
        else:
            real, imag = bins[2 * length - p]
            spectrum.append((real, -imag))
    values = complex_transform(spectrum, 1)
    values = [turn(value, j / (2 * length)) for j, value in enumerate(values)]
    return [value[0] for value in values] + [-value[1] for value in values]


def real_bins_back(bins, length):
    if length == 2:
        return [bins[0][0] + bins[1][0], bins[0][0] - bins[1][0]]
    half = length // 2
    even = real_bins_back({s: bins[2 * s] for s in range(half // 2 + 1)}, half)
    odd = odd_bins_back(bins, half)
    return [e + o for e, o in zip(even, odd)] + [e - o for e, o in zip(even, odd)]


def padded_bins_back(bins, length):
    even = real_bins_back({s: bins[2 * s] for s in range(length // 2 + 1)}, length)
    odd = odd_bins_back(bins, length)
    return [e + o for e, o in zip(even, odd)]


def tables(blocks, rows):
    extent = 2 * blocks * rows
    positions = np.arange(rows)
    angle = 2 * np.pi * (np.outer(positions, positions) % rows) / rows
    cosine, sine = np.cos(angle), np.sin(angle)
    forward = np.block([[cosine, -sine], [sine, cosine]])
    matrices = []
    for matrix in (forward, forward.T):
        high = matrix.astype(jnp.bfloat16)
        low = (matrix - high.astype(np.float64)).astype(jnp.bfloat16)
        matrices += [high, low]
    phase = 2 * np.pi * np.outer(np.arange(blocks + 1), positions) / extent
    weight = np.where(np.arange(blocks + 1) % blocks == 0, 1.0, 2.0)[:, None] / extent
    twists = np.stack(
        [np.cos(phase), -np.sin(phase), weight * np.cos(phase), weight * np.sin(phase)], 1
    )
    return np.stack(matrices), twists.astype(np.float32)


def multiply(values, high, low):
    values_high = values.astype(jnp.bfloat16)
    values_low = (values - values_high.astype(jnp.float32)).astype(jnp.bfloat16)
    dot = functools.partial(jnp.dot, preferred_element_type=jnp.float32)
    return dot(values_high, high) + (dot(values_low, high) + dot(values_high, low))


def pack_kernel(product, mix_grad, out):
    blocks, _, share, rows = out.shape
    for a, field in enumerate((product, mix_grad)):
        out[:, a] = field[...].T.reshape(blocks, share, rows)


def chunk(sizes, count, field, at):
    return pl.ds(count * sum(sizes[:field]) + at * sizes[field], sizes[field])


def split_kernel(field, *rest, near_count):
    outs, turned = rest[:-1], rest[-1]
    share = outs[0].shape[0] // near_count
    turned[...] = field[...].T
    me = lax.axis_index("ctx") if near_count > 1 else 0
    for far, out in enumerate(outs):
        for near in range(near_count):
            start = (me ^ (far * near_count + near)) * share
            start = start if near_count == 1 else pl.multiple_of(start, share)
            out[chunk((share,), near_count, 0, near), :] = turned[pl.ds(start, share), :]


def gather_blocks(outs, sizes, far_parts, near_parts, me):
    far_count, near_count = len(far_parts), len(near_parts) + 1
    for far, part in enumerate(far_parts):
        for near in range(near_count):
            source = me ^ (far * near_count + near)
            for k, size in enumerate(sizes):
                if near:
                    rows = near_parts[near - 1][chunk(sizes, far_count, k, far), :]
                else:
                    rows = part[chunk(sizes, near_count, k, 0), :]
                outs[k][source, :size, :] = rows
            if len(outs) > len(sizes):
                extra = outs[len(sizes)].shape[1]
                if near:
                    rows = near_parts[near - 1][pl.ds(far_count * sum(sizes) + far * extra, extra), :]
                else:
                    rows = part[pl.ds(near_count * sum(sizes), extra), :]
                outs[len(sizes)][source] = rows


def spectra_kernel(taps, skip, matrices, twists, gates, *rest, near_count, early, grad_scale):
    blocks, _, channels, rows = gates.shape
    far_count = blocks // near_count
    far_parts, rest = rest[:far_count], rest[far_count:]
    near_parts, rest = rest[: near_count - 1], rest[near_count - 1 :]
    products, *outs, spectra, results, direct, lags, back, filters = rest
    me = lax.axis_index("ctx") if near_count > 1 else 0
    gather_blocks((filters,), (channels,), far_parts, near_parts, me)
    row = lax.broadcasted_iota(jnp.int32, taps.shape, 0)
    direct[...] = (taps[...] + jnp.where(row == 0, skip[...], 0.0)).T
    own = 0 if direct.shape[0] == channels else pl.multiple_of(lax.axis_index("ctx") * channels, channels)
    for a in range(3):
        for low in range(0, channels, 8):
            part = pl.ds(low, 8)
            if a == 1:
                values = [filters[j, part, :] for j in range(blocks)]
                values[0] = values[0] + direct[pl.ds(own + low, 8), :]
            else:
                values = [gates[j, a // 2, part, :] for j in range(blocks)]
            bins = padded_bins(values)
            for p in range(blocks + 1):
                real, imag = bins[p]
                cosine, sine = twists[p, 0:1, :], twists[p, 1:2, :]
                place = pl.ds(p * channels + low, 8)
                if imag is None:
                    spectra[a, place, :rows] = real * cosine
                    spectra[a, place, rows:] = real * sine
                else:
                    spectra[a, place, :rows] = real * cosine - imag * sine
                    spectra[a, place, rows:] = real * sine + imag * cosine
    product, filt, mix_grad = [multiply(spectra[a], matrices[0], matrices[1]) for a in range(3)]
    pr, pi = product[:, :rows], product[:, rows:]
    fr, fi = filt[:, :rows], filt[:, rows:]
    gr, gi = mix_grad[:, :rows], mix_grad[:, rows:]
    spectra[0, :, :rows] = pr * gr + pi * gi
    spectra[0, :, rows:] = pr * gi - pi * gr
    products[0, :, :rows] = fr * pr - fi * pi
    products[0, :, rows:] = fr * pi + fi * pr
    products[1, :, :rows] = fr * gr + fi * gi
    products[1, :, rows:] = fr * gi - fi * gr
    for low, values in blocks_back(spectra.at[0], results, matrices, twists, channels, 0, channels):
        for j, value in enumerate(values):
            lags[j, pl.ds(low, 8), :] = value * grad_scale
    for low, values in blocks_back(products.at[1], results, matrices, twists, channels, 0, early):
        for j, value in enumerate(values):
            back[j, pl.ds(low, 8), :] = value
    sizes = (channels, early) if early else (channels,)
    for far, out in enumerate(outs):
        for near in range(near_count):
            target = me ^ (far * near_count + near)
            for k, size in enumerate(sizes):
                out[chunk(sizes, near_count, k, near), :] = (lags, back)[k][target]
        out[pl.ds(near_count * sum(sizes), channels), :] = lags[0]


def blocks_back(spectrum, result, matrices, twists, channels, first, last):
    blocks, rows = twists.shape[0] - 1, twists.shape[2]
    count = last - first
    if count == 0:
        return
    height = (blocks + 1) * count
    wanted = spectrum[...].reshape(blocks + 1, channels, 2 * rows)[:, first:last].reshape(height, 2 * rows)
    result[:height, :] = multiply(wanted, matrices[2], matrices[3])
    for low in range(0, count, 8):
        bins = {}
        for p in range(blocks + 1):
            cosine, sine = twists[p, 2:3, :], twists[p, 3:4, :]
            place = pl.ds(p * count + low, 8)
            real, imag = result[place, :rows], result[place, rows:]
            new_real = real * cosine - imag * sine
            bins[p] = (new_real, None if p % blocks == 0 else real * sine + imag * cosine)
        yield low, padded_bins_back(bins, blocks)


def mix_kernel(matrices, twists, products, out, results, *, channels, early):
    for a, first in enumerate((0, early)):
        for low, values in blocks_back(products.at[a], results.at[a], matrices, twists, channels, first, channels):
            for j, value in enumerate(values):
                out[j, pl.ds(a * channels + low, 8), :] = value


def relay_kernel(*refs, far_count, sizes, extra):
    parts = (refs[0], *refs[1:far_count][::-1])
    outs = refs[far_count:]
    near_count = len(outs) + 1
    for near, out in enumerate(outs, 1):
        for far, part in enumerate(parts):
            for k in range(len(sizes)):
                out[chunk(sizes, far_count, k, far), :] = part[chunk(sizes, near_count, k, near), :]
            if extra:
                place = pl.ds(far_count * sum(sizes) + far * extra, extra)
                out[place, :] = part[pl.ds(near_count * sum(sizes), extra), :]


def unpack_kernel(query, key, value, grad, parts, *rest, far_count, near_count, early):
    far_parts, rest = rest[:far_count], rest[far_count:]
    near_parts, rest = rest[: near_count - 1], rest[near_count - 1 :]
    outs, held, sent, lags, back, first_lags = rest[:7], rest[7:14], rest[14], rest[15], rest[16], rest[17]
    rows, channels = query.shape
    blocks, share, _ = lags.shape
    copies = [
        pltpu.make_async_copy(source, target, sent.at[i])
        for i, (source, target) in enumerate(zip(held, outs))
    ]

    def whole(array):
        return array.reshape(channels, rows).T

    def put(i, array):
        held[i][...] = array
        copies[i].start()

    mixer = whole(parts[:, :share])
    put(0, query[...].astype(jnp.float32) * mixer)
    put(1, grad[...].astype(jnp.float32) * mixer)
    me = lax.axis_index("ctx") if near_count > 1 else 0
    if early:
        gather_blocks((lags, back, first_lags), (share, early), far_parts, near_parts, me)
    else:
        gather_blocks((lags, first_lags), (share,), far_parts, near_parts, me)
    back[:, early:, :] = parts[:, share:]
    product_grad = whole(back[...])
    put(2, product_grad * value[...].astype(jnp.float32))
    put(3, product_grad * key[...].astype(jnp.float32))
    put(4, whole(lags[...]))
    first = whole(first_lags[...])
    put(5, first)
    put(6, first[0:1, :])
    for copy in copies:
        copy.wait()


def call(kernel, name, out_shape, places, scratch=(), flops=0, size=0, limit=VMEM_LIMIT, to=pltpu.VMEM):
    return pl.pallas_call(
        kernel,
        name=name,
        out_shape=out_shape,
        in_specs=[pl.BlockSpec(memory_space=place) for place in places],
        out_specs=jax.tree.map(lambda _: pl.BlockSpec(memory_space=to), out_shape),
        scratch_shapes=list(scratch),
        compiler_params=pltpu.CompilerParams(vmem_limit_bytes=limit),
        cost_estimate=pl.CostEstimate(flops=flops, bytes_accessed=size, transcendentals=0),
    )


def exchange(value, axis, distance):
    return lax.ppermute(value, axis, [(i, i ^ distance) for i in range(lax.axis_size(axis))])


def send_parts(parts, axis, near_count, sizes, extra=0):
    far_parts, far_count = list(parts), len(parts)
    for far in range(far_count - 1, 0, -1):
        far_parts[far] = exchange(parts[far], axis, far * near_count)
    payload = jax.ShapeDtypeStruct((far_count * (sum(sizes) + extra), parts[0].shape[1]), jnp.float32)
    relay = call(
        functools.partial(relay_kernel, far_count=far_count, sizes=sizes, extra=extra),
        "relay",
        (payload,) * (near_count - 1),
        (pltpu.VMEM,) * far_count,
        flops=RELAY_WEIGHT,
    )
    near_parts = relay(far_parts[0], *far_parts[:0:-1])
    return far_parts, [exchange(part, axis, near) for near, part in enumerate(near_parts, 1)]


def body(query, key, value, implicit_filter, explicit_taps, skip_gain, out_grad):
    rows, channels = query.shape
    blocks = lax.axis_size("ctx")
    share = channels // blocks
    padded = -(-share // 8) * 8
    f32 = jnp.float32
    shape = functools.partial(jax.ShapeDtypeStruct, dtype=f32)
    grad_scale = 1.0 / math.sqrt(blocks * rows)
    taps, skip = explicit_taps, skip_gain.reshape(1, channels)

    near_count = 1 << (blocks.bit_length() - 1) // 2 if share == padded else 1
    far_count = blocks // near_count
    product = key.astype(f32) * value.astype(f32)
    mix_grad = out_grad.astype(f32) * query.astype(f32)
    split_parts = call(
        functools.partial(split_kernel, near_count=near_count),
        "split",
        (shape((near_count * share, rows)),) * far_count,
        (pltpu.VMEM,),
        scratch=(pltpu.VMEM((channels, rows), f32),),
        size=8 * rows * channels,
    )(implicit_filter)
    packed = call(
        pack_kernel, "pack", shape((blocks, 2, share, rows)), (pltpu.VMEM,) * 2, size=16 * rows * channels
    )(product, mix_grad)
    if near_count > 1:
        far_parts, near_parts = send_parts(split_parts, "ctx", near_count, (share,))
        gates = lax.all_to_all(packed, "ctx", 0, 0, tiled=True)
    else:
        together = jnp.concatenate([packed, jnp.stack(split_parts)[:, None]], axis=1)
        together = lax.all_to_all(together, "ctx", 0, 0, tiled=True)
        together = jnp.pad(together, ((0, 0), (0, 0), (0, padded - share), (0, 0)))
        gates, far_parts, near_parts = together[:, :2], list(together[:, 2]), []
        own = lax.axis_index("ctx") * share
        taps, skip = [
            jnp.pad(lax.dynamic_slice_in_dim(each, own, share, 1), ((0, 0), (0, padded - share)))
            for each in (taps, skip)
        ]
    matrices, twists = tables(blocks, rows)
    height = (blocks + 1) * padded
    matrices, twists = jnp.asarray(matrices), jnp.asarray(twists)
    early = padded // 16 * 8 if near_count > 1 else 0
    block = pltpu.VMEM((blocks, padded, rows), f32)
    products, *split_parts = call(
        functools.partial(spectra_kernel, near_count=near_count, early=early, grad_scale=grad_scale),
        "spectra",
        (shape((2, height, 2 * rows)),) + (shape((near_count * (padded + early) + padded, rows)),) * far_count,
        (pltpu.VMEM,) * (4 + far_count + near_count),
        scratch=(
            pltpu.VMEM((3, height, 2 * rows), f32),
            pltpu.VMEM((height, 2 * rows), f32),
            pltpu.VMEM(taps.shape[::-1], f32),
            block,
            pltpu.VMEM((blocks, max(early, 8), rows), f32),
            block,
        ),
        flops=27 * height * (2 * rows) ** 2,
        size=24 * blocks * padded * rows,
    )(taps, skip, matrices, twists, gates, *far_parts, *near_parts)
    if near_count > 1:
        sizes = (share, early) if early else (share,)
        far_parts, near_parts = send_parts(split_parts, "ctx", near_count, sizes, share)
    results = call(
        functools.partial(mix_kernel, channels=padded, early=early),
        "mix",
        shape((blocks, 2 * padded - early, rows)),
        (pltpu.VMEM,) * 3,
        scratch=(pltpu.VMEM((2, height, 2 * rows), f32),),
        flops=9 * height * (2 * rows) ** 2,
        size=24 * blocks * padded * rows,
    )(matrices, twists, products)
    if near_count > 1:
        parts = lax.all_to_all(results, "ctx", 0, 0, tiled=True)
    else:
        together = jnp.concatenate([results, jnp.stack(split_parts)], axis=1).reshape(blocks, 4, padded, rows)
        together = lax.all_to_all(together[:, :, :share], "ctx", 0, 0, tiled=True).reshape(blocks, 4 * share, rows)
        parts, far_parts, near_parts = together[:, : 2 * share], list(together[:, 2 * share :]), []
    full, one = shape((rows, channels)), shape((1, channels))
    block = pltpu.VMEM((blocks, share, rows), f32)
    outs = call(
        functools.partial(unpack_kernel, far_count=far_count, near_count=near_count, early=early),
        "unpack",
        (full,) * 6 + (one,),
        (pltpu.VMEM,) * (4 + far_count + near_count),
        scratch=tuple(pltpu.VMEM(out.shape, f32) for out in (full,) * 6 + (one,))
        + (pltpu.SemaphoreType.DMA((7,)), block, block, block),
        to=pltpu.HBM,
        size=48 * rows * channels,
    )(query, key, value, out_grad, parts, *far_parts, *near_parts)
    return (*outs[:6], outs[6].reshape(channels))


def solution(mesh):
    in_specs = (
        P("ctx", "ch"),
        P("ctx", "ch"),
        P("ctx", "ch"),
        P("ctx", "ch"),
        P(None, "ch"),
        P("ch"),
        P("ctx", "ch"),
    )
    out_specs = (
        P("ctx", "ch"),
        P("ctx", "ch"),
        P("ctx", "ch"),
        P("ctx", "ch"),
        P("ctx", "ch"),
        P(None, "ch"),
        P("ch"),
    )
    return jax.shard_map(body, mesh=mesh, in_specs=in_specs, out_specs=out_specs, check_vma=False)
```

```python
import functools
import math

import jax
import jax.numpy as jnp
import numpy as np
from jax import lax
from jax.experimental import pallas as pl
from jax.experimental.pallas import tpu as pltpu
from jax.sharding import PartitionSpec as P

VMEM_LIMIT = 48 * 1024 * 1024
RELAY_WEIGHT = 10**11


def turn(value, turns):
    turns = turns % 1.0
    real, imag = value
    if turns == 0.0:
        return value
    if turns == 0.5:
        return (-real, -imag)
    if turns == 0.25:
        return (-imag, real)
    if turns == 0.75:
        return (imag, -real)
    cosine, sine = math.cos(2 * math.pi * turns), math.sin(2 * math.pi * turns)
    if abs(abs(cosine) - abs(sine)) < 1e-12:
        scale = abs(cosine)
        one, two = math.copysign(1.0, cosine), math.copysign(1.0, sine)
        new_real = (real if one > 0 else -real) - (imag if two > 0 else -imag)
        new_imag = (real if two > 0 else -real) + (imag if one > 0 else -imag)
        return (new_real * scale, new_imag * scale)
    return (real * cosine - imag * sine, real * sine + imag * cosine)


def plus(a, b):
    return (a[0] + b[0], a[1] + b[1])


def minus(a, b):
    return (a[0] - b[0], a[1] - b[1])


def complex_transform(values, sign):
    count = len(values)
    if count == 1:
        return values
    even = complex_transform(values[0::2], sign)
    odd = complex_transform(values[1::2], sign)
    odd = [turn(odd[k], sign * k / count) for k in range(count // 2)]
    return [plus(e, o) for e, o in zip(even, odd)] + [minus(e, o) for e, o in zip(even, odd)]


def odd_bins(values):
    length = len(values)
    half = length // 2
    turned = [turn((values[j], -values[j + half]), -j / (2 * length)) for j in range(half)]
    bins = {}
    for m, (real, imag) in enumerate(complex_transform(turned, -1)):
        p = 4 * m + 1
        if p < length:
            bins[p] = (real, imag)
        else:
            bins[2 * length - p] = (real, -imag)
    return bins


def real_bins(values):
    length = len(values)
    if length == 2:
        return {0: (values[0] + values[1], None), 1: (values[0] - values[1], None)}
    half = length // 2
    bins = {}
    for s, value in real_bins([values[j] + values[j + half] for j in range(half)]).items():
        bins[2 * s] = value
    bins.update(odd_bins([values[j] - values[j + half] for j in range(half)]))
    return bins


def padded_bins(values):
    bins = {2 * s: value for s, value in real_bins(values).items()}
    bins.update(odd_bins(values))
    return bins


def odd_bins_back(bins, length):
    half = length // 2
    spectrum = []
    for m in range(half):
        p = 4 * m + 1
        if p < length:
            spectrum.append(bins[p])
        else:
            real, imag = bins[2 * length - p]
            spectrum.append((real, -imag))
    values = complex_transform(spectrum, 1)
    values = [turn(value, j / (2 * length)) for j, value in enumerate(values)]
    return [value[0] for value in values] + [-value[1] for value in values]


def real_bins_back(bins, length):
    if length == 2:
        return [bins[0][0] + bins[1][0], bins[0][0] - bins[1][0]]
    half = length // 2
    even = real_bins_back({s: bins[2 * s] for s in range(half // 2 + 1)}, half)
    odd = odd_bins_back(bins, half)
    return [e + o for e, o in zip(even, odd)] + [e - o for e, o in zip(even, odd)]


def padded_bins_back(bins, length):
    even = real_bins_back({s: bins[2 * s] for s in range(length // 2 + 1)}, length)
    odd = odd_bins_back(bins, length)
    return [e + o for e, o in zip(even, odd)]


def tables(blocks, rows):
    extent = 2 * blocks * rows
    positions = np.arange(rows)
    angle = 2 * np.pi * (np.outer(positions, positions) % rows) / rows
    cosine, sine = np.cos(angle), np.sin(angle)
    forward = np.block([[cosine, -sine], [sine, cosine]])
    matrices = []
    for matrix in (forward, forward.T):
        high = matrix.astype(jnp.bfloat16)
        low = (matrix - high.astype(np.float64)).astype(jnp.bfloat16)
        matrices += [high, low]
    phase = 2 * np.pi * np.outer(np.arange(blocks + 1), positions) / extent
    weight = np.where(np.arange(blocks + 1) % blocks == 0, 1.0, 2.0)[:, None] / extent
    twists = np.stack(
        [np.cos(phase), -np.sin(phase), weight * np.cos(phase), weight * np.sin(phase)], 1
    )
    return np.stack(matrices), twists.astype(np.float32)


def multiply(values, high, low):
    values_high = values.astype(jnp.bfloat16)
    values_low = (values - values_high.astype(jnp.float32)).astype(jnp.bfloat16)
    dot = functools.partial(jnp.dot, preferred_element_type=jnp.float32)
    return dot(values_high, high) + (dot(values_low, high) + dot(values_high, low))


def pack_kernel(product, mix_grad, out):
    blocks, _, share, rows = out.shape
    for a, field in enumerate((product, mix_grad)):
        out[:, a] = field[...].T.reshape(blocks, share, rows)


def farthest_first(far_count):
    return [0, *range(far_count - 1, 0, -1)]


def chunk(sizes, count, field, at):
    return pl.ds(count * sum(sizes[:field]) + at * sizes[field], sizes[field])


def split_kernel(field, *rest, near_count):
    outs, turned = rest[:-1], rest[-1]
    share = outs[0].shape[0] // near_count
    turned[...] = field[...].T
    me = lax.axis_index("ctx") if near_count > 1 else 0
    for far, out in zip(farthest_first(len(outs)), outs):
        for near in range(near_count):
            start = (me ^ (far * near_count + near)) * share
            start = start if near_count == 1 else pl.multiple_of(start, share)
            out[chunk((share,), near_count, 0, near), :] = turned[pl.ds(start, share), :]


def gather_blocks(outs, sizes, far_parts, near_parts, me):
    far_count, near_count = len(far_parts), len(near_parts) + 1
    for far, part in zip(farthest_first(far_count), far_parts):
        for near in range(near_count):
            source = me ^ (far * near_count + near)
            for k, size in enumerate(sizes):
                if near:
                    rows = near_parts[near - 1][chunk(sizes, far_count, k, far), :]
                else:
                    rows = part[chunk(sizes, near_count, k, 0), :]
                outs[k][source, :size, :] = rows
            if len(outs) > len(sizes):
                extra = outs[len(sizes)].shape[1]
                if near:
                    rows = near_parts[near - 1][pl.ds(far_count * sum(sizes) + far * extra, extra), :]
                else:
                    rows = part[pl.ds(near_count * sum(sizes), extra), :]
                outs[len(sizes)][source] = rows


def spectra_kernel(taps, skip, matrices, twists, gates, *rest, near_count, early, grad_scale):
    blocks, _, channels, rows = gates.shape
    far_count = blocks // near_count
    far_parts, rest = rest[:far_count], rest[far_count:]
    near_parts, rest = rest[: near_count - 1], rest[near_count - 1 :]
    products, *outs, spectra, results, direct, lags, back, filters = rest
    me = lax.axis_index("ctx") if near_count > 1 else 0
    gather_blocks((filters,), (channels,), far_parts, near_parts, me)
    row = lax.broadcasted_iota(jnp.int32, taps.shape, 0)
    direct[...] = (taps[...] + jnp.where(row == 0, skip[...], 0.0)).T
    own = 0 if direct.shape[0] == channels else pl.multiple_of(lax.axis_index("ctx") * channels, channels)
    for a in range(3):
        for low in range(0, channels, 8):
            part = pl.ds(low, 8)
            if a == 1:
                values = [filters[j, part, :] for j in range(blocks)]
                values[0] = values[0] + direct[pl.ds(own + low, 8), :]
            else:
                values = [gates[j, a // 2, part, :] for j in range(blocks)]
            bins = padded_bins(values)
            for p in range(blocks + 1):
                real, imag = bins[p]
                cosine, sine = twists[p, 0:1, :], twists[p, 1:2, :]
                place = pl.ds(p * channels + low, 8)
                if imag is None:
                    spectra[a, place, :rows] = real * cosine
                    spectra[a, place, rows:] = real * sine
                else:
                    spectra[a, place, :rows] = real * cosine - imag * sine
                    spectra[a, place, rows:] = real * sine + imag * cosine
    product, filt, mix_grad = [multiply(spectra[a], matrices[0], matrices[1]) for a in range(3)]
    pr, pi = product[:, :rows], product[:, rows:]
    fr, fi = filt[:, :rows], filt[:, rows:]
    gr, gi = mix_grad[:, :rows], mix_grad[:, rows:]
    spectra[0, :, :rows] = pr * gr + pi * gi
    spectra[0, :, rows:] = pr * gi - pi * gr
    products[0, :, :rows] = fr * pr - fi * pi
    products[0, :, rows:] = fr * pi + fi * pr
    products[1, :, :rows] = fr * gr + fi * gi
    products[1, :, rows:] = fr * gi - fi * gr
    for low, values in blocks_back(spectra.at[0], results, matrices, twists, channels, 0, channels):
        for j, value in enumerate(values):
            lags[j, pl.ds(low, 8), :] = value * grad_scale
    for low, values in blocks_back(products.at[1], results, matrices, twists, channels, 0, early):
        for j, value in enumerate(values):
            back[j, pl.ds(low, 8), :] = value
    sizes = (channels, early) if early else (channels,)
    for far, out in zip(farthest_first(far_count), outs):
        for near in range(near_count):
            target = me ^ (far * near_count + near)
            for k, size in enumerate(sizes):
                out[chunk(sizes, near_count, k, near), :] = (lags, back)[k][target]
        out[pl.ds(near_count * sum(sizes), channels), :] = lags[0]


def blocks_back(spectrum, result, matrices, twists, channels, first, last):
    blocks, rows = twists.shape[0] - 1, twists.shape[2]
    count = last - first
    if count == 0:
        return
    height = (blocks + 1) * count
    wanted = spectrum[...].reshape(blocks + 1, channels, 2 * rows)[:, first:last].reshape(height, 2 * rows)
    result[:height, :] = multiply(wanted, matrices[2], matrices[3])
    for low in range(0, count, 8):
        bins = {}
        for p in range(blocks + 1):
            cosine, sine = twists[p, 2:3, :], twists[p, 3:4, :]
            place = pl.ds(p * count + low, 8)
            real, imag = result[place, :rows], result[place, rows:]
            new_real = real * cosine - imag * sine
            bins[p] = (new_real, None if p % blocks == 0 else real * sine + imag * cosine)
        yield low, padded_bins_back(bins, blocks)


def mix_kernel(matrices, twists, products, out, results, *, channels, early):
    for a, first in enumerate((0, early)):
        for low, values in blocks_back(products.at[a], results.at[a], matrices, twists, channels, first, channels):
            for j, value in enumerate(values):
                out[j, pl.ds(a * channels + low, 8), :] = value


def relay_kernel(*refs, far_count, sizes, extra):
    parts = refs[:far_count]
    outs = refs[far_count:]
    near_count = len(outs) + 1
    for near, out in enumerate(outs, 1):
        for far, part in enumerate(parts):
            for k in range(len(sizes)):
                out[chunk(sizes, far_count, k, far), :] = part[chunk(sizes, near_count, k, near), :]
            if extra:
                place = pl.ds(far_count * sum(sizes) + far * extra, extra)
                out[place, :] = part[pl.ds(near_count * sum(sizes), extra), :]


def unpack_kernel(query, key, value, grad, parts, *rest, far_count, near_count, early):
    far_parts, rest = rest[:far_count], rest[far_count:]
    near_parts, rest = rest[: near_count - 1], rest[near_count - 1 :]
    outs, held, sent, lags, back, first_lags = rest[:7], rest[7:14], rest[14], rest[15], rest[16], rest[17]
    rows, channels = query.shape
    blocks, share, _ = lags.shape
    copies = [
        pltpu.make_async_copy(source, target, sent.at[i])
        for i, (source, target) in enumerate(zip(held, outs))
    ]

    def whole(array):
        return array.reshape(channels, rows).T

    def put(i, array):
        held[i][...] = array
        copies[i].start()

    mixer = whole(parts[:, :share])
    put(0, query[...].astype(jnp.float32) * mixer)
    put(1, grad[...].astype(jnp.float32) * mixer)
    me = lax.axis_index("ctx") if near_count > 1 else 0
    if early:
        gather_blocks((lags, back, first_lags), (share, early), far_parts, near_parts, me)
    else:
        gather_blocks((lags, first_lags), (share,), far_parts, near_parts, me)
    back[:, early:, :] = parts[:, share:]
    product_grad = whole(back[...])
    put(2, product_grad * value[...].astype(jnp.float32))
    put(3, product_grad * key[...].astype(jnp.float32))
    put(4, whole(lags[...]))
    first = whole(first_lags[...])
    put(5, first)
    put(6, first[0:1, :])
    for copy in copies:
        copy.wait()


def call(kernel, name, out_shape, places, scratch=(), flops=0, size=0, limit=VMEM_LIMIT, to=pltpu.VMEM):
    return pl.pallas_call(
        kernel,
        name=name,
        out_shape=out_shape,
        in_specs=[pl.BlockSpec(memory_space=place) for place in places],
        out_specs=jax.tree.map(lambda _: pl.BlockSpec(memory_space=to), out_shape),
        scratch_shapes=list(scratch),
        compiler_params=pltpu.CompilerParams(vmem_limit_bytes=limit),
        cost_estimate=pl.CostEstimate(flops=flops, bytes_accessed=size, transcendentals=0),
    )


def exchange(value, axis, distance):
    return lax.ppermute(value, axis, [(i, i ^ distance) for i in range(lax.axis_size(axis))])


def send_parts(parts, axis, near_count, sizes, extra=0):
    far_count = len(parts)
    far_parts = [parts[0]] * far_count
    for far, part in zip(farthest_first(far_count)[1:], parts[1:]):
        far_parts[far] = exchange(part, axis, far * near_count)
    payload = jax.ShapeDtypeStruct((far_count * (sum(sizes) + extra), parts[0].shape[1]), jnp.float32)
    relay = call(
        functools.partial(relay_kernel, far_count=far_count, sizes=sizes, extra=extra),
        "relay",
        (payload,) * (near_count - 1),
        (pltpu.VMEM,) * far_count,
        flops=RELAY_WEIGHT,
    )
    near_parts = relay(*far_parts)
    return [far_parts[far] for far in farthest_first(far_count)], [exchange(part, axis, near) for near, part in enumerate(near_parts, 1)]


def body(query, key, value, implicit_filter, explicit_taps, skip_gain, out_grad):
    rows, channels = query.shape
    blocks = lax.axis_size("ctx")
    share = channels // blocks
    padded = -(-share // 8) * 8
    f32 = jnp.float32
    shape = functools.partial(jax.ShapeDtypeStruct, dtype=f32)
    grad_scale = 1.0 / math.sqrt(blocks * rows)
    taps, skip = explicit_taps, skip_gain.reshape(1, channels)

    near_count = 1 << (blocks.bit_length() - 1) // 2 if share == padded else 1
    far_count = blocks // near_count
    product = key.astype(f32) * value.astype(f32)
    mix_grad = out_grad.astype(f32) * query.astype(f32)
    split_parts = call(
        functools.partial(split_kernel, near_count=near_count),
        "split",
        (shape((near_count * share, rows)),) * far_count,
        (pltpu.VMEM,),
        scratch=(pltpu.VMEM((channels, rows), f32),),
        size=8 * rows * channels,
    )(implicit_filter)
    packed = call(
        pack_kernel, "pack", shape((blocks, 2, share, rows)), (pltpu.VMEM,) * 2, size=16 * rows * channels
    )(product, mix_grad)
    if near_count > 1:
        far_parts, near_parts = send_parts(split_parts, "ctx", near_count, (share,))
        gates = lax.all_to_all(packed, "ctx", 0, 0, tiled=True)
    else:
        together = jnp.concatenate([packed, jnp.stack([split_parts[far] for far in farthest_first(blocks)])[:, None]], axis=1)
        together = lax.all_to_all(together, "ctx", 0, 0, tiled=True)
        together = jnp.pad(together, ((0, 0), (0, 0), (0, padded - share), (0, 0)))
        gates, far_parts, near_parts = together[:, :2], [together[far, 2] for far in farthest_first(blocks)], []
        own = lax.axis_index("ctx") * share
        taps, skip = [
            jnp.pad(lax.dynamic_slice_in_dim(each, own, share, 1), ((0, 0), (0, padded - share)))
            for each in (taps, skip)
        ]
    matrices, twists = tables(blocks, rows)
    height = (blocks + 1) * padded
    matrices, twists = jnp.asarray(matrices), jnp.asarray(twists)
    early = padded // 16 * 8 if near_count > 1 else 0
    block = pltpu.VMEM((blocks, padded, rows), f32)
    products, *split_parts = call(
        functools.partial(spectra_kernel, near_count=near_count, early=early, grad_scale=grad_scale),
        "spectra",
        (shape((2, height, 2 * rows)),) + (shape((near_count * (padded + early) + padded, rows)),) * far_count,
        (pltpu.VMEM,) * (4 + far_count + near_count),
        scratch=(
            pltpu.VMEM((3, height, 2 * rows), f32),
            pltpu.VMEM((height, 2 * rows), f32),
            pltpu.VMEM(taps.shape[::-1], f32),
            block,
            pltpu.VMEM((blocks, max(early, 8), rows), f32),
            block,
        ),
        flops=27 * height * (2 * rows) ** 2,
        size=24 * blocks * padded * rows,
    )(taps, skip, matrices, twists, gates, *far_parts, *near_parts)
    if near_count > 1:
        sizes = (share, early) if early else (share,)
        far_parts, near_parts = send_parts(split_parts, "ctx", near_count, sizes, share)
    results = call(
        functools.partial(mix_kernel, channels=padded, early=early),
        "mix",
        shape((blocks, 2 * padded - early, rows)),
        (pltpu.VMEM,) * 3,
        scratch=(pltpu.VMEM((2, height, 2 * rows), f32),),
        flops=9 * height * (2 * rows) ** 2,
        size=24 * blocks * padded * rows,
    )(matrices, twists, products)
    if near_count > 1:
        parts = lax.all_to_all(results, "ctx", 0, 0, tiled=True)
    else:
        together = jnp.concatenate(
            [results, jnp.stack([split_parts[far] for far in farthest_first(blocks)])], axis=1
        ).reshape(blocks, 4, padded, rows)
        together = lax.all_to_all(together[:, :, :share], "ctx", 0, 0, tiled=True).reshape(blocks, 4 * share, rows)
        parts, near_parts = together[:, : 2 * share], []
        far_parts = [together[far, 2 * share :] for far in farthest_first(blocks)]
    full, one = shape((rows, channels)), shape((1, channels))
    block = pltpu.VMEM((blocks, share, rows), f32)
    outs = call(
        functools.partial(unpack_kernel, far_count=far_count, near_count=near_count, early=early),
        "unpack",
        (full,) * 6 + (one,),
        (pltpu.VMEM,) * (4 + far_count + near_count),
        scratch=tuple(pltpu.VMEM(out.shape, f32) for out in (full,) * 6 + (one,))
        + (pltpu.SemaphoreType.DMA((7,)), block, block, block),
        to=pltpu.HBM,
        size=48 * rows * channels,
    )(query, key, value, out_grad, parts, *far_parts, *near_parts)
    return (*outs[:6], outs[6].reshape(channels))


def solution(mesh):
    in_specs = (
        P("ctx", "ch"),
        P("ctx", "ch"),
        P("ctx", "ch"),
        P("ctx", "ch"),
        P(None, "ch"),
        P("ch"),
        P("ctx", "ch"),
    )
    out_specs = (
        P("ctx", "ch"),
        P("ctx", "ch"),
        P("ctx", "ch"),
        P("ctx", "ch"),
        P("ctx", "ch"),
        P(None, "ch"),
        P("ch"),
    )
    return jax.shard_map(body, mesh=mesh, in_specs=in_specs, out_specs=out_specs, check_vma=False)
```

```python
import functools
import math

import jax
import jax.numpy as jnp
import numpy as np
from jax import lax
from jax.experimental import pallas as pl
from jax.experimental.pallas import tpu as pltpu
from jax.sharding import PartitionSpec as P

VMEM_LIMIT = 48 * 1024 * 1024
RELAY_WEIGHT = 10**11


def turn(value, turns):
    turns = turns % 1.0
    real, imag = value
    if turns == 0.0:
        return value
    if turns == 0.5:
        return (-real, -imag)
    if turns == 0.25:
        return (-imag, real)
    if turns == 0.75:
        return (imag, -real)
    cosine, sine = math.cos(2 * math.pi * turns), math.sin(2 * math.pi * turns)
    if abs(abs(cosine) - abs(sine)) < 1e-12:
        scale = abs(cosine)
        one, two = math.copysign(1.0, cosine), math.copysign(1.0, sine)
        new_real = (real if one > 0 else -real) - (imag if two > 0 else -imag)
        new_imag = (real if two > 0 else -real) + (imag if one > 0 else -imag)
        return (new_real * scale, new_imag * scale)
    return (real * cosine - imag * sine, real * sine + imag * cosine)


def plus(a, b):
    return (a[0] + b[0], a[1] + b[1])


def minus(a, b):
    return (a[0] - b[0], a[1] - b[1])


def complex_transform(values, sign):
    count = len(values)
    if count == 1:
        return values
    even = complex_transform(values[0::2], sign)
    odd = complex_transform(values[1::2], sign)
    odd = [turn(odd[k], sign * k / count) for k in range(count // 2)]
    return [plus(e, o) for e, o in zip(even, odd)] + [minus(e, o) for e, o in zip(even, odd)]


def odd_bins(values):
    length = len(values)
    half = length // 2
    turned = [turn((values[j], -values[j + half]), -j / (2 * length)) for j in range(half)]
    bins = {}
    for m, (real, imag) in enumerate(complex_transform(turned, -1)):
        p = 4 * m + 1
        if p < length:
            bins[p] = (real, imag)
        else:
            bins[2 * length - p] = (real, -imag)
    return bins


def real_bins(values):
    length = len(values)
    if length == 2:
        return {0: (values[0] + values[1], None), 1: (values[0] - values[1], None)}
    half = length // 2
    bins = {}
    for s, value in real_bins([values[j] + values[j + half] for j in range(half)]).items():
        bins[2 * s] = value
    bins.update(odd_bins([values[j] - values[j + half] for j in range(half)]))
    return bins


def padded_bins(values):
    bins = {2 * s: value for s, value in real_bins(values).items()}
    bins.update(odd_bins(values))
    return bins


def odd_bins_back(bins, length):
    half = length // 2
    spectrum = []
    for m in range(half):
        p = 4 * m + 1
        if p < length:
            spectrum.append(bins[p])
        else:
            real, imag = bins[2 * length - p]
            spectrum.append((real, -imag))
    values = complex_transform(spectrum, 1)
    values = [turn(value, j / (2 * length)) for j, value in enumerate(values)]
    return [value[0] for value in values] + [-value[1] for value in values]


def real_bins_back(bins, length):
    if length == 2:
        return [bins[0][0] + bins[1][0], bins[0][0] - bins[1][0]]
    half = length // 2
    even = real_bins_back({s: bins[2 * s] for s in range(half // 2 + 1)}, half)
    odd = odd_bins_back(bins, half)
    return [e + o for e, o in zip(even, odd)] + [e - o for e, o in zip(even, odd)]


def padded_bins_back(bins, length):
    even = real_bins_back({s: bins[2 * s] for s in range(length // 2 + 1)}, length)
    odd = odd_bins_back(bins, length)
    return [e + o for e, o in zip(even, odd)]


def tables(blocks, rows):
    extent = 2 * blocks * rows
    positions = np.arange(rows)
    angle = 2 * np.pi * (np.outer(positions, positions) % rows) / rows
    cosine, sine = np.cos(angle), np.sin(angle)
    forward = np.block([[cosine, -sine], [sine, cosine]])
    matrices = []
    for matrix in (forward, forward.T):
        high = matrix.astype(jnp.bfloat16)
        low = (matrix - high.astype(np.float64)).astype(jnp.bfloat16)
        matrices += [high, low]
    phase = 2 * np.pi * np.outer(np.arange(blocks + 1), positions) / extent
    weight = np.where(np.arange(blocks + 1) % blocks == 0, 1.0, 2.0)[:, None] / extent
    twists = np.stack(
        [np.cos(phase), -np.sin(phase), weight * np.cos(phase), weight * np.sin(phase)], 1
    )
    return np.stack(matrices), twists.astype(np.float32)


def multiply(values, high, low):
    values_high = values.astype(jnp.bfloat16)
    values_low = (values - values_high.astype(jnp.float32)).astype(jnp.bfloat16)
    dot = functools.partial(jnp.dot, preferred_element_type=jnp.float32)
    return dot(values_high, high) + (dot(values_low, high) + dot(values_high, low))


def pack_kernel(product, mix_grad, out, held, sent):
    blocks, _, share, rows = out.shape
    copies = [pltpu.make_async_copy(held.at[:, a], out.at[:, a], sent.at[a]) for a in range(2)]
    for a, field in enumerate((product, mix_grad)):
        held[:, a] = field[...].T.reshape(blocks, share, rows)
        copies[a].start()
    for copy in copies:
        copy.wait()


def chunk(sizes, count, field, at):
    return pl.ds(count * sum(sizes[:field]) + at * sizes[field], sizes[field])


def split_kernel(field, *rest, near_count):
    outs, turned = rest[:-1], rest[-1]
    share = outs[0].shape[0] // near_count
    turned[...] = field[...].T
    me = lax.axis_index("ctx") if near_count > 1 else 0
    for far, out in enumerate(outs):
        for near in range(near_count):
            start = (me ^ (far * near_count + near)) * share
            start = start if near_count == 1 else pl.multiple_of(start, share)
            out[chunk((share,), near_count, 0, near), :] = turned[pl.ds(start, share), :]


def gather_blocks(outs, sizes, far_parts, near_parts, me):
    far_count, near_count = len(far_parts), len(near_parts) + 1
    for far, part in enumerate(far_parts):
        for near in range(near_count):
            source = me ^ (far * near_count + near)
            for k, size in enumerate(sizes):
                if near:
                    rows = near_parts[near - 1][chunk(sizes, far_count, k, far), :]
                else:
                    rows = part[chunk(sizes, near_count, k, 0), :]
                outs[k][source, :size, :] = rows
            if len(outs) > len(sizes):
                extra = outs[len(sizes)].shape[1]
                if near:
                    rows = near_parts[near - 1][pl.ds(far_count * sum(sizes) + far * extra, extra), :]
                else:
                    rows = part[pl.ds(near_count * sum(sizes), extra), :]
                outs[len(sizes)][source] = rows


def spectra_kernel(taps, skip, matrices, twists, gates, *rest, near_count, early, grad_scale):
    blocks, _, channels, rows = gates.shape
    far_count = blocks // near_count
    far_parts, rest = rest[:far_count], rest[far_count:]
    near_parts, rest = rest[: near_count - 1], rest[near_count - 1 :]
    products, *outs, spectra, results, direct, lags, back, filters = rest
    me = lax.axis_index("ctx") if near_count > 1 else 0
    gather_blocks((filters,), (channels,), far_parts, near_parts, me)
    row = lax.broadcasted_iota(jnp.int32, taps.shape, 0)
    direct[...] = (taps[...] + jnp.where(row == 0, skip[...], 0.0)).T
    own = 0 if direct.shape[0] == channels else pl.multiple_of(lax.axis_index("ctx") * channels, channels)
    for a in range(3):
        for low in range(0, channels, 8):
            part = pl.ds(low, 8)
            if a == 1:
                values = [filters[j, part, :] for j in range(blocks)]
                values[0] = values[0] + direct[pl.ds(own + low, 8), :]
            else:
                values = [gates[j, a // 2, part, :] for j in range(blocks)]
            bins = padded_bins(values)
            for p in range(blocks + 1):
                real, imag = bins[p]
                cosine, sine = twists[p, 0:1, :], twists[p, 1:2, :]
                place = pl.ds(p * channels + low, 8)
                if imag is None:
                    spectra[a, place, :rows] = real * cosine
                    spectra[a, place, rows:] = real * sine
                else:
                    spectra[a, place, :rows] = real * cosine - imag * sine
                    spectra[a, place, rows:] = real * sine + imag * cosine
    product, filt, mix_grad = [multiply(spectra[a], matrices[0], matrices[1]) for a in range(3)]
    pr, pi = product[:, :rows], product[:, rows:]
    fr, fi = filt[:, :rows], filt[:, rows:]
    gr, gi = mix_grad[:, :rows], mix_grad[:, rows:]
    spectra[0, :, :rows] = pr * gr + pi * gi
    spectra[0, :, rows:] = pr * gi - pi * gr
    products[0, :, :rows] = fr * pr - fi * pi
    products[0, :, rows:] = fr * pi + fi * pr
    products[1, :, :rows] = fr * gr + fi * gi
    products[1, :, rows:] = fr * gi - fi * gr
    for low, values in blocks_back(spectra.at[0], results, matrices, twists, channels, 0, channels):
        for j, value in enumerate(values):
            lags[j, pl.ds(low, 8), :] = value * grad_scale
    for low, values in blocks_back(products.at[1], results, matrices, twists, channels, 0, early):
        for j, value in enumerate(values):
            back[j, pl.ds(low, 8), :] = value
    sizes = (channels, early) if early else (channels,)
    for far, out in enumerate(outs):
        for near in range(near_count):
            target = me ^ (far * near_count + near)
            for k, size in enumerate(sizes):
                out[chunk(sizes, near_count, k, near), :] = (lags, back)[k][target]
        out[pl.ds(near_count * sum(sizes), channels), :] = lags[0]


def blocks_back(spectrum, result, matrices, twists, channels, first, last):
    blocks, rows = twists.shape[0] - 1, twists.shape[2]
    count = last - first
    if count == 0:
        return
    height = (blocks + 1) * count
    wanted = spectrum[...].reshape(blocks + 1, channels, 2 * rows)[:, first:last].reshape(height, 2 * rows)
    result[:height, :] = multiply(wanted, matrices[2], matrices[3])
    for low in range(0, count, 8):
        bins = {}
        for p in range(blocks + 1):
            cosine, sine = twists[p, 2:3, :], twists[p, 3:4, :]
            place = pl.ds(p * count + low, 8)
            real, imag = result[place, :rows], result[place, rows:]
            new_real = real * cosine - imag * sine
            bins[p] = (new_real, None if p % blocks == 0 else real * sine + imag * cosine)
        yield low, padded_bins_back(bins, blocks)


def mix_kernel(matrices, twists, products, out, results, held, sent, *, channels, early):
    places = [pl.ds(0, channels), pl.ds(channels, channels - early)]
    copies = [
        pltpu.make_async_copy(held.at[:, place], out.at[:, place], sent.at[a]) for a, place in enumerate(places)
    ]
    for a, first in enumerate((0, early)):
        for low, values in blocks_back(products.at[a], results.at[a], matrices, twists, channels, first, channels):
            for j, value in enumerate(values):
                held[j, pl.ds(a * channels + low, 8), :] = value
        copies[a].start()
    for copy in copies:
        copy.wait()


def relay_kernel(*refs, far_count, sizes, extra):
    parts = (refs[0], *refs[1:far_count][::-1])
    outs = refs[far_count:]
    near_count = len(outs) + 1
    for near, out in enumerate(outs, 1):
        for far, part in enumerate(parts):
            for k in range(len(sizes)):
                out[chunk(sizes, far_count, k, far), :] = part[chunk(sizes, near_count, k, near), :]
            if extra:
                place = pl.ds(far_count * sum(sizes) + far * extra, extra)
                out[place, :] = part[pl.ds(near_count * sum(sizes), extra), :]


def unpack_kernel(query, key, value, grad, parts, *rest, far_count, near_count, early):
    far_parts, rest = rest[:far_count], rest[far_count:]
    near_parts, rest = rest[: near_count - 1], rest[near_count - 1 :]
    outs, held, sent, lags, back, first_lags = rest[:7], rest[7:14], rest[14], rest[15], rest[16], rest[17]
    rows, channels = query.shape
    blocks, share, _ = lags.shape
    copies = [
        pltpu.make_async_copy(source, target, sent.at[i])
        for i, (source, target) in enumerate(zip(held, outs))
    ]

    def whole(array):
        return array.reshape(channels, rows).T

    def put(i, array):
        held[i][...] = array
        copies[i].start()

    mixer = whole(parts[:, :share])
    put(0, query[...].astype(jnp.float32) * mixer)
    put(1, grad[...].astype(jnp.float32) * mixer)
    me = lax.axis_index("ctx") if near_count > 1 else 0
    if early:
        gather_blocks((lags, back, first_lags), (share, early), far_parts, near_parts, me)
    else:
        gather_blocks((lags, first_lags), (share,), far_parts, near_parts, me)
    back[:, early:, :] = parts[:, share:]
    product_grad = whole(back[...])
    put(2, product_grad * value[...].astype(jnp.float32))
    put(3, product_grad * key[...].astype(jnp.float32))
    put(4, whole(lags[...]))
    first = whole(first_lags[...])
    put(5, first)
    put(6, first[0:1, :])
    for copy in copies:
        copy.wait()


def call(kernel, name, out_shape, places, scratch=(), flops=0, size=0, limit=VMEM_LIMIT, to=pltpu.VMEM):
    return pl.pallas_call(
        kernel,
        name=name,
        out_shape=out_shape,
        in_specs=[pl.BlockSpec(memory_space=place) for place in places],
        out_specs=jax.tree.map(lambda _: pl.BlockSpec(memory_space=to), out_shape),
        scratch_shapes=list(scratch),
        compiler_params=pltpu.CompilerParams(vmem_limit_bytes=limit),
        cost_estimate=pl.CostEstimate(flops=flops, bytes_accessed=size, transcendentals=0),
    )


def exchange(value, axis, distance):
    return lax.ppermute(value, axis, [(i, i ^ distance) for i in range(lax.axis_size(axis))])


def send_parts(parts, axis, near_count, sizes, extra=0):
    far_parts, far_count = list(parts), len(parts)
    for far in range(far_count - 1, 0, -1):
        far_parts[far] = exchange(parts[far], axis, far * near_count)
    payload = jax.ShapeDtypeStruct((far_count * (sum(sizes) + extra), parts[0].shape[1]), jnp.float32)
    relay = call(
        functools.partial(relay_kernel, far_count=far_count, sizes=sizes, extra=extra),
        "relay",
        (payload,) * (near_count - 1),
        (pltpu.VMEM,) * far_count,
        flops=RELAY_WEIGHT,
    )
    near_parts = relay(far_parts[0], *far_parts[:0:-1])
    return far_parts, [exchange(part, axis, near) for near, part in enumerate(near_parts, 1)]


def body(query, key, value, implicit_filter, explicit_taps, skip_gain, out_grad):
    rows, channels = query.shape
    blocks = lax.axis_size("ctx")
    share = channels // blocks
    padded = -(-share // 8) * 8
    f32 = jnp.float32
    shape = functools.partial(jax.ShapeDtypeStruct, dtype=f32)
    grad_scale = 1.0 / math.sqrt(blocks * rows)
    taps, skip = explicit_taps, skip_gain.reshape(1, channels)

    near_count = 1 << (blocks.bit_length() - 1) // 2 if share == padded else 1
    far_count = blocks // near_count
    product = key.astype(f32) * value.astype(f32)
    mix_grad = out_grad.astype(f32) * query.astype(f32)
    split_parts = call(
        functools.partial(split_kernel, near_count=near_count),
        "split",
        (shape((near_count * share, rows)),) * far_count,
        (pltpu.VMEM,),
        scratch=(pltpu.VMEM((channels, rows), f32),),
        size=8 * rows * channels,
    )(implicit_filter)
    both = shape((blocks, 2, share, rows))
    packed = call(
        pack_kernel,
        "pack",
        both,
        (pltpu.VMEM,) * 2,
        scratch=(pltpu.VMEM(both.shape, f32), pltpu.SemaphoreType.DMA((2,))),
        to=pltpu.HBM,
        size=16 * rows * channels,
    )(product, mix_grad)
    if near_count > 1:
        far_parts, near_parts = send_parts(split_parts, "ctx", near_count, (share,))
        gates = lax.all_to_all(packed, "ctx", 0, 0, tiled=True)
    else:
        together = jnp.concatenate([packed, jnp.stack(split_parts)[:, None]], axis=1)
        together = lax.all_to_all(together, "ctx", 0, 0, tiled=True)
        together = jnp.pad(together, ((0, 0), (0, 0), (0, padded - share), (0, 0)))
        gates, far_parts, near_parts = together[:, :2], list(together[:, 2]), []
        own = lax.axis_index("ctx") * share
        taps, skip = [
            jnp.pad(lax.dynamic_slice_in_dim(each, own, share, 1), ((0, 0), (0, padded - share)))
            for each in (taps, skip)
        ]
    matrices, twists = tables(blocks, rows)
    height = (blocks + 1) * padded
    matrices, twists = jnp.asarray(matrices), jnp.asarray(twists)
    early = padded // 32 * 8 if near_count > 1 else 0
    block = pltpu.VMEM((blocks, padded, rows), f32)
    products, *split_parts = call(
        functools.partial(spectra_kernel, near_count=near_count, early=early, grad_scale=grad_scale),
        "spectra",
        (shape((2, height, 2 * rows)),) + (shape((near_count * (padded + early) + padded, rows)),) * far_count,
        (pltpu.VMEM,) * (4 + far_count + near_count),
        scratch=(
            pltpu.VMEM((3, height, 2 * rows), f32),
            pltpu.VMEM((height, 2 * rows), f32),
            pltpu.VMEM(taps.shape[::-1], f32),
            block,
            pltpu.VMEM((blocks, max(early, 8), rows), f32),
            block,
        ),
        flops=27 * height * (2 * rows) ** 2,
        size=24 * blocks * padded * rows,
    )(taps, skip, matrices, twists, gates, *far_parts, *near_parts)
    if near_count > 1:
        sizes = (share, early) if early else (share,)
        far_parts, near_parts = send_parts(split_parts, "ctx", near_count, sizes, share)
    late = shape((blocks, 2 * padded - early, rows))
    results = call(
        functools.partial(mix_kernel, channels=padded, early=early),
        "mix",
        late,
        (pltpu.VMEM,) * 3,
        scratch=(pltpu.VMEM((2, height, 2 * rows), f32), pltpu.VMEM(late.shape, f32), pltpu.SemaphoreType.DMA((2,))),
        to=pltpu.HBM,
        flops=9 * height * (2 * rows) ** 2,
        size=24 * blocks * padded * rows,
    )(matrices, twists, products)
    if near_count > 1:
        parts = lax.all_to_all(results, "ctx", 0, 0, tiled=True)
    else:
        together = jnp.concatenate([results, jnp.stack(split_parts)], axis=1).reshape(blocks, 4, padded, rows)
        together = lax.all_to_all(together[:, :, :share], "ctx", 0, 0, tiled=True).reshape(blocks, 4 * share, rows)
        parts, far_parts, near_parts = together[:, : 2 * share], list(together[:, 2 * share :]), []
    full, one = shape((rows, channels)), shape((1, channels))
    block = pltpu.VMEM((blocks, share, rows), f32)
    outs = call(
        functools.partial(unpack_kernel, far_count=far_count, near_count=near_count, early=early),
        "unpack",
        (full,) * 6 + (one,),
        (pltpu.VMEM,) * (4 + far_count + near_count),
        scratch=tuple(pltpu.VMEM(out.shape, f32) for out in (full,) * 6 + (one,))
        + (pltpu.SemaphoreType.DMA((7,)), block, block, block),
        to=pltpu.HBM,
        size=48 * rows * channels,
    )(query, key, value, out_grad, parts, *far_parts, *near_parts)
    return (*outs[:6], outs[6].reshape(channels))


def solution(mesh):
    in_specs = (
        P("ctx", "ch"),
        P("ctx", "ch"),
        P("ctx", "ch"),
        P("ctx", "ch"),
        P(None, "ch"),
        P("ch"),
        P("ctx", "ch"),
    )
    out_specs = (
        P("ctx", "ch"),
        P("ctx", "ch"),
        P("ctx", "ch"),
        P("ctx", "ch"),
        P("ctx", "ch"),
        P(None, "ch"),
        P("ch"),
    )
    return jax.shard_map(body, mesh=mesh, in_specs=in_specs, out_specs=out_specs, check_vma=False)
```

```python
import functools
import math

import jax
import jax.numpy as jnp
import numpy as np
from jax import lax
from jax.experimental import pallas as pl
from jax.experimental.pallas import tpu as pltpu
from jax.sharding import PartitionSpec as P

VMEM_LIMIT = 48 * 1024 * 1024
RELAY_WEIGHT = 10**11


def turn(value, turns):
    turns = turns % 1.0
    real, imag = value
    if turns == 0.0:
        return value
    if turns == 0.5:
        return (-real, -imag)
    if turns == 0.25:
        return (-imag, real)
    if turns == 0.75:
        return (imag, -real)
    cosine, sine = math.cos(2 * math.pi * turns), math.sin(2 * math.pi * turns)
    if abs(abs(cosine) - abs(sine)) < 1e-12:
        scale = abs(cosine)
        one, two = math.copysign(1.0, cosine), math.copysign(1.0, sine)
        new_real = (real if one > 0 else -real) - (imag if two > 0 else -imag)
        new_imag = (real if two > 0 else -real) + (imag if one > 0 else -imag)
        return (new_real * scale, new_imag * scale)
    return (real * cosine - imag * sine, real * sine + imag * cosine)


def plus(a, b):
    return (a[0] + b[0], a[1] + b[1])


def minus(a, b):
    return (a[0] - b[0], a[1] - b[1])


def complex_transform(values, sign):
    count = len(values)
    if count == 1:
        return values
    even = complex_transform(values[0::2], sign)
    odd = complex_transform(values[1::2], sign)
    odd = [turn(odd[k], sign * k / count) for k in range(count // 2)]
    return [plus(e, o) for e, o in zip(even, odd)] + [minus(e, o) for e, o in zip(even, odd)]


def odd_bins(values):
    length = len(values)
    half = length // 2
    turned = [turn((values[j], -values[j + half]), -j / (2 * length)) for j in range(half)]
    bins = {}
    for m, (real, imag) in enumerate(complex_transform(turned, -1)):
        p = 4 * m + 1
        if p < length:
            bins[p] = (real, imag)
        else:
            bins[2 * length - p] = (real, -imag)
    return bins


def real_bins(values):
    length = len(values)
    if length == 2:
        return {0: (values[0] + values[1], None), 1: (values[0] - values[1], None)}
    half = length // 2
    bins = {}
    for s, value in real_bins([values[j] + values[j + half] for j in range(half)]).items():
        bins[2 * s] = value
    bins.update(odd_bins([values[j] - values[j + half] for j in range(half)]))
    return bins


def padded_bins(values):
    bins = {2 * s: value for s, value in real_bins(values).items()}
    bins.update(odd_bins(values))
    return bins


def odd_bins_back(bins, length):
    half = length // 2
    spectrum = []
    for m in range(half):
        p = 4 * m + 1
        if p < length:
            spectrum.append(bins[p])
        else:
            real, imag = bins[2 * length - p]
            spectrum.append((real, -imag))
    values = complex_transform(spectrum, 1)
    values = [turn(value, j / (2 * length)) for j, value in enumerate(values)]
    return [value[0] for value in values] + [-value[1] for value in values]


def real_bins_back(bins, length):
    if length == 2:
        return [bins[0][0] + bins[1][0], bins[0][0] - bins[1][0]]
    half = length // 2
    even = real_bins_back({s: bins[2 * s] for s in range(half // 2 + 1)}, half)
    odd = odd_bins_back(bins, half)
    return [e + o for e, o in zip(even, odd)] + [e - o for e, o in zip(even, odd)]


def padded_bins_back(bins, length):
    even = real_bins_back({s: bins[2 * s] for s in range(length // 2 + 1)}, length)
    odd = odd_bins_back(bins, length)
    return [e + o for e, o in zip(even, odd)]


def tables(blocks, rows):
    extent = 2 * blocks * rows
    positions = np.arange(rows)
    angle = 2 * np.pi * (np.outer(positions, positions) % rows) / rows
    cosine, sine = np.cos(angle), np.sin(angle)
    forward = np.block([[cosine, -sine], [sine, cosine]])
    matrices = []
    for matrix in (forward, forward.T):
        high = matrix.astype(jnp.bfloat16)
        low = (matrix - high.astype(np.float64)).astype(jnp.bfloat16)
        matrices += [high, low]
    phase = 2 * np.pi * np.outer(np.arange(blocks + 1), positions) / extent
    weight = np.where(np.arange(blocks + 1) % blocks == 0, 1.0, 2.0)[:, None] / extent
    twists = np.stack(
        [np.cos(phase), -np.sin(phase), weight * np.cos(phase), weight * np.sin(phase)], 1
    )
    return np.stack(matrices), twists.astype(np.float32)


def multiply(values, high, low):
    values_high = values.astype(jnp.bfloat16)
    values_low = (values - values_high.astype(jnp.float32)).astype(jnp.bfloat16)
    dot = functools.partial(jnp.dot, preferred_element_type=jnp.float32)
    return dot(values_high, high) + (dot(values_low, high) + dot(values_high, low))


def pack_kernel(product, mix_grad, out, held, sent, *, early):
    blocks, _, rows = out.shape
    share = product.shape[1] // blocks
    places = [pl.ds(0, share), pl.ds(share, share - early)]
    copies = [
        pltpu.make_async_copy(held.at[:, place], out.at[:, place], sent.at[a]) for a, place in enumerate(places)
    ]
    held[:, places[0], :] = mix_grad[...].T.reshape(blocks, share, rows)
    copies[0].start()
    held[:, places[1], :] = product[...].T.reshape(blocks, share, rows)[:, early:]
    copies[1].start()
    for copy in copies:
        copy.wait()


def chunk(sizes, count, field, at):
    return pl.ds(count * sum(sizes[:field]) + at * sizes[field], sizes[field])


def split_kernel(*refs, near_count, sizes):
    fields, outs, turned = refs[: len(sizes)], refs[len(sizes) : -1], refs[-1]
    share = turned.shape[0] // (near_count * len(outs))
    me = lax.axis_index("ctx") if near_count > 1 else 0
    for k, field in enumerate(fields):
        turned[...] = field[...].T
        for far, out in enumerate(outs):
            for near in range(near_count):
                start = (me ^ (far * near_count + near)) * share
                start = start if near_count == 1 else pl.multiple_of(start, share)
                out[chunk(sizes, near_count, k, near), :] = turned[pl.ds(start, sizes[k]), :]


def gather_blocks(outs, sizes, far_parts, near_parts, me):
    far_count, near_count = len(far_parts), len(near_parts) + 1
    for far, part in enumerate(far_parts):
        for near in range(near_count):
            source = me ^ (far * near_count + near)
            for k, size in enumerate(sizes):
                if near:
                    rows = near_parts[near - 1][chunk(sizes, far_count, k, far), :]
                else:
                    rows = part[chunk(sizes, near_count, k, 0), :]
                outs[k][source, :size, :] = rows
            if len(outs) > len(sizes):
                extra = outs[len(sizes)].shape[1]
                if near:
                    rows = near_parts[near - 1][pl.ds(far_count * sum(sizes) + far * extra, extra), :]
                else:
                    rows = part[pl.ds(near_count * sum(sizes), extra), :]
                outs[len(sizes)][source] = rows


def spectra_kernel(taps, skip, matrices, twists, gates, *rest, near_count, first_early, early, grad_scale):
    blocks, rows = gates.shape[0], gates.shape[2]
    channels = (gates.shape[1] + first_early) // 2
    far_count = blocks // near_count
    far_parts, rest = rest[:far_count], rest[far_count:]
    near_parts, rest = rest[: near_count - 1], rest[near_count - 1 :]
    products, *outs, spectra, results, direct, lags, back, filters, factors = rest
    me = lax.axis_index("ctx") if near_count > 1 else 0
    if first_early:
        gather_blocks((filters, factors), (channels, first_early), far_parts, near_parts, me)
    else:
        gather_blocks((filters,), (channels,), far_parts, near_parts, me)
    factors[:, first_early:, :] = gates[:, channels:, :]
    row = lax.broadcasted_iota(jnp.int32, taps.shape, 0)
    direct[...] = (taps[...] + jnp.where(row == 0, skip[...], 0.0)).T
    own = 0 if direct.shape[0] == channels else pl.multiple_of(lax.axis_index("ctx") * channels, channels)
    for a in range(3):
        for low in range(0, channels, 8):
            part = pl.ds(low, 8)
            if a == 1:
                values = [filters[j, part, :] for j in range(blocks)]
                values[0] = values[0] + direct[pl.ds(own + low, 8), :]
            else:
                values = [(factors, None, gates)[a][j, part, :] for j in range(blocks)]
            bins = padded_bins(values)
            for p in range(blocks + 1):
                real, imag = bins[p]
                cosine, sine = twists[p, 0:1, :], twists[p, 1:2, :]
                place = pl.ds(p * channels + low, 8)
                if imag is None:
                    spectra[a, place, :rows] = real * cosine
                    spectra[a, place, rows:] = real * sine
                else:
                    spectra[a, place, :rows] = real * cosine - imag * sine
                    spectra[a, place, rows:] = real * sine + imag * cosine
    product, filt, mix_grad = [multiply(spectra[a], matrices[0], matrices[1]) for a in range(3)]
    pr, pi = product[:, :rows], product[:, rows:]
    fr, fi = filt[:, :rows], filt[:, rows:]
    gr, gi = mix_grad[:, :rows], mix_grad[:, rows:]
    spectra[0, :, :rows] = pr * gr + pi * gi
    spectra[0, :, rows:] = pr * gi - pi * gr
    products[0, :, :rows] = fr * pr - fi * pi
    products[0, :, rows:] = fr * pi + fi * pr
    products[1, :, :rows] = fr * gr + fi * gi
    products[1, :, rows:] = fr * gi - fi * gr
    for low, values in blocks_back(spectra.at[0], results, matrices, twists, channels, 0, channels):
        for j, value in enumerate(values):
            lags[j, pl.ds(low, 8), :] = value * grad_scale
    for low, values in blocks_back(products.at[1], results, matrices, twists, channels, 0, early):
        for j, value in enumerate(values):
            back[j, pl.ds(low, 8), :] = value
    sizes = (channels, early) if early else (channels,)
    for far, out in enumerate(outs):
        for near in range(near_count):
            target = me ^ (far * near_count + near)
            for k, size in enumerate(sizes):
                out[chunk(sizes, near_count, k, near), :] = (lags, back)[k][target]
        out[pl.ds(near_count * sum(sizes), channels), :] = lags[0]


def blocks_back(spectrum, result, matrices, twists, channels, first, last):
    blocks, rows = twists.shape[0] - 1, twists.shape[2]
    count = last - first
    if count == 0:
        return
    height = (blocks + 1) * count
    wanted = spectrum[...].reshape(blocks + 1, channels, 2 * rows)[:, first:last].reshape(height, 2 * rows)
    result[:height, :] = multiply(wanted, matrices[2], matrices[3])
    for low in range(0, count, 8):
        bins = {}
        for p in range(blocks + 1):
            cosine, sine = twists[p, 2:3, :], twists[p, 3:4, :]
            place = pl.ds(p * count + low, 8)
            real, imag = result[place, :rows], result[place, rows:]
            new_real = real * cosine - imag * sine
            bins[p] = (new_real, None if p % blocks == 0 else real * sine + imag * cosine)
        yield low, padded_bins_back(bins, blocks)


def mix_kernel(matrices, twists, products, out, results, held, sent, *, channels, early):
    places = [pl.ds(0, channels), pl.ds(channels, channels - early)]
    copies = [
        pltpu.make_async_copy(held.at[:, place], out.at[:, place], sent.at[a]) for a, place in enumerate(places)
    ]
    for a, first in enumerate((0, early)):
        for low, values in blocks_back(products.at[a], results.at[a], matrices, twists, channels, first, channels):
            for j, value in enumerate(values):
                held[j, pl.ds(a * channels + low, 8), :] = value
        copies[a].start()
    for copy in copies:
        copy.wait()


def relay_kernel(*refs, far_count, sizes, extra):
    parts = (refs[0], *refs[1:far_count][::-1])
    outs = refs[far_count:]
    near_count = len(outs) + 1
    for near, out in enumerate(outs, 1):
        for far, part in enumerate(parts):
            for k in range(len(sizes)):
                out[chunk(sizes, far_count, k, far), :] = part[chunk(sizes, near_count, k, near), :]
            if extra:
                place = pl.ds(far_count * sum(sizes) + far * extra, extra)
                out[place, :] = part[pl.ds(near_count * sum(sizes), extra), :]


def unpack_kernel(query, key, value, grad, parts, *rest, far_count, near_count, early):
    far_parts, rest = rest[:far_count], rest[far_count:]
    near_parts, rest = rest[: near_count - 1], rest[near_count - 1 :]
    outs, held, sent, lags, back, first_lags = rest[:7], rest[7:14], rest[14], rest[15], rest[16], rest[17]
    rows, channels = query.shape
    blocks, share, _ = lags.shape
    copies = [
        pltpu.make_async_copy(source, target, sent.at[i])
        for i, (source, target) in enumerate(zip(held, outs))
    ]

    def whole(array):
        return array.reshape(channels, rows).T

    def put(i, array):
        held[i][...] = array
        copies[i].start()

    mixer = whole(parts[:, :share])
    put(0, query[...].astype(jnp.float32) * mixer)
    put(1, grad[...].astype(jnp.float32) * mixer)
    me = lax.axis_index("ctx") if near_count > 1 else 0
    if early:
        gather_blocks((lags, back, first_lags), (share, early), far_parts, near_parts, me)
    else:
        gather_blocks((lags, first_lags), (share,), far_parts, near_parts, me)
    back[:, early:, :] = parts[:, share:]
    product_grad = whole(back[...])
    put(2, product_grad * value[...].astype(jnp.float32))
    put(3, product_grad * key[...].astype(jnp.float32))
    put(4, whole(lags[...]))
    first = whole(first_lags[...])
    put(5, first)
    put(6, first[0:1, :])
    for copy in copies:
        copy.wait()


def call(kernel, name, out_shape, places, scratch=(), flops=0, size=0, limit=VMEM_LIMIT, to=pltpu.VMEM):
    return pl.pallas_call(
        kernel,
        name=name,
        out_shape=out_shape,
        in_specs=[pl.BlockSpec(memory_space=place) for place in places],
        out_specs=jax.tree.map(lambda _: pl.BlockSpec(memory_space=to), out_shape),
        scratch_shapes=list(scratch),
        compiler_params=pltpu.CompilerParams(vmem_limit_bytes=limit),
        cost_estimate=pl.CostEstimate(flops=flops, bytes_accessed=size, transcendentals=0),
    )


def exchange(value, axis, distance):
    return lax.ppermute(value, axis, [(i, i ^ distance) for i in range(lax.axis_size(axis))])


def send_parts(parts, axis, near_count, sizes, extra=0):
    far_parts, far_count = list(parts), len(parts)
    for far in range(far_count - 1, 0, -1):
        far_parts[far] = exchange(parts[far], axis, far * near_count)
    payload = jax.ShapeDtypeStruct((far_count * (sum(sizes) + extra), parts[0].shape[1]), jnp.float32)
    relay = call(
        functools.partial(relay_kernel, far_count=far_count, sizes=sizes, extra=extra),
        "relay",
        (payload,) * (near_count - 1),
        (pltpu.VMEM,) * far_count,
        flops=RELAY_WEIGHT,
    )
    near_parts = relay(far_parts[0], *far_parts[:0:-1])
    return far_parts, [exchange(part, axis, near) for near, part in enumerate(near_parts, 1)]


def body(query, key, value, implicit_filter, explicit_taps, skip_gain, out_grad):
    rows, channels = query.shape
    blocks = lax.axis_size("ctx")
    share = channels // blocks
    padded = -(-share // 8) * 8
    f32 = jnp.float32
    shape = functools.partial(jax.ShapeDtypeStruct, dtype=f32)
    grad_scale = 1.0 / math.sqrt(blocks * rows)
    taps, skip = explicit_taps, skip_gain.reshape(1, channels)

    near_count = 1 << (blocks.bit_length() - 1) // 2 if share == padded else 1
    far_count = blocks // near_count
    product = key.astype(f32) * value.astype(f32)
    mix_grad = out_grad.astype(f32) * query.astype(f32)
    first_early = share // 32 * 8 if near_count > 1 else 0
    sizes = (share, first_early) if first_early else (share,)
    split_parts = call(
        functools.partial(split_kernel, near_count=near_count, sizes=sizes),
        "split",
        (shape((near_count * sum(sizes), rows)),) * far_count,
        (pltpu.VMEM,) * len(sizes),
        scratch=(pltpu.VMEM((channels, rows), f32),),
        size=16 * rows * channels,
    )(*(implicit_filter, product)[: len(sizes)])
    both = shape((blocks, 2 * share - first_early, rows))
    packed = call(
        functools.partial(pack_kernel, early=first_early),
        "pack",
        both,
        (pltpu.VMEM,) * 2,
        scratch=(pltpu.VMEM(both.shape, f32), pltpu.SemaphoreType.DMA((2,))),
        to=pltpu.HBM,
        size=16 * rows * channels,
    )(product, mix_grad)
    if near_count > 1:
        far_parts, near_parts = send_parts(split_parts, "ctx", near_count, sizes)
        gates = lax.all_to_all(packed, "ctx", 0, 0, tiled=True)
    else:
        together = jnp.concatenate([packed, jnp.stack(split_parts)], axis=1).reshape(blocks, 3, share, rows)
        together = lax.all_to_all(together, "ctx", 0, 0, tiled=True)
        together = jnp.pad(together, ((0, 0), (0, 0), (0, padded - share), (0, 0)))
        gates, near_parts = together[:, :2].reshape(blocks, 2 * padded, rows), []
        far_parts = list(together[:, 2])
        own = lax.axis_index("ctx") * share
        taps, skip = [
            jnp.pad(lax.dynamic_slice_in_dim(each, own, share, 1), ((0, 0), (0, padded - share)))
            for each in (taps, skip)
        ]
    matrices, twists = tables(blocks, rows)
    height = (blocks + 1) * padded
    matrices, twists = jnp.asarray(matrices), jnp.asarray(twists)
    early = padded // 32 * 8 if near_count > 1 else 0
    block = pltpu.VMEM((blocks, padded, rows), f32)
    products, *split_parts = call(
        functools.partial(
            spectra_kernel, near_count=near_count, first_early=first_early, early=early, grad_scale=grad_scale
        ),
        "spectra",
        (shape((2, height, 2 * rows)),) + (shape((near_count * (padded + early) + padded, rows)),) * far_count,
        (pltpu.VMEM,) * (4 + far_count + near_count),
        scratch=(
            pltpu.VMEM((3, height, 2 * rows), f32),
            pltpu.VMEM((height, 2 * rows), f32),
            pltpu.VMEM(taps.shape[::-1], f32),
            block,
            pltpu.VMEM((blocks, max(early, 8), rows), f32),
            block,
            block,
        ),
        flops=27 * height * (2 * rows) ** 2,
        size=24 * blocks * padded * rows,
    )(taps, skip, matrices, twists, gates, *far_parts, *near_parts)
    if near_count > 1:
        sizes = (share, early) if early else (share,)
        far_parts, near_parts = send_parts(split_parts, "ctx", near_count, sizes, share)
    late = shape((blocks, 2 * padded - early, rows))
    results = call(
        functools.partial(mix_kernel, channels=padded, early=early),
        "mix",
        late,
        (pltpu.VMEM,) * 3,
        scratch=(pltpu.VMEM((2, height, 2 * rows), f32), pltpu.VMEM(late.shape, f32), pltpu.SemaphoreType.DMA((2,))),
        to=pltpu.HBM,
        flops=9 * height * (2 * rows) ** 2,
        size=24 * blocks * padded * rows,
    )(matrices, twists, products)
    if near_count > 1:
        parts = lax.all_to_all(results, "ctx", 0, 0, tiled=True)
    else:
        together = jnp.concatenate([results, jnp.stack(split_parts)], axis=1).reshape(blocks, 4, padded, rows)
        together = lax.all_to_all(together[:, :, :share], "ctx", 0, 0, tiled=True).reshape(blocks, 4 * share, rows)
        parts, far_parts, near_parts = together[:, : 2 * share], list(together[:, 2 * share :]), []
    full, one = shape((rows, channels)), shape((1, channels))
    block = pltpu.VMEM((blocks, share, rows), f32)
    outs = call(
        functools.partial(unpack_kernel, far_count=far_count, near_count=near_count, early=early),
        "unpack",
        (full,) * 6 + (one,),
        (pltpu.VMEM,) * (4 + far_count + near_count),
        scratch=tuple(pltpu.VMEM(out.shape, f32) for out in (full,) * 6 + (one,))
        + (pltpu.SemaphoreType.DMA((7,)), block, block, block),
        to=pltpu.HBM,
        size=48 * rows * channels,
    )(query, key, value, out_grad, parts, *far_parts, *near_parts)
    return (*outs[:6], outs[6].reshape(channels))


def solution(mesh):
    in_specs = (
        P("ctx", "ch"),
        P("ctx", "ch"),
        P("ctx", "ch"),
        P("ctx", "ch"),
        P(None, "ch"),
        P("ch"),
        P("ctx", "ch"),
    )
    out_specs = (
        P("ctx", "ch"),
        P("ctx", "ch"),
        P("ctx", "ch"),
        P("ctx", "ch"),
        P("ctx", "ch"),
        P(None, "ch"),
        P("ch"),
    )
    return jax.shard_map(body, mesh=mesh, in_specs=in_specs, out_specs=out_specs, check_vma=False)
```

```python
import functools
import math

import jax
import jax.numpy as jnp
import numpy as np
from jax import lax
from jax.experimental import pallas as pl
from jax.experimental.pallas import tpu as pltpu
from jax.sharding import PartitionSpec as P

VMEM_LIMIT = 48 * 1024 * 1024
RELAY_WEIGHT = 10**11


def turn(value, turns):
    turns = turns % 1.0
    real, imag = value
    if turns == 0.0:
        return value
    if turns == 0.5:
        return (-real, -imag)
    if turns == 0.25:
        return (-imag, real)
    if turns == 0.75:
        return (imag, -real)
    cosine, sine = math.cos(2 * math.pi * turns), math.sin(2 * math.pi * turns)
    if abs(abs(cosine) - abs(sine)) < 1e-12:
        scale = abs(cosine)
        one, two = math.copysign(1.0, cosine), math.copysign(1.0, sine)
        new_real = (real if one > 0 else -real) - (imag if two > 0 else -imag)
        new_imag = (real if two > 0 else -real) + (imag if one > 0 else -imag)
        return (new_real * scale, new_imag * scale)
    return (real * cosine - imag * sine, real * sine + imag * cosine)


def plus(a, b):
    return (a[0] + b[0], a[1] + b[1])


def minus(a, b):
    return (a[0] - b[0], a[1] - b[1])


def complex_transform(values, sign):
    count = len(values)
    if count == 1:
        return values
    even = complex_transform(values[0::2], sign)
    odd = complex_transform(values[1::2], sign)
    odd = [turn(odd[k], sign * k / count) for k in range(count // 2)]
    return [plus(e, o) for e, o in zip(even, odd)] + [minus(e, o) for e, o in zip(even, odd)]


def odd_bins(values):
    length = len(values)
    half = length // 2
    turned = [turn((values[j], -values[j + half]), -j / (2 * length)) for j in range(half)]
    bins = {}
    for m, (real, imag) in enumerate(complex_transform(turned, -1)):
        p = 4 * m + 1
        if p < length:
            bins[p] = (real, imag)
        else:
            bins[2 * length - p] = (real, -imag)
    return bins


def real_bins(values):
    length = len(values)
    if length == 2:
        return {0: (values[0] + values[1], None), 1: (values[0] - values[1], None)}
    half = length // 2
    bins = {}
    for s, value in real_bins([values[j] + values[j + half] for j in range(half)]).items():
        bins[2 * s] = value
    bins.update(odd_bins([values[j] - values[j + half] for j in range(half)]))
    return bins


def padded_bins(values):
    bins = {2 * s: value for s, value in real_bins(values).items()}
    bins.update(odd_bins(values))
    return bins


def odd_bins_back(bins, length):
    half = length // 2
    spectrum = []
    for m in range(half):
        p = 4 * m + 1
        if p < length:
            spectrum.append(bins[p])
        else:
            real, imag = bins[2 * length - p]
            spectrum.append((real, -imag))
    values = complex_transform(spectrum, 1)
    values = [turn(value, j / (2 * length)) for j, value in enumerate(values)]
    return [value[0] for value in values] + [-value[1] for value in values]


def real_bins_back(bins, length):
    if length == 2:
        return [bins[0][0] + bins[1][0], bins[0][0] - bins[1][0]]
    half = length // 2
    even = real_bins_back({s: bins[2 * s] for s in range(half // 2 + 1)}, half)
    odd = odd_bins_back(bins, half)
    return [e + o for e, o in zip(even, odd)] + [e - o for e, o in zip(even, odd)]


def padded_bins_back(bins, length):
    even = real_bins_back({s: bins[2 * s] for s in range(length // 2 + 1)}, length)
    odd = odd_bins_back(bins, length)
    return [e + o for e, o in zip(even, odd)]


def tables(blocks, rows):
    extent = 2 * blocks * rows
    positions = np.arange(rows)
    angle = 2 * np.pi * (np.outer(positions, positions) % rows) / rows
    cosine, sine = np.cos(angle), np.sin(angle)
    forward = np.block([[cosine, -sine], [sine, cosine]])
    matrices = []
    for matrix in (forward, forward.T):
        high = matrix.astype(jnp.bfloat16)
        low = (matrix - high.astype(np.float64)).astype(jnp.bfloat16)
        matrices += [high, low]
    phase = 2 * np.pi * np.outer(np.arange(blocks + 1), positions) / extent
    weight = np.where(np.arange(blocks + 1) % blocks == 0, 1.0, 2.0)[:, None] / extent
    twists = np.stack(
        [np.cos(phase), -np.sin(phase), weight * np.cos(phase), weight * np.sin(phase)], 1
    )
    return np.stack(matrices), twists.astype(np.float32)


def multiply(values, high, low):
    values_high = values.astype(jnp.bfloat16)
    values_low = (values - values_high.astype(jnp.float32)).astype(jnp.bfloat16)
    dot = functools.partial(jnp.dot, preferred_element_type=jnp.float32)
    return dot(values_high, high) + (dot(values_low, high) + dot(values_high, low))


def pack_kernel(product, mix_grad, out, held, sent, *, early):
    blocks, _, rows = out.shape
    share = product.shape[1] // blocks
    places = [pl.ds(0, share), pl.ds(share, share - early)]
    copies = [
        pltpu.make_async_copy(held.at[:, place], out.at[:, place], sent.at[a]) for a, place in enumerate(places)
    ]
    held[:, places[0], :] = mix_grad[...].T.reshape(blocks, share, rows)
    copies[0].start()
    held[:, places[1], :] = product[...].T.reshape(blocks, share, rows)[:, early:]
    copies[1].start()
    for copy in copies:
        copy.wait()


def chunk(sizes, count, field, at):
    return pl.ds(count * sum(sizes[:field]) + at * sizes[field], sizes[field])


def split_kernel(*refs, near_count, sizes):
    fields, outs, turned = refs[: len(sizes)], refs[len(sizes) : -1], refs[-1]
    share = turned.shape[0] // (near_count * len(outs))
    me = lax.axis_index("ctx") if near_count > 1 else 0
    for k, field in enumerate(fields):
        turned[...] = field[...].T
        for far, out in enumerate(outs):
            for near in range(near_count):
                start = (me ^ (far * near_count + near)) * share
                start = start if near_count == 1 else pl.multiple_of(start, share)
                out[chunk(sizes, near_count, k, near), :] = turned[pl.ds(start, sizes[k]), :]


def gather_blocks(outs, sizes, far_parts, near_parts, me):
    far_count, near_count = len(far_parts), len(near_parts) + 1
    for far, part in enumerate(far_parts):
        for near in range(near_count):
            source = me ^ (far * near_count + near)
            for k, size in enumerate(sizes):
                if near:
                    rows = near_parts[near - 1][chunk(sizes, far_count, k, far), :]
                else:
                    rows = part[chunk(sizes, near_count, k, 0), :]
                outs[k][source, :size, :] = rows
            if len(outs) > len(sizes):
                extra = outs[len(sizes)].shape[1]
                if near:
                    rows = near_parts[near - 1][pl.ds(far_count * sum(sizes) + far * extra, extra), :]
                else:
                    rows = part[pl.ds(near_count * sum(sizes), extra), :]
                outs[len(sizes)][source] = rows


def spectra_kernel(taps, skip, matrices, twists, gates, *rest, near_count, first_early, early, grad_scale):
    blocks, rows = gates.shape[0], gates.shape[2]
    channels = (gates.shape[1] + first_early) // 2
    far_count = blocks // near_count
    far_parts, rest = rest[:far_count], rest[far_count:]
    near_parts, rest = rest[: near_count - 1], rest[near_count - 1 :]
    products, *outs, spectra, results, direct, lags, back, filters, factors = rest
    me = lax.axis_index("ctx") if near_count > 1 else 0
    if first_early:
        gather_blocks((filters, factors), (channels, first_early), far_parts, near_parts, me)
    else:
        gather_blocks((filters,), (channels,), far_parts, near_parts, me)
    factors[:, first_early:, :] = gates[:, channels:, :]
    row = lax.broadcasted_iota(jnp.int32, taps.shape, 0)
    direct[...] = (taps[...] + jnp.where(row == 0, skip[...], 0.0)).T
    own = 0 if direct.shape[0] == channels else pl.multiple_of(lax.axis_index("ctx") * channels, channels)
    for a in range(3):
        for low in range(0, channels, 8):
            part = pl.ds(low, 8)
            if a == 1:
                values = [filters[j, part, :] for j in range(blocks)]
                values[0] = values[0] + direct[pl.ds(own + low, 8), :]
            else:
                values = [(factors, None, gates)[a][j, part, :] for j in range(blocks)]
            bins = padded_bins(values)
            for p in range(blocks + 1):
                real, imag = bins[p]
                cosine, sine = twists[p, 0:1, :], twists[p, 1:2, :]
                place = pl.ds(p * channels + low, 8)
                if imag is None:
                    spectra[a, place, :rows] = real * cosine
                    spectra[a, place, rows:] = real * sine
                else:
                    spectra[a, place, :rows] = real * cosine - imag * sine
                    spectra[a, place, rows:] = real * sine + imag * cosine
    product, filt, mix_grad = [multiply(spectra[a], matrices[0], matrices[1]) for a in range(3)]
    pr, pi = product[:, :rows], product[:, rows:]
    fr, fi = filt[:, :rows], filt[:, rows:]
    gr, gi = mix_grad[:, :rows], mix_grad[:, rows:]
    spectra[0, :, :rows] = pr * gr + pi * gi
    spectra[0, :, rows:] = pr * gi - pi * gr
    products[0, :, :rows] = fr * pr - fi * pi
    products[0, :, rows:] = fr * pi + fi * pr
    products[1, :, :rows] = fr * gr + fi * gi
    products[1, :, rows:] = fr * gi - fi * gr
    for low, values in blocks_back(spectra.at[0], results, matrices, twists, channels, 0, channels):
        for j, value in enumerate(values):
            lags[j, pl.ds(low, 8), :] = value * grad_scale
    for low, values in blocks_back(products.at[1], results, matrices, twists, channels, 0, early):
        for j, value in enumerate(values):
            back[j, pl.ds(low, 8), :] = value
    sizes = (channels, early) if early else (channels,)
    for far, out in enumerate(outs):
        for near in range(near_count):
            target = me ^ (far * near_count + near)
            for k, size in enumerate(sizes):
                out[chunk(sizes, near_count, k, near), :] = (lags, back)[k][target]
        out[pl.ds(near_count * sum(sizes), channels), :] = lags[0]


def blocks_back(spectrum, result, matrices, twists, channels, first, last):
    blocks, rows = twists.shape[0] - 1, twists.shape[2]
    count = last - first
    if count == 0:
        return
    height = (blocks + 1) * count
    wanted = spectrum[...].reshape(blocks + 1, channels, 2 * rows)[:, first:last].reshape(height, 2 * rows)
    result[:height, :] = multiply(wanted, matrices[2], matrices[3])
    for low in range(0, count, 8):
        bins = {}
        for p in range(blocks + 1):
            cosine, sine = twists[p, 2:3, :], twists[p, 3:4, :]
            place = pl.ds(p * count + low, 8)
            real, imag = result[place, :rows], result[place, rows:]
            new_real = real * cosine - imag * sine
            bins[p] = (new_real, None if p % blocks == 0 else real * sine + imag * cosine)
        yield low, padded_bins_back(bins, blocks)


def mix_kernel(matrices, twists, products, out, results, held, sent, *, channels, early):
    places = [pl.ds(0, channels), pl.ds(channels, channels - early)]
    copies = [
        pltpu.make_async_copy(held.at[:, place], out.at[:, place], sent.at[a]) for a, place in enumerate(places)
    ]
    for a, first in enumerate((0, early)):
        for low, values in blocks_back(products.at[a], results.at[a], matrices, twists, channels, first, channels):
            for j, value in enumerate(values):
                held[j, pl.ds(a * channels + low, 8), :] = value
        copies[a].start()
    for copy in copies:
        copy.wait()


def relay_kernel(*refs, far_count, sizes, extra):
    parts = (refs[0], *refs[1:far_count][::-1])
    outs = refs[far_count:]
    near_count = len(outs) + 1
    for near, out in enumerate(outs, 1):
        for far, part in enumerate(parts):
            for k in range(len(sizes)):
                out[chunk(sizes, far_count, k, far), :] = part[chunk(sizes, near_count, k, near), :]
            if extra:
                place = pl.ds(far_count * sum(sizes) + far * extra, extra)
                out[place, :] = part[pl.ds(near_count * sum(sizes), extra), :]


def unpack_kernel(query, key, value, grad, parts, *rest, far_count, near_count, early):
    far_parts, rest = rest[:far_count], rest[far_count:]
    near_parts, rest = rest[: near_count - 1], rest[near_count - 1 :]
    outs, held, sent, lags, back, first_lags = rest[:7], rest[7:14], rest[14], rest[15], rest[16], rest[17]
    rows, channels = query.shape
    blocks, share, _ = lags.shape
    copies = [
        pltpu.make_async_copy(source, target, sent.at[i])
        for i, (source, target) in enumerate(zip(held, outs))
    ]

    def whole(array):
        return array.reshape(channels, rows).T

    def put(i, array):
        held[i][...] = array
        copies[i].start()

    mixer = whole(parts[:, :share])
    put(0, query[...].astype(jnp.float32) * mixer)
    put(1, grad[...].astype(jnp.float32) * mixer)
    me = lax.axis_index("ctx") if near_count > 1 else 0
    if early:
        gather_blocks((lags, back, first_lags), (share, early), far_parts, near_parts, me)
    else:
        gather_blocks((lags, first_lags), (share,), far_parts, near_parts, me)
    back[:, early:, :] = parts[:, share:]
    product_grad = whole(back[...])
    put(2, product_grad * value[...].astype(jnp.float32))
    put(3, product_grad * key[...].astype(jnp.float32))
    put(4, whole(lags[...]))
    first = whole(first_lags[...])
    put(5, first)
    put(6, first[0:1, :])
    for copy in copies:
        copy.wait()


def call(kernel, name, out_shape, places, scratch=(), flops=0, size=0, limit=VMEM_LIMIT, to=pltpu.VMEM):
    return pl.pallas_call(
        kernel,
        name=name,
        out_shape=out_shape,
        in_specs=[pl.BlockSpec(memory_space=place) for place in places],
        out_specs=jax.tree.map(lambda _: pl.BlockSpec(memory_space=to), out_shape),
        scratch_shapes=list(scratch),
        compiler_params=pltpu.CompilerParams(vmem_limit_bytes=limit),
        cost_estimate=pl.CostEstimate(flops=flops, bytes_accessed=size, transcendentals=0),
    )


def exchange(value, axis, distance):
    return lax.ppermute(value, axis, [(i, i ^ distance) for i in range(lax.axis_size(axis))])


def send_parts(parts, axis, near_count, sizes, extra=0):
    far_parts, far_count = list(parts), len(parts)
    for far in range(far_count - 1, 0, -1):
        far_parts[far] = exchange(parts[far], axis, far * near_count)
    payload = jax.ShapeDtypeStruct((far_count * (sum(sizes) + extra), parts[0].shape[1]), jnp.float32)
    relay = call(
        functools.partial(relay_kernel, far_count=far_count, sizes=sizes, extra=extra),
        "relay",
        (payload,) * (near_count - 1),
        (pltpu.VMEM,) * far_count,
        flops=RELAY_WEIGHT,
    )
    near_parts = relay(far_parts[0], *far_parts[:0:-1])
    return far_parts, [exchange(part, axis, near) for near, part in enumerate(near_parts, 1)]


def body(query, key, value, implicit_filter, explicit_taps, skip_gain, out_grad):
    rows, channels = query.shape
    blocks = lax.axis_size("ctx")
    share = channels // blocks
    padded = -(-share // 8) * 8
    f32 = jnp.float32
    shape = functools.partial(jax.ShapeDtypeStruct, dtype=f32)
    grad_scale = 1.0 / math.sqrt(blocks * rows)
    taps, skip = explicit_taps, skip_gain.reshape(1, channels)

    near_count = 1 << (blocks.bit_length() - 1) // 2 if share == padded else 1
    far_count = blocks // near_count
    product = key.astype(f32) * value.astype(f32)
    mix_grad = out_grad.astype(f32) * query.astype(f32)
    first_early = share // 32 * 16 if near_count > 1 else 0
    sizes = (share, first_early) if first_early else (share,)
    split_parts = call(
        functools.partial(split_kernel, near_count=near_count, sizes=sizes),
        "split",
        (shape((near_count * sum(sizes), rows)),) * far_count,
        (pltpu.VMEM,) * len(sizes),
        scratch=(pltpu.VMEM((channels, rows), f32),),
        size=16 * rows * channels,
    )(*(implicit_filter, product)[: len(sizes)])
    both = shape((blocks, 2 * share - first_early, rows))
    packed = call(
        functools.partial(pack_kernel, early=first_early),
        "pack",
        both,
        (pltpu.VMEM,) * 2,
        scratch=(pltpu.VMEM(both.shape, f32), pltpu.SemaphoreType.DMA((2,))),
        to=pltpu.HBM,
        size=16 * rows * channels,
    )(product, mix_grad)
    if near_count > 1:
        far_parts, near_parts = send_parts(split_parts, "ctx", near_count, sizes)
        gates = lax.all_to_all(packed, "ctx", 0, 0, tiled=True)
    else:
        together = jnp.concatenate([packed, jnp.stack(split_parts)], axis=1).reshape(blocks, 3, share, rows)
        together = lax.all_to_all(together, "ctx", 0, 0, tiled=True)
        together = jnp.pad(together, ((0, 0), (0, 0), (0, padded - share), (0, 0)))
        gates, near_parts = together[:, :2].reshape(blocks, 2 * padded, rows), []
        far_parts = list(together[:, 2])
        own = lax.axis_index("ctx") * share
        taps, skip = [
            jnp.pad(lax.dynamic_slice_in_dim(each, own, share, 1), ((0, 0), (0, padded - share)))
            for each in (taps, skip)
        ]
    matrices, twists = tables(blocks, rows)
    height = (blocks + 1) * padded
    matrices, twists = jnp.asarray(matrices), jnp.asarray(twists)
    early = padded // 32 * 8 if near_count > 1 else 0
    block = pltpu.VMEM((blocks, padded, rows), f32)
    products, *split_parts = call(
        functools.partial(
            spectra_kernel, near_count=near_count, first_early=first_early, early=early, grad_scale=grad_scale
        ),
        "spectra",
        (shape((2, height, 2 * rows)),) + (shape((near_count * (padded + early) + padded, rows)),) * far_count,
        (pltpu.VMEM,) * (4 + far_count + near_count),
        scratch=(
            pltpu.VMEM((3, height, 2 * rows), f32),
            pltpu.VMEM((height, 2 * rows), f32),
            pltpu.VMEM(taps.shape[::-1], f32),
            block,
            pltpu.VMEM((blocks, max(early, 8), rows), f32),
            block,
            block,
        ),
        flops=27 * height * (2 * rows) ** 2,
        size=24 * blocks * padded * rows,
    )(taps, skip, matrices, twists, gates, *far_parts, *near_parts)
    if near_count > 1:
        sizes = (share, early) if early else (share,)
        far_parts, near_parts = send_parts(split_parts, "ctx", near_count, sizes, share)
    late = shape((blocks, 2 * padded - early, rows))
    results = call(
        functools.partial(mix_kernel, channels=padded, early=early),
        "mix",
        late,
        (pltpu.VMEM,) * 3,
        scratch=(pltpu.VMEM((2, height, 2 * rows), f32), pltpu.VMEM(late.shape, f32), pltpu.SemaphoreType.DMA((2,))),
        to=pltpu.HBM,
        flops=9 * height * (2 * rows) ** 2,
        size=24 * blocks * padded * rows,
    )(matrices, twists, products)
    if near_count > 1:
        parts = lax.all_to_all(results, "ctx", 0, 0, tiled=True)
    else:
        together = jnp.concatenate([results, jnp.stack(split_parts)], axis=1).reshape(blocks, 4, padded, rows)
        together = lax.all_to_all(together[:, :, :share], "ctx", 0, 0, tiled=True).reshape(blocks, 4 * share, rows)
        parts, far_parts, near_parts = together[:, : 2 * share], list(together[:, 2 * share :]), []
    full, one = shape((rows, channels)), shape((1, channels))
    block = pltpu.VMEM((blocks, share, rows), f32)
    outs = call(
        functools.partial(unpack_kernel, far_count=far_count, near_count=near_count, early=early),
        "unpack",
        (full,) * 6 + (one,),
        (pltpu.VMEM,) * (4 + far_count + near_count),
        scratch=tuple(pltpu.VMEM(out.shape, f32) for out in (full,) * 6 + (one,))
        + (pltpu.SemaphoreType.DMA((7,)), block, block, block),
        to=pltpu.HBM,
        size=48 * rows * channels,
    )(query, key, value, out_grad, parts, *far_parts, *near_parts)
    return (*outs[:6], outs[6].reshape(channels))


def solution(mesh):
    in_specs = (
        P("ctx", "ch"),
        P("ctx", "ch"),
        P("ctx", "ch"),
        P("ctx", "ch"),
        P(None, "ch"),
        P("ch"),
        P("ctx", "ch"),
    )
    out_specs = (
        P("ctx", "ch"),
        P("ctx", "ch"),
        P("ctx", "ch"),
        P("ctx", "ch"),
        P("ctx", "ch"),
        P(None, "ch"),
        P("ch"),
    )
    return jax.shard_map(body, mesh=mesh, in_specs=in_specs, out_specs=out_specs, check_vma=False)
```

```python
import functools
import math

import jax
import jax.numpy as jnp
import numpy as np
from jax import lax
from jax.experimental import pallas as pl
from jax.experimental.pallas import tpu as pltpu
from jax.sharding import PartitionSpec as P

VMEM_LIMIT = 48 * 1024 * 1024
RELAY_WEIGHT = 10**11


def turn(value, turns):
    turns = turns % 1.0
    real, imag = value
    if turns == 0.0:
        return value
    if turns == 0.5:
        return (-real, -imag)
    if turns == 0.25:
        return (-imag, real)
    if turns == 0.75:
        return (imag, -real)
    cosine, sine = math.cos(2 * math.pi * turns), math.sin(2 * math.pi * turns)
    if abs(abs(cosine) - abs(sine)) < 1e-12:
        scale = abs(cosine)
        one, two = math.copysign(1.0, cosine), math.copysign(1.0, sine)
        new_real = (real if one > 0 else -real) - (imag if two > 0 else -imag)
        new_imag = (real if two > 0 else -real) + (imag if one > 0 else -imag)
        return (new_real * scale, new_imag * scale)
    return (real * cosine - imag * sine, real * sine + imag * cosine)


def plus(a, b):
    return (a[0] + b[0], a[1] + b[1])


def minus(a, b):
    return (a[0] - b[0], a[1] - b[1])


def complex_transform(values, sign):
    count = len(values)
    if count == 1:
        return values
    even = complex_transform(values[0::2], sign)
    odd = complex_transform(values[1::2], sign)
    odd = [turn(odd[k], sign * k / count) for k in range(count // 2)]
    return [plus(e, o) for e, o in zip(even, odd)] + [minus(e, o) for e, o in zip(even, odd)]


def odd_bins(values):
    length = len(values)
    half = length // 2
    turned = [turn((values[j], -values[j + half]), -j / (2 * length)) for j in range(half)]
    bins = {}
    for m, (real, imag) in enumerate(complex_transform(turned, -1)):
        p = 4 * m + 1
        if p < length:
            bins[p] = (real, imag)
        else:
            bins[2 * length - p] = (real, -imag)
    return bins


def real_bins(values):
    length = len(values)
    if length == 2:
        return {0: (values[0] + values[1], None), 1: (values[0] - values[1], None)}
    half = length // 2
    bins = {}
    for s, value in real_bins([values[j] + values[j + half] for j in range(half)]).items():
        bins[2 * s] = value
    bins.update(odd_bins([values[j] - values[j + half] for j in range(half)]))
    return bins


def padded_bins(values):
    bins = {2 * s: value for s, value in real_bins(values).items()}
    bins.update(odd_bins(values))
    return bins


def odd_bins_back(bins, length):
    half = length // 2
    spectrum = []
    for m in range(half):
        p = 4 * m + 1
        if p < length:
            spectrum.append(bins[p])
        else:
            real, imag = bins[2 * length - p]
            spectrum.append((real, -imag))
    values = complex_transform(spectrum, 1)
    values = [turn(value, j / (2 * length)) for j, value in enumerate(values)]
    return [value[0] for value in values] + [-value[1] for value in values]


def real_bins_back(bins, length):
    if length == 2:
        return [bins[0][0] + bins[1][0], bins[0][0] - bins[1][0]]
    half = length // 2
    even = real_bins_back({s: bins[2 * s] for s in range(half // 2 + 1)}, half)
    odd = odd_bins_back(bins, half)
    return [e + o for e, o in zip(even, odd)] + [e - o for e, o in zip(even, odd)]


def padded_bins_back(bins, length):
    even = real_bins_back({s: bins[2 * s] for s in range(length // 2 + 1)}, length)
    odd = odd_bins_back(bins, length)
    return [e + o for e, o in zip(even, odd)]


def tables(blocks, rows):
    extent = 2 * blocks * rows
    positions = np.arange(rows)
    angle = 2 * np.pi * (np.outer(positions, positions) % rows) / rows
    cosine, sine = np.cos(angle), np.sin(angle)
    forward = np.block([[cosine, -sine], [sine, cosine]])
    matrices = []
    for matrix in (forward, forward.T):
        high = matrix.astype(jnp.bfloat16)
        low = (matrix - high.astype(np.float64)).astype(jnp.bfloat16)
        matrices += [high, low]
    phase = 2 * np.pi * np.outer(np.arange(blocks + 1), positions) / extent
    weight = np.where(np.arange(blocks + 1) % blocks == 0, 1.0, 2.0)[:, None] / extent
    twists = np.stack(
        [np.cos(phase), -np.sin(phase), weight * np.cos(phase), weight * np.sin(phase)], 1
    )
    return np.stack(matrices), twists.astype(np.float32)


def multiply(values, high, low):
    values_high = values.astype(jnp.bfloat16)
    values_low = (values - values_high.astype(jnp.float32)).astype(jnp.bfloat16)
    dot = functools.partial(jnp.dot, preferred_element_type=jnp.float32)
    return dot(values_high, high) + (dot(values_low, high) + dot(values_high, low))


def pack_kernel(product, mix_grad, out, held, sent, *, early):
    blocks, _, rows = out.shape
    share = product.shape[1] // blocks
    places = [pl.ds(0, share), pl.ds(share, share - early)]
    copies = [
        pltpu.make_async_copy(held.at[:, place], out.at[:, place], sent.at[a]) for a, place in enumerate(places)
    ]
    held[:, places[0], :] = mix_grad[...].T.reshape(blocks, share, rows)
    copies[0].start()
    held[:, places[1], :] = product[...].T.reshape(blocks, share, rows)[:, early:]
    copies[1].start()
    for copy in copies:
        copy.wait()


def chunk(sizes, count, field, at):
    return pl.ds(count * sum(sizes[:field]) + at * sizes[field], sizes[field])


def split_kernel(*refs, near_count, sizes):
    fields, outs, turned = refs[: len(sizes)], refs[len(sizes) : -1], refs[-1]
    share = turned.shape[0] // (near_count * len(outs))
    me = lax.axis_index("ctx") if near_count > 1 else 0
    for k, field in enumerate(fields):
        turned[...] = field[...].T
        for far, out in enumerate(outs):
            for near in range(near_count):
                start = (me ^ (far * near_count + near)) * share
                start = start if near_count == 1 else pl.multiple_of(start, share)
                out[chunk(sizes, near_count, k, near), :] = turned[pl.ds(start, sizes[k]), :]


def gather_blocks(outs, sizes, far_parts, near_parts, me):
    far_count, near_count = len(far_parts), len(near_parts) + 1
    for far, part in enumerate(far_parts):
        for near in range(near_count):
            source = me ^ (far * near_count + near)
            for k, size in enumerate(sizes):
                if near:
                    rows = near_parts[near - 1][chunk(sizes, far_count, k, far), :]
                else:
                    rows = part[chunk(sizes, near_count, k, 0), :]
                outs[k][source, :size, :] = rows
            if len(outs) > len(sizes):
                extra = outs[len(sizes)].shape[1]
                if near:
                    rows = near_parts[near - 1][pl.ds(far_count * sum(sizes) + far * extra, extra), :]
                else:
                    rows = part[pl.ds(near_count * sum(sizes), extra), :]
                outs[len(sizes)][source] = rows


def spectra_kernel(taps, skip, matrices, twists, gates, *rest, near_count, first_early, early, grad_scale):
    blocks, rows = gates.shape[0], gates.shape[2]
    channels = (gates.shape[1] + first_early) // 2
    far_count = blocks // near_count
    far_parts, rest = rest[:far_count], rest[far_count:]
    near_parts, rest = rest[: near_count - 1], rest[near_count - 1 :]
    products, *outs, spectra, results, direct, lags, back, filters, factors = rest
    me = lax.axis_index("ctx") if near_count > 1 else 0
    if first_early:
        gather_blocks((filters, factors), (channels, first_early), far_parts, near_parts, me)
    else:
        gather_blocks((filters,), (channels,), far_parts, near_parts, me)
    factors[:, first_early:, :] = gates[:, channels:, :]
    row = lax.broadcasted_iota(jnp.int32, taps.shape, 0)
    direct[...] = (taps[...] + jnp.where(row == 0, skip[...], 0.0)).T
    own = 0 if direct.shape[0] == channels else pl.multiple_of(lax.axis_index("ctx") * channels, channels)
    for a in range(3):
        for low in range(0, channels, 8):
            part = pl.ds(low, 8)
            if a == 1:
                values = [filters[j, part, :] for j in range(blocks)]
                values[0] = values[0] + direct[pl.ds(own + low, 8), :]
            else:
                values = [(factors, None, gates)[a][j, part, :] for j in range(blocks)]
            bins = padded_bins(values)
            for p in range(blocks + 1):
                real, imag = bins[p]
                cosine, sine = twists[p, 0:1, :], twists[p, 1:2, :]
                place = pl.ds(p * channels + low, 8)
                if imag is None:
                    spectra[a, place, :rows] = real * cosine
                    spectra[a, place, rows:] = real * sine
                else:
                    spectra[a, place, :rows] = real * cosine - imag * sine
                    spectra[a, place, rows:] = real * sine + imag * cosine
    product, filt, mix_grad = [multiply(spectra[a], matrices[0], matrices[1]) for a in range(3)]
    pr, pi = product[:, :rows], product[:, rows:]
    fr, fi = filt[:, :rows], filt[:, rows:]
    gr, gi = mix_grad[:, :rows], mix_grad[:, rows:]
    spectra[0, :, :rows] = pr * gr + pi * gi
    spectra[0, :, rows:] = pr * gi - pi * gr
    products[0, :, :rows] = fr * pr - fi * pi
    products[0, :, rows:] = fr * pi + fi * pr
    products[1, :, :rows] = fr * gr + fi * gi
    products[1, :, rows:] = fr * gi - fi * gr
    for low, values in blocks_back(spectra.at[0], results, matrices, twists, channels, 0, channels):
        for j, value in enumerate(values):
            lags[j, pl.ds(low, 8), :] = value * grad_scale
    for low, values in blocks_back(products.at[1], results, matrices, twists, channels, 0, early):
        for j, value in enumerate(values):
            back[j, pl.ds(low, 8), :] = value
    sizes = (channels, early) if early else (channels,)
    for far, out in enumerate(outs):
        for near in range(near_count):
            target = me ^ (far * near_count + near)
            for k, size in enumerate(sizes):
                out[chunk(sizes, near_count, k, near), :] = (lags, back)[k][target]
        out[pl.ds(near_count * sum(sizes), channels), :] = lags[0]


def blocks_back(spectrum, result, matrices, twists, channels, first, last):
    blocks, rows = twists.shape[0] - 1, twists.shape[2]
    count = last - first
    if count == 0:
        return
    height = (blocks + 1) * count
    wanted = spectrum[...].reshape(blocks + 1, channels, 2 * rows)[:, first:last].reshape(height, 2 * rows)
    result[:height, :] = multiply(wanted, matrices[2], matrices[3])
    for low in range(0, count, 8):
        bins = {}
        for p in range(blocks + 1):
            cosine, sine = twists[p, 2:3, :], twists[p, 3:4, :]
            place = pl.ds(p * count + low, 8)
            real, imag = result[place, :rows], result[place, rows:]
            new_real = real * cosine - imag * sine
            bins[p] = (new_real, None if p % blocks == 0 else real * sine + imag * cosine)
        yield low, padded_bins_back(bins, blocks)


def mix_kernel(matrices, twists, products, out, results, held, sent, *, channels, early):
    places = [pl.ds(0, channels), pl.ds(channels, channels - early)]
    copies = [
        pltpu.make_async_copy(held.at[:, place], out.at[:, place], sent.at[a]) for a, place in enumerate(places)
    ]
    for a, first in enumerate((0, early)):
        for low, values in blocks_back(products.at[a], results.at[a], matrices, twists, channels, first, channels):
            for j, value in enumerate(values):
                held[j, pl.ds(a * channels + low, 8), :] = value
        copies[a].start()
    for copy in copies:
        copy.wait()


def relay_kernel(*refs, far_count, sizes, extra):
    parts = (refs[0], *refs[1:far_count][::-1])
    outs = refs[far_count:]
    near_count = len(outs) + 1
    for near, out in enumerate(outs, 1):
        for far, part in enumerate(parts):
            for k in range(len(sizes)):
                out[chunk(sizes, far_count, k, far), :] = part[chunk(sizes, near_count, k, near), :]
            if extra:
                place = pl.ds(far_count * sum(sizes) + far * extra, extra)
                out[place, :] = part[pl.ds(near_count * sum(sizes), extra), :]


def unpack_kernel(query, key, value, grad, parts, *rest, far_count, near_count, early):
    far_parts, rest = rest[:far_count], rest[far_count:]
    near_parts, rest = rest[: near_count - 1], rest[near_count - 1 :]
    outs, held, sent, lags, back, first_lags = rest[:7], rest[7:14], rest[14], rest[15], rest[16], rest[17]
    rows, channels = query.shape
    blocks, share, _ = lags.shape
    copies = [
        pltpu.make_async_copy(source, target, sent.at[i])
        for i, (source, target) in enumerate(zip(held, outs))
    ]

    def whole(array):
        return array.reshape(channels, rows).T

    def put(i, array):
        held[i][...] = array
        copies[i].start()

    mixer = whole(parts[:, :share])
    put(0, query[...].astype(jnp.float32) * mixer)
    put(1, grad[...].astype(jnp.float32) * mixer)
    me = lax.axis_index("ctx") if near_count > 1 else 0
    if early:
        gather_blocks((lags, back, first_lags), (share, early), far_parts, near_parts, me)
    else:
        gather_blocks((lags, first_lags), (share,), far_parts, near_parts, me)
    back[:, early:, :] = parts[:, share:]
    product_grad = whole(back[...])
    put(2, product_grad * value[...].astype(jnp.float32))
    put(3, product_grad * key[...].astype(jnp.float32))
    put(4, whole(lags[...]))
    first = whole(first_lags[...])
    put(5, first)
    put(6, first[0:1, :])
    for copy in copies:
        copy.wait()


def call(kernel, name, out_shape, places, scratch=(), flops=0, size=0, limit=VMEM_LIMIT, to=pltpu.VMEM):
    return pl.pallas_call(
        kernel,
        name=name,
        out_shape=out_shape,
        in_specs=[pl.BlockSpec(memory_space=place) for place in places],
        out_specs=jax.tree.map(lambda _: pl.BlockSpec(memory_space=to), out_shape),
        scratch_shapes=list(scratch),
        compiler_params=pltpu.CompilerParams(vmem_limit_bytes=limit),
        cost_estimate=pl.CostEstimate(flops=flops, bytes_accessed=size, transcendentals=0),
    )


def exchange(value, axis, distance):
    return lax.ppermute(value, axis, [(i, i ^ distance) for i in range(lax.axis_size(axis))])


def send_parts(parts, axis, near_count, sizes, extra=0):
    far_parts, far_count = list(parts), len(parts)
    for far in range(far_count - 1, 0, -1):
        far_parts[far] = exchange(parts[far], axis, far * near_count)
    payload = jax.ShapeDtypeStruct((far_count * (sum(sizes) + extra), parts[0].shape[1]), jnp.float32)
    relay = call(
        functools.partial(relay_kernel, far_count=far_count, sizes=sizes, extra=extra),
        "relay",
        (payload,) * (near_count - 1),
        (pltpu.VMEM,) * far_count,
        flops=RELAY_WEIGHT,
    )
    near_parts = relay(far_parts[0], *far_parts[:0:-1])
    return far_parts, [exchange(part, axis, near) for near, part in enumerate(near_parts, 1)]


def body(query, key, value, implicit_filter, explicit_taps, skip_gain, out_grad):
    rows, channels = query.shape
    blocks = lax.axis_size("ctx")
    share = channels // blocks
    padded = -(-share // 8) * 8
    f32 = jnp.float32
    shape = functools.partial(jax.ShapeDtypeStruct, dtype=f32)
    grad_scale = 1.0 / math.sqrt(blocks * rows)
    taps, skip = explicit_taps, skip_gain.reshape(1, channels)

    near_count = 1 << (blocks.bit_length() - 1) // 2 if share == padded else 1
    far_count = blocks // near_count
    product = key.astype(f32) * value.astype(f32)
    mix_grad = out_grad.astype(f32) * query.astype(f32)
    first_early = share // 32 * 24 if near_count > 1 else 0
    sizes = (share, first_early) if first_early else (share,)
    split_parts = call(
        functools.partial(split_kernel, near_count=near_count, sizes=sizes),
        "split",
        (shape((near_count * sum(sizes), rows)),) * far_count,
        (pltpu.VMEM,) * len(sizes),
        scratch=(pltpu.VMEM((channels, rows), f32),),
        size=16 * rows * channels,
    )(*(implicit_filter, product)[: len(sizes)])
    both = shape((blocks, 2 * share - first_early, rows))
    packed = call(
        functools.partial(pack_kernel, early=first_early),
        "pack",
        both,
        (pltpu.VMEM,) * 2,
        scratch=(pltpu.VMEM(both.shape, f32), pltpu.SemaphoreType.DMA((2,))),
        to=pltpu.HBM,
        size=16 * rows * channels,
    )(product, mix_grad)
    if near_count > 1:
        far_parts, near_parts = send_parts(split_parts, "ctx", near_count, sizes)
        gates = lax.all_to_all(packed, "ctx", 0, 0, tiled=True)
    else:
        together = jnp.concatenate([packed, jnp.stack(split_parts)], axis=1).reshape(blocks, 3, share, rows)
        together = lax.all_to_all(together, "ctx", 0, 0, tiled=True)
        together = jnp.pad(together, ((0, 0), (0, 0), (0, padded - share), (0, 0)))
        gates, near_parts = together[:, :2].reshape(blocks, 2 * padded, rows), []
        far_parts = list(together[:, 2])
        own = lax.axis_index("ctx") * share
        taps, skip = [
            jnp.pad(lax.dynamic_slice_in_dim(each, own, share, 1), ((0, 0), (0, padded - share)))
            for each in (taps, skip)
        ]
    matrices, twists = tables(blocks, rows)
    height = (blocks + 1) * padded
    matrices, twists = jnp.asarray(matrices), jnp.asarray(twists)
    early = padded // 32 * 8 if near_count > 1 else 0
    block = pltpu.VMEM((blocks, padded, rows), f32)
    products, *split_parts = call(
        functools.partial(
            spectra_kernel, near_count=near_count, first_early=first_early, early=early, grad_scale=grad_scale
        ),
        "spectra",
        (shape((2, height, 2 * rows)),) + (shape((near_count * (padded + early) + padded, rows)),) * far_count,
        (pltpu.VMEM,) * (4 + far_count + near_count),
        scratch=(
            pltpu.VMEM((3, height, 2 * rows), f32),
            pltpu.VMEM((height, 2 * rows), f32),
            pltpu.VMEM(taps.shape[::-1], f32),
            block,
            pltpu.VMEM((blocks, max(early, 8), rows), f32),
            block,
            block,
        ),
        flops=27 * height * (2 * rows) ** 2,
        size=24 * blocks * padded * rows,
    )(taps, skip, matrices, twists, gates, *far_parts, *near_parts)
    if near_count > 1:
        sizes = (share, early) if early else (share,)
        far_parts, near_parts = send_parts(split_parts, "ctx", near_count, sizes, share)
    late = shape((blocks, 2 * padded - early, rows))
    results = call(
        functools.partial(mix_kernel, channels=padded, early=early),
        "mix",
        late,
        (pltpu.VMEM,) * 3,
        scratch=(pltpu.VMEM((2, height, 2 * rows), f32), pltpu.VMEM(late.shape, f32), pltpu.SemaphoreType.DMA((2,))),
        to=pltpu.HBM,
        flops=9 * height * (2 * rows) ** 2,
        size=24 * blocks * padded * rows,
    )(matrices, twists, products)
    if near_count > 1:
        parts = lax.all_to_all(results, "ctx", 0, 0, tiled=True)
    else:
        together = jnp.concatenate([results, jnp.stack(split_parts)], axis=1).reshape(blocks, 4, padded, rows)
        together = lax.all_to_all(together[:, :, :share], "ctx", 0, 0, tiled=True).reshape(blocks, 4 * share, rows)
        parts, far_parts, near_parts = together[:, : 2 * share], list(together[:, 2 * share :]), []
    full, one = shape((rows, channels)), shape((1, channels))
    block = pltpu.VMEM((blocks, share, rows), f32)
    outs = call(
        functools.partial(unpack_kernel, far_count=far_count, near_count=near_count, early=early),
        "unpack",
        (full,) * 6 + (one,),
        (pltpu.VMEM,) * (4 + far_count + near_count),
        scratch=tuple(pltpu.VMEM(out.shape, f32) for out in (full,) * 6 + (one,))
        + (pltpu.SemaphoreType.DMA((7,)), block, block, block),
        to=pltpu.HBM,
        size=48 * rows * channels,
    )(query, key, value, out_grad, parts, *far_parts, *near_parts)
    return (*outs[:6], outs[6].reshape(channels))


def solution(mesh):
    in_specs = (
        P("ctx", "ch"),
        P("ctx", "ch"),
        P("ctx", "ch"),
        P("ctx", "ch"),
        P(None, "ch"),
        P("ch"),
        P("ctx", "ch"),
    )
    out_specs = (
        P("ctx", "ch"),
        P("ctx", "ch"),
        P("ctx", "ch"),
        P("ctx", "ch"),
        P("ctx", "ch"),
        P(None, "ch"),
        P("ch"),
    )
    return jax.shard_map(body, mesh=mesh, in_specs=in_specs, out_specs=out_specs, check_vma=False)
```
